256 devices in a mesh: ctx: 64 (over y, x, z_hi, core), head: 4 (over z_lo).
Axes of the slice: x: 4, y: 4, z: 8 (z_hi: 2, z_lo: 4; z = z_hi * 4 + z_lo), core: 2. Of those that a mesh axis runs over, the one named last changes fastest.
Arguments:
- query_unrotated: bfloat16 [1024, 8192], P('ctx', 'head'), may hold values from -6 to 6
- q_rope: bfloat16 [1024, 4096], P('ctx', 'head'), may hold values from -200 to 200
- latent: bfloat16 [1, 16384, 512], P(None, 'ctx'), may hold values from -6 to 6
- k_rope: bfloat16 [1, 16384, 64], P(None, 'ctx'), may hold values from -4 to 4
- key_pos: int32 [1, 16384], P(None, 'ctx'), may hold values from 0 to 16383, as said below
- offset: int32 [1], replicated, may hold values from 0 to 15360
- w_uk: bfloat16 [64, 128, 512], P('head'), may hold values from -0.5 to 0.5
- value_up_weight: bfloat16 [64, 512, 128], P('head'), may hold values from -0.25 to 0.25
- w_out: bfloat16 [8192, 7168], P('head', 'ctx'), may hold values from -0.0625 to 0.0625
Outputs:
- attn_out: bfloat16 [1024, 7168], P('head', 'ctx')
The draws below stay inside these ranges and needn't reach their ends.
Inputs may be any that keep to these rules, and one draw needn't show every extreme that they name: `key_pos`: for each prompt the positions of its 16384 cached rows are a permutation of 0 to 16383 made of whole pages of 16 consecutive positions.
All inputs are finite; a program needn't handle non-finite values.
Results may differ from the reference program's by a relative error of at most 0.015.
Values may be sent and summed in bfloat16 or wider, within the bound.
No kernel may reach another device: no remote copies, remote signals or barrier semaphores. Data moves between devices by JAX's collectives and lax.ppermute only.
A program may use at most 128 MiB of HBM per device.

```python
import jax
import jax.numpy as jnp
from jax import lax

D = 7168
HEADS = 64
KV_RANK = 512
ROPE = 64
NOPE = 128
VDIM = 128
PROMPTS = 1
PAGE = 16
QROWS = 1024
QWIN = 1024
CTX_P = 16384


def single_order(key):
    return jax.random.permutation(key, CTX_P // PAGE)


def page_orders(key):
    return jax.vmap(single_order)(jax.random.split(key, PROMPTS)).astype(jnp.int32)


def rotary_frequency_base(key):
    return jax.random.truncated_normal(key, -4.0, 4.0, (PROMPTS, CTX_P, ROPE), jnp.float32)


def draw_key_pos(key, part):
    orders = page_orders(jax.random.fold_in(key, 101))
    within = jnp.arange(CTX_P, dtype=jnp.int32)
    return jnp.take(orders, within // PAGE, axis=1) * PAGE + within % PAGE


def draw_k_rope(key, part):
    base = rotary_frequency_base(jax.random.fold_in(key, 102))
    return base.astype(jnp.bfloat16)


def draw_q_rope(key, part):
    own_key = jax.random.fold_in(key, 7)
    base = jax.random.truncated_normal(own_key, -4.0, 4.0, (QROWS, HEADS, ROPE), jnp.float32)
    return base.reshape(QROWS, HEADS * ROPE).astype(jnp.bfloat16)


def levels(key, dims, pieces, least, top_value):
    factor_of = 1.0
    for dim, parts in pieces:
        draws = jax.random.uniform(jax.random.fold_in(jax.random.fold_in(key, 6), dim), (parts,), jnp.float32, least / len(pieces), top_value / len(pieces))
        factor_of = factor_of * jnp.repeat(jnp.exp(draws), dims[dim] // parts).reshape((-1,) + (1,) * (len(dims) - 1 - dim))
    return factor_of


def centred(stream_key, extent, deviation, most, pieces=(), kind=jnp.bfloat16):
    loudness = levels(stream_key, extent, pieces, -0.22, 0.18) if pieces else 1.0
    drawn = jax.random.normal(stream_key, extent, jnp.float32) * deviation * loudness
    return jnp.minimum(jnp.maximum(drawn, -most), most).astype(kind)


def setup_inputs(seed: int = 0) -> dict:
    seeds = jax.random.split(jax.random.key(seed), 10)
    query_unrotated = centred(seeds[0], (QROWS, HEADS * NOPE), 1.0, 6.0, ((0, 64), (1, 4)))
    q_rope = draw_q_rope(jax.random.fold_in(seeds[9], 71), 0)
    latent = centred(seeds[2], (PROMPTS, CTX_P, KV_RANK), 1.0, 6.0, ((1, 64),))
    k_rope = draw_k_rope(jax.random.fold_in(seeds[9], 71), 0)
    key_pos = draw_key_pos(jax.random.fold_in(seeds[9], 71), 0)
    offset = jax.random.randint(seeds[5], (PROMPTS,), 0, CTX_P - QWIN + 1).astype(jnp.int32)
    w_uk = centred(seeds[6], (HEADS, NOPE, KV_RANK), NOPE ** -0.5, 0.5, ((0, 4),))
    value_up_weight = centred(seeds[7], (HEADS, KV_RANK, VDIM), KV_RANK ** -0.5, 0.25, ((0, 4),))
    w_out = centred(seeds[8], (HEADS * VDIM, D), (HEADS * VDIM) ** -0.5, 0.0625, ((0, 4), (1, 64)))
    return {"query_unrotated": query_unrotated, "q_rope": q_rope, "latent": latent, "k_rope": k_rope, "key_pos": key_pos, "offset": offset, "w_uk": w_uk, "value_up_weight": value_up_weight, "w_out": w_out}


def reference(query_unrotated, q_rope, latent, k_rope, key_pos, offset, w_uk, value_up_weight, w_out):
    score_scale = (NOPE + ROPE) ** -0.5
    query_heads = jnp.transpose(query_unrotated.reshape(PROMPTS, QWIN, HEADS, NOPE), (2, 0, 1, 3))
    rotary_heads = jnp.transpose(q_rope.reshape(PROMPTS, QWIN, HEADS, ROPE), (2, 0, 1, 3))
    query_pos = offset[:, None] + jnp.arange(QWIN, dtype=jnp.int32)[None, :]
    visible = key_pos[:, None, :] <= query_pos[:, :, None]
    latent_expanded = latent.astype(jnp.float32)
    rotary_keys = k_rope.astype(jnp.float32)

    def one_head(operands):
        query_head, rotary_head, absorb_weight, value_weight = operands
        query_latent = jnp.einsum("pqn,nk->pqk", query_head.astype(jnp.float32), absorb_weight.astype(jnp.float32))
        query_latent = lax.optimization_barrier(query_latent.astype(jnp.bfloat16))
        score_matrix = jnp.einsum("pqk,pjk->pqj", query_latent.astype(jnp.float32), latent_expanded)
        score_matrix = score_matrix + jnp.einsum("pqr,pjr->pqj", rotary_head.astype(jnp.float32), rotary_keys)
        score_matrix = score_matrix * score_scale
        masked = jnp.where(visible, score_matrix, -1e30)
        row_max = jnp.max(masked, axis=2, keepdims=True)
        weights_raw = jnp.where(visible, jnp.exp(masked - row_max), 0.0)
        denominator = jnp.sum(weights_raw, axis=2, keepdims=True)
        weights_low = lax.optimization_barrier(weights_raw.astype(jnp.bfloat16))
        context_vectors = jnp.einsum("pqj,pjk->pqk", weights_low.astype(jnp.float32), latent_expanded) / denominator
        context_vectors = lax.optimization_barrier(context_vectors.astype(jnp.bfloat16))
        result = jnp.einsum("pqk,kv->pqv", context_vectors.astype(jnp.float32), value_weight.astype(jnp.float32))
        return result.astype(jnp.bfloat16)

    head_outputs = lax.map(one_head, (query_heads, rotary_heads, w_uk, value_up_weight))
    flattened = jnp.transpose(head_outputs, (1, 2, 0, 3)).reshape(QROWS, HEADS * VDIM)
    return jnp.dot(flattened, w_out, preferred_element_type=jnp.float32).astype(jnp.bfloat16)
```

```python
import functools

import jax
import jax.numpy as jnp
from jax import lax
from jax.experimental import pallas as pl
from jax.experimental.pallas import tpu as pltpu
from jax.sharding import Mesh, PartitionSpec as P

ROPE = 64
NOPE = 128
RANK = 512
VDIM = 128
HG = 16
R = 16
GROUP = 4
ROWS = GROUP * R
ITEMS = HG * ROWS
KEYW = RANK + 128
SENDW = HG * VDIM + 128
SCALE2 = (NOPE + ROPE) ** -0.5 * 1.4426950408889634
NEG = -1e30
CTX = ("y", "x", "z", "c")
SWAP = ((0, 1), (1, 0))
MIB = 1 << 20


def shift(n, d):
    return [(i, (i + d) % n) for i in range(n)]


def call(kernel, out_shape, flops, nbytes, vmem=40, **kw):
    return pl.pallas_call(
        kernel,
        out_shape=out_shape,
        compiler_params=pltpu.CompilerParams(vmem_limit_bytes=vmem * MIB),
        cost_estimate=pl.CostEstimate(flops=flops, bytes_accessed=nbytes, transcendentals=0),
        **kw,
    )


def nt_dot(a, b):
    return lax.dot_general(a, b, (((1,), (1,)), ((), ())), preferred_element_type=jnp.float32)


def absorb_kernel(q_ref, w_ref, out_ref):
    lane = lax.broadcasted_iota(jnp.int32, (ROWS, 128), 1)
    row = lax.broadcasted_iota(jnp.int32, (ROWS, 128), 0)
    eye = (lane - ROPE == row).astype(jnp.float32)
    for h in range(HG):
        latent = jnp.dot(
            q_ref[:, h * NOPE : (h + 1) * NOPE], w_ref[h], preferred_element_type=jnp.float32
        )
        out_ref[h * ROWS : (h + 1) * ROWS, :RANK] = latent.astype(jnp.bfloat16)
        start = HG * NOPE + (h // 2) * 128
        pair = q_ref[:, start : start + 128].astype(jnp.float32)
        if h % 2:
            pair = pltpu.roll(pair, ROPE, 1)
        ext = jnp.where(lane < ROPE, pair, eye)
        out_ref[h * ROWS : (h + 1) * ROWS, RANK:] = ext.astype(jnp.bfloat16)


def absorb(q, w_uk):
    return call(
        absorb_kernel,
        jax.ShapeDtypeStruct((ITEMS, KEYW), jnp.bfloat16),
        2 * ITEMS * NOPE * RANK,
        4 * MIB,
    )(q, w_uk)


def attend_kernel(pieces, first, *refs):
    q_ref, qpos_ref = refs[:2]
    key_refs = refs[2 : 2 + pieces]
    rest = refs[2 + pieces :]
    if first:
        acc_out, st_out, ext_ref = rest
    else:
        acc_in, st_in, acc_out, st_out, ext_ref = rest
    keys = key_refs[0].shape[0]

    @pl.when(pl.program_id(0) == 0)
    def _():
        qpos = qpos_ref[0:1, :]
        lane = lax.broadcasted_iota(jnp.int32, (keys, 128), 1)
        for i, key_ref in enumerate(key_refs):
            ext = key_ref[:, RANK:].astype(jnp.float32)
            pos = ext[:, ROPE : ROPE + 1] * 128.0 + ext[:, ROPE + 1 : ROPE + 2]
            bias = jnp.where(pos <= qpos, 0.0, NEG)
            ext_ref[i] = jnp.where(lane < ROPE, ext, bias).astype(jnp.bfloat16)

    tile = q_ref.shape[0]
    sub = 128
    lane = lax.broadcasted_iota(jnp.int32, (sub, 128), 1)
    for t in range(tile // sub):
        rows = slice(t * sub, (t + 1) * sub)
        q_latent, q_ext = q_ref[rows, :RANK], q_ref[rows, RANK:]
        scores = [
            (nt_dot(q_latent, key_refs[i][:, :RANK]) + nt_dot(q_ext, ext_ref[i])) * SCALE2
            for i in range(pieces)
        ]
        top = functools.reduce(jnp.maximum, [jnp.max(s, axis=1, keepdims=True) for s in scores])
        if not first:
            top = jnp.maximum(top, st_in[rows, 0:1])
        weights = [jnp.exp2(s - top) for s in scores]
        total = sum(jnp.sum(w, axis=1, keepdims=True) for w in weights)
        acc = sum(
            jnp.dot(
                w.astype(jnp.bfloat16), key_refs[i][:, :RANK], preferred_element_type=jnp.float32
            )
            for i, w in enumerate(weights)
        )
        if not first:
            keep = jnp.exp2(st_in[rows, 0:1] - top)
            total = total + keep * st_in[rows, 1:2]
            acc = acc + keep * acc_in[rows, :]
        acc_out[rows, :] = acc
        st_out[rows, :] = jnp.where(lane == 0, top, total)


def attend(q, qpos, pieces, state, tile=256):
    n, keys = len(pieces), pieces[0].shape[0]
    first = state is None
    whole = lambda shape: pl.BlockSpec(shape, lambda i: (0, 0))
    part = lambda width: pl.BlockSpec((tile, width), lambda i: (i, 0))
    carried = [part(RANK), part(128)]
    return call(
        functools.partial(attend_kernel, n, first),
        (
            jax.ShapeDtypeStruct((ITEMS, RANK), jnp.float32),
            jax.ShapeDtypeStruct((ITEMS, 128), jnp.float32),
        ),
        2 * ITEMS * n * keys * (KEYW + RANK),
        (ITEMS * (KEYW + RANK) + n * keys * KEYW) * 2,
        grid=(ITEMS // tile,),
        in_specs=[part(KEYW), whole((8, 128))]
        + [whole((keys, KEYW))] * n
        + ([] if first else carried),
        out_specs=carried,
        scratch_shapes=[pltpu.VMEM((n, keys, 128), jnp.bfloat16)],
    )(q, qpos, *pieces, *([] if first else state))


def value_kernel(acc_ref, st_ref, v_ref, keep_ref, send_ref):
    half = ROWS // 2
    lane = lax.broadcasted_iota(jnp.int32, (ROWS, 128), 1)
    stats = jnp.zeros((ROWS, 128), jnp.float32)
    for h in range(HG):
        rows = slice(h * ROWS, (h + 1) * ROWS)
        top, total = st_ref[rows, 0:1], st_ref[rows, 1:2]
        context = (acc_ref[rows, :] / total).astype(jnp.bfloat16)
        out = jnp.dot(context, v_ref[h], preferred_element_type=jnp.float32).astype(jnp.bfloat16)
        cols = slice(h * VDIM, (h + 1) * VDIM)
        keep_ref[:, cols] = out[:half]
        send_ref[:, cols] = out[half:]
        stats = jnp.where(lane == h, top + jnp.log2(total), stats)
    high = stats.astype(jnp.bfloat16).astype(jnp.float32)
    mid = (stats - high).astype(jnp.bfloat16).astype(jnp.float32)
    low = stats - high - mid
    packed = high + pltpu.roll(mid, HG, 1) + pltpu.roll(low, 2 * HG, 1)
    packed = packed.astype(jnp.bfloat16)
    keep_ref[:, HG * VDIM :] = packed[:half]
    send_ref[:, HG * VDIM :] = packed[half:]


def value_up(state, value_weight):
    half = jax.ShapeDtypeStruct((ROWS // 2, SENDW), jnp.bfloat16)
    return call(value_kernel, (half, half), 2 * ITEMS * RANK * VDIM, 5 * MIB)(
        *state, value_weight
    )


def merge(a_ref, b_ref):
    def stats(ref):
        packed = ref[:, HG * VDIM :].astype(jnp.float32)
        return (
            packed
            + pltpu.roll(packed, 128 - HG, 1)
            + pltpu.roll(packed, 128 - 2 * HG, 1)
        )

    a, b = stats(a_ref), stats(b_ref)
    top = jnp.maximum(a, b)
    wa, wb = jnp.exp2(a - top), jnp.exp2(b - top)
    total = wa + wb
    return wa / total, wb / total, top + jnp.log2(total)


def merge_core_kernel(a_ref, b_ref, own_ref, send_ref):
    wa, wb, lse = merge(a_ref, b_ref)
    for h in range(HG):
        cols = slice(h * VDIM, (h + 1) * VDIM)
        out = a_ref[:, cols].astype(jnp.float32) * wa[:, h : h + 1]
        out = out + b_ref[:, cols].astype(jnp.float32) * wb[:, h : h + 1]
        out = out.astype(jnp.bfloat16)
        own_ref[:, cols] = out[:R]
        send_ref[:, cols] = out[R:]
    lane = lax.broadcasted_iota(jnp.int32, lse.shape, 1)
    lse = jnp.where(lane < HG, lse, 0.0)
    high = lse.astype(jnp.bfloat16).astype(jnp.float32)
    mid = (lse - high).astype(jnp.bfloat16).astype(jnp.float32)
    low = lse - high - mid
    packed = high + pltpu.roll(mid, HG, 1) + pltpu.roll(low, 2 * HG, 1)
    packed = packed.astype(jnp.bfloat16)
    own_ref[:, HG * VDIM :] = packed[:R]
    send_ref[:, HG * VDIM :] = packed[R:]


def merge_zhi_kernel(a_ref, b_ref, out_ref):
    wa, wb, _ = merge(a_ref, b_ref)
    for h in range(HG):
        cols = slice(h * VDIM, (h + 1) * VDIM)
        out = a_ref[:, cols].astype(jnp.float32) * wa[:, h : h + 1]
        out = out + b_ref[:, cols].astype(jnp.float32) * wb[:, h : h + 1]
        out = out.astype(jnp.bfloat16)
        for i in range(out_ref.shape[0]):
            out_ref[i, :, cols] = out


def project_kernel(zc_ref, x_ref, *refs):
    out_ref = refs[-1]
    z, c = zc_ref[0], zc_ref[1]
    for k in range(GROUP):
        to_z = z if k % 2 == 0 else 1 - z
        to_c = c if k < 2 else 1 - c
        out_ref[to_z * 2 + to_c] = jnp.dot(
            x_ref[...], refs[k][...], preferred_element_type=jnp.float32
        ).astype(jnp.bfloat16)


def gather_keys(block):
    half = block.shape[0] // 2
    a, b = block[:half], block[half:]
    a_row = [a] + [lax.ppermute(a, "x", shift(4, d)) for d in (1, 3, 2)]
    b_row = [b] + [lax.ppermute(b, "y", shift(4, d)) for d in (1, 3, 2)]
    a_all, b_all = jnp.concatenate(a_row), jnp.concatenate(b_row)
    a_far = [lax.ppermute(a_all, "y", shift(4, d)) for d in (1, 3, 2)]
    b_far = [lax.ppermute(b_all, "x", shift(4, d)) for d in (1, 3, 2)]
    return [a_all, b_all], [a_far[0], b_far[0], a_far[1], b_far[1]], [a_far[2], b_far[2]]


def local(query_unrotated, q_rope, latent, k_rope, key_pos, offset, w_uk, value_up_weight, w_out):
    y, x, z, c = (lax.axis_index(n) for n in CTX)

    q_own = jnp.concatenate([query_unrotated, q_rope], axis=1)
    q_z = lax.ppermute(q_own, "z", SWAP)
    q_chip = jnp.concatenate([q_own, q_z])
    q_all = jnp.concatenate([q_chip, lax.ppermute(q_chip, "c", SWAP)])

    pos = key_pos.reshape(-1, 1)
    keys = jnp.concatenate(
        [
            latent[0],
            k_rope[0],
            (pos // 128).astype(jnp.bfloat16),
            (pos % 128).astype(jnp.bfloat16),
            jnp.zeros((pos.shape[0], KEYW - RANK - ROPE - 2), jnp.bfloat16),
        ],
        axis=1,
    )
    near, mid, far = gather_keys(keys)

    lane = jnp.arange(128, dtype=jnp.int32) - ROPE
    part = jnp.maximum(lane, 0) // R
    row_z = jnp.where(part % 2 == 0, z, 1 - z)
    row_c = jnp.where(part < 2, c, 1 - c)
    row = (((y * 4 + x) * 2 + row_z) * 2 + row_c) * R + lane % R
    qpos = jnp.broadcast_to((offset[0] + row).astype(jnp.float32)[None, :], (8, 128))

    q = absorb(q_all, w_uk)
    state = attend(q, qpos, near, None)
    state = attend(q, qpos, mid, state)
    state = attend(q, qpos, far, state)

    w_own, _ = lax.optimization_barrier((w_out, q_z))
    w_z = lax.ppermute(w_own, "z", SWAP)
    w_c = lax.ppermute(w_own, "c", SWAP)
    w_zc = lax.ppermute(w_z, "c", SWAP)

    keep, send = value_up(state, value_up_weight)
    both = jax.ShapeDtypeStruct((R, SENDW), jnp.bfloat16)
    own, send = call(merge_core_kernel, (both, both), MIB, MIB)(
        keep, lax.ppermute(send, "c", SWAP)
    )
    heads = call(
        merge_zhi_kernel, jax.ShapeDtypeStruct((16, R, HG * VDIM), jnp.bfloat16), MIB, MIB
    )(own, lax.ppermute(send, "z", SWAP))

    rows = lax.all_to_all(heads, ("y", "x"), 0, 0, tiled=True).reshape(16 * R, HG * VDIM)
    ncol = w_out.shape[1]
    sums = call(
        project_kernel,
        jax.ShapeDtypeStruct((GROUP, 16 * R, ncol), jnp.bfloat16),
        2 * 16 * R * HG * VDIM * GROUP * ncol,
        4 * MIB,
        in_specs=[pl.BlockSpec(memory_space=pltpu.SMEM)]
        + [pl.BlockSpec(memory_space=pltpu.VMEM)] * (1 + GROUP),
    )(jnp.stack([z, c]), rows, w_own, w_z, w_c, w_zc)
    sums = lax.all_to_all(
        sums.reshape(16, 4 * R, ncol), ("z", "c", "head"), 0, 0, tiled=True
    )
    total = jnp.sum(sums.reshape(GROUP, 4, 4, R, ncol).astype(jnp.float32), axis=1)
    return jnp.transpose(total.astype(jnp.bfloat16), (1, 0, 2, 3)).reshape(16 * R, ncol)


def solution(mesh):
    grid = Mesh(mesh.devices.reshape(4, 4, 2, 2, 4), CTX + ("head",))
    return jax.shard_map(
        local,
        mesh=grid,
        in_specs=(
            P(CTX, "head"),
            P(CTX, "head"),
            P(None, CTX, None),
            P(None, CTX, None),
            P(None, CTX),
            P(),
            P("head", None, None),
            P("head", None, None),
            P("head", CTX),
        ),
        out_specs=P("head", CTX),
        check_vma=False,
    )
```

```python
import functools

import jax
import jax.numpy as jnp
from jax import lax
from jax.experimental import pallas as pl
from jax.experimental.pallas import tpu as pltpu
from jax.sharding import Mesh, PartitionSpec as P

ROPE = 64
NOPE = 128
RANK = 512
VDIM = 128
HG = 16
R = 16
GROUP = 8
ROWS = GROUP * R
ITEMS = HG * ROWS
KEYW = RANK + 128
ITEMW = RANK + 256
SENDW = HG * VDIM + 128
SCALE2 = (NOPE + ROPE) ** -0.5 * 1.4426950408889634
NEG = -1e30
CTX = ("y", "u", "x", "z", "c")
SWAP = ((0, 1), (1, 0))
MIB = 1 << 20


def shift(n, d):
    return [(i, (i + d) % n) for i in range(n)]


def call(kernel, out_shape, flops, nbytes, vmem=40, **kw):
    return pl.pallas_call(
        kernel,
        out_shape=out_shape,
        compiler_params=pltpu.CompilerParams(vmem_limit_bytes=vmem * MIB),
        cost_estimate=pl.CostEstimate(flops=flops, bytes_accessed=nbytes, transcendentals=0),
        **kw,
    )


def nt_dot(a, b):
    return lax.dot_general(a, b, (((1,), (1,)), ((), ())), preferred_element_type=jnp.float32)


def pack_kernel(query_ref, rope_ref, latent_ref, key_rope_ref, pos_ref, q_ref, key_ref):
    q_ref[:, : HG * NOPE] = query_ref[...]
    q_ref[:, HG * NOPE :] = rope_ref[...]
    key_ref[:, :RANK] = latent_ref[...]
    key_ref[:, RANK : RANK + ROPE] = key_rope_ref[...]
    keys = latent_ref.shape[0]
    pos = jnp.transpose(jnp.broadcast_to(pos_ref[...], (128, keys)).astype(jnp.float32))
    high = jnp.floor(pos * (1 / 128))
    lane = lax.broadcasted_iota(jnp.int32, (keys, 128), 1)
    ext = jnp.where(lane == ROPE, high, jnp.where(lane == ROPE + 1, pos - high * 128, 0.0))
    key_ref[:, RANK + ROPE :] = ext[:, ROPE:].astype(jnp.bfloat16)


def pack(query, q_rope, latent, k_rope, key_pos):
    return call(
        pack_kernel,
        (
            jax.ShapeDtypeStruct((R, HG * (NOPE + ROPE)), jnp.bfloat16),
            jax.ShapeDtypeStruct((latent.shape[0], KEYW), jnp.bfloat16),
        ),
        MIB,
        MIB,
    )(query, q_rope, latent, k_rope, key_pos)


def absorb_kernel(q_ref, w_ref, out_ref):
    lane = lax.broadcasted_iota(jnp.int32, (ROWS, 128), 1)
    row = lax.broadcasted_iota(jnp.int32, (ROWS, 128), 0)
    one_hot = (lane == row).astype(jnp.bfloat16)
    for h in range(HG):
        rows = slice(h * ROWS, (h + 1) * ROWS)
        latent = jnp.dot(
            q_ref[:, h * NOPE : (h + 1) * NOPE], w_ref[h], preferred_element_type=jnp.float32
        )
        out_ref[rows, :RANK] = latent.astype(jnp.bfloat16)
        start = HG * NOPE + (h // 2) * 128
        pair = q_ref[:, start : start + 128].astype(jnp.float32)
        if h % 2:
            pair = pltpu.roll(pair, ROPE, 1)
        rope = jnp.where(lane < ROPE, pair, 0.0)
        out_ref[rows, RANK : RANK + 128] = rope.astype(jnp.bfloat16)
        out_ref[rows, RANK + 128 :] = one_hot


def absorb(q, w_uk):
    return call(
        absorb_kernel,
        jax.ShapeDtypeStruct((ITEMS, ITEMW), jnp.bfloat16),
        2 * ITEMS * NOPE * RANK,
        6 * MIB,
    )(q, w_uk)


def pack_stats(stats):
    high = stats.astype(jnp.bfloat16).astype(jnp.float32)
    mid = (stats - high).astype(jnp.bfloat16).astype(jnp.float32)
    low = stats - high - mid
    packed = high + pltpu.roll(mid, HG, 1) + pltpu.roll(low, 2 * HG, 1)
    return packed.astype(jnp.bfloat16)


def unpack_stats(packed):
    packed = packed.astype(jnp.float32)
    return packed + pltpu.roll(packed, 128 - HG, 1) + pltpu.roll(packed, 128 - 2 * HG, 1)


def attend_kernel(pieces, last, *refs):
    q_ref, qpos_ref = refs[:2]
    key_refs = refs[2 : 2 + pieces]
    rest = refs[2 + pieces :]
    if last:
        acc_in, st_in, v_ref, keep_ref, send_ref, ext_ref, lse_ref = rest
    else:
        acc_out, st_out, ext_ref = rest
    keys = key_refs[0].shape[0]
    step = pl.program_id(0)

    @pl.when(step == 0)
    def _():
        qpos = qpos_ref[0:1, :]
        for i, key_ref in enumerate(key_refs):
            ext = key_ref[:, RANK:]
            ext_ref[i, :, :128] = ext
            ext = ext.astype(jnp.float32)
            pos = ext[:, ROPE : ROPE + 1] * 128.0 + ext[:, ROPE + 1 : ROPE + 2]
            ext_ref[i, :, 128:] = jnp.where(pos <= qpos, 0.0, NEG).astype(jnp.bfloat16)
        if last:
            lse_ref[...] = jnp.zeros_like(lse_ref)

    tile = q_ref.shape[0]
    q_latent, q_ext = q_ref[:, :RANK], q_ref[:, RANK:]
    scores = [
        (nt_dot(q_latent, key_refs[i][:, :RANK]) + nt_dot(q_ext, ext_ref[i])) * SCALE2
        for i in range(pieces)
    ]
    top = functools.reduce(jnp.maximum, [jnp.max(s, axis=1, keepdims=True) for s in scores])
    if last:
        top = jnp.maximum(top, st_in[:, 0:1])
    weights = [jnp.exp2(s - top) for s in scores]
    total = sum(jnp.sum(w, axis=1, keepdims=True) for w in weights)
    acc = sum(
        jnp.dot(w.astype(jnp.bfloat16), key_refs[i][:, :RANK], preferred_element_type=jnp.float32)
        for i, w in enumerate(weights)
    )
    if not last:
        acc_out[...] = acc
        lane = lax.broadcasted_iota(jnp.int32, (tile, 128), 1)
        st_out[...] = jnp.where(lane == 0, top, total)
        return

    keep = jnp.exp2(st_in[:, 0:1] - top)
    total = total + keep * st_in[:, 1:2]
    context = ((acc + keep * acc_in[...]) / total).astype(jnp.bfloat16)
    lse = top + jnp.log2(total)
    half = ROWS // 2
    lane = lax.broadcasted_iota(jnp.int32, (ROWS, 128), 1)
    for i in range(tile // ROWS):
        rows = slice(i * ROWS, (i + 1) * ROWS)
        head = step * (tile // ROWS) + i
        out = jnp.dot(context[rows], v_ref[i], preferred_element_type=jnp.float32)
        out = out.astype(jnp.bfloat16)
        cols = pl.ds(pl.multiple_of(head * VDIM, VDIM), VDIM)
        keep_ref[:, cols] = out[:half]
        send_ref[:, cols] = out[half:]
        lse_ref[...] = jnp.where(lane == head, lse[rows], lse_ref[...])

    @pl.when(step == pl.num_programs(0) - 1)
    def _():
        packed = pack_stats(lse_ref[...])
        keep_ref[:, HG * VDIM :] = packed[:half]
        send_ref[:, HG * VDIM :] = packed[half:]


def attend(q, qpos, pieces, state=None, value_weight=None, tile=512):
    n, keys = len(pieces), pieces[0].shape[0]
    last = state is not None
    whole = lambda shape: pl.BlockSpec(shape, lambda i: (0, 0))
    part = lambda width: pl.BlockSpec((tile, width), lambda i: (i, 0))
    carried = [part(RANK), part(128)]
    in_specs = [part(ITEMW), whole((8, 128))] + [whole((keys, KEYW))] * n
    scratch = [pltpu.VMEM((n, keys, 256), jnp.bfloat16)]
    args = [q, qpos, *pieces]
    if last:
        heads = tile // ROWS
        in_specs += carried + [pl.BlockSpec((heads, RANK, VDIM), lambda i: (i, 0, 0))]
        args += [*state, value_weight]
        half = jax.ShapeDtypeStruct((ROWS // 2, SENDW), jnp.bfloat16)
        out_shape, out_specs = (half, half), [whole((ROWS // 2, SENDW))] * 2
        scratch.append(pltpu.VMEM((ROWS, 128), jnp.float32))
    else:
        out_shape = (
            jax.ShapeDtypeStruct((ITEMS, RANK), jnp.float32),
            jax.ShapeDtypeStruct((ITEMS, 128), jnp.float32),
        )
        out_specs = carried
    return call(
        functools.partial(attend_kernel, n, last),
        out_shape,
        2 * ITEMS * n * keys * (KEYW + RANK),
        (ITEMS * (ITEMW + RANK) + n * keys * KEYW) * 2,
        grid=(ITEMS // tile,),
        in_specs=in_specs,
        out_specs=out_specs,
        scratch_shapes=scratch,
    )(*args)


def merge(a_ref, b_ref):
    a, b = (unpack_stats(ref[:, HG * VDIM :]) for ref in (a_ref, b_ref))
    top = jnp.maximum(a, b)
    wa, wb = jnp.exp2(a - top), jnp.exp2(b - top)
    total = wa + wb
    wa, wb = wa / total, wb / total
    out = []
    for h in range(HG):
        cols = slice(h * VDIM, (h + 1) * VDIM)
        head = a_ref[:, cols].astype(jnp.float32) * wa[:, h : h + 1]
        head = head + b_ref[:, cols].astype(jnp.float32) * wb[:, h : h + 1]
        out.append((cols, head.astype(jnp.bfloat16)))
    return out, top + jnp.log2(total)


def merge_kernel(a_ref, b_ref, own_ref, send_ref):
    heads, lse = merge(a_ref, b_ref)
    half = own_ref.shape[0]
    lane = lax.broadcasted_iota(jnp.int32, lse.shape, 1)
    packed = pack_stats(jnp.where(lane < HG, lse, 0.0))
    for cols, head in heads + [(slice(HG * VDIM, SENDW), packed)]:
        own_ref[:, cols] = head[:half]
        send_ref[:, cols] = head[half:]


def merge_last_kernel(a_ref, b_ref, out_ref):
    heads, _ = merge(a_ref, b_ref)
    for cols, head in heads:
        for i in range(out_ref.shape[0]):
            out_ref[i, :, cols] = head


def merge_over(axis, own, send):
    half = jax.ShapeDtypeStruct((own.shape[0] // 2, SENDW), jnp.bfloat16)
    return call(merge_kernel, (half, half), MIB, MIB)(own, lax.ppermute(send, axis, SWAP))


def project_kernel(zc_ref, x_ref, *refs):
    out_ref = refs[-1]
    z, c = zc_ref[0], zc_ref[1]
    for k in range(4):
        to_z = z if k % 2 == 0 else 1 - z
        to_c = c if k < 2 else 1 - c
        out_ref[to_z * 2 + to_c] = jnp.dot(
            x_ref[...], refs[k][...], preferred_element_type=jnp.float32
        ).astype(jnp.bfloat16)


def local(query_unrotated, q_rope, latent, k_rope, key_pos, offset, w_uk, value_up_weight, w_out):
    y, u, x, z, c = (lax.axis_index(n) for n in CTX)

    q_own, keys = pack(query_unrotated, q_rope, latent[0], k_rope[0], key_pos)

    keys_u = lax.ppermute(keys, "u", SWAP)
    keys_up = lax.ppermute(keys, "y", shift(4, 1))
    keys_down = lax.ppermute(keys, "y", shift(4, 3))
    near = [jnp.concatenate([keys, keys_u]), jnp.concatenate([keys_up, keys_down])]
    far = [lax.ppermute(near[0], "y", shift(4, 2)), lax.ppermute(near[1], "u", SWAP)]

    q_z = lax.ppermute(q_own, "z", SWAP)
    q_all = jnp.concatenate([q_own, q_z])
    q_all = jnp.concatenate([q_all, lax.ppermute(q_all, "x", SWAP)])
    q_all = jnp.concatenate([q_all, lax.ppermute(q_all, "c", SWAP)])

    w_own, _ = lax.optimization_barrier((w_out, q_z))
    w_z = lax.ppermute(w_own, "z", SWAP)
    w_c = lax.ppermute(w_own, "c", SWAP)
    w_zc = lax.ppermute(w_z, "c", SWAP)

    row = jnp.arange(ROWS, dtype=jnp.int32)
    part = row // R
    row_z = jnp.where(part % 2 == 0, z, 1 - z)
    row_x = jnp.where(part // 2 % 2 == 0, x, 1 - x)
    row_c = jnp.where(part < 4, c, 1 - c)
    row = ((((y * 2 + u) * 2 + row_x) * 2 + row_z) * 2 + row_c) * R + row % R
    qpos = jnp.broadcast_to((offset[0] + row).astype(jnp.float32)[None, :], (8, ROWS))

    q = absorb(q_all, w_uk)
    state = attend(q, qpos, near)
    state, w_z = lax.optimization_barrier((state, w_z))
    own, send = attend(q, qpos, far, state, value_up_weight)
    own, send = merge_over("c", own, send)
    own, send = merge_over("x", own, send)
    heads = call(
        merge_last_kernel, jax.ShapeDtypeStruct((16, R, HG * VDIM), jnp.bfloat16), MIB, MIB
    )(own, lax.ppermute(send, "z", SWAP))

    rows = lax.all_to_all(heads, ("y", "u", "x"), 0, 0, tiled=True).reshape(16 * R, HG * VDIM)
    ncol = w_out.shape[1]
    sums = call(
        project_kernel,
        jax.ShapeDtypeStruct((4, 16 * R, ncol), jnp.bfloat16),
        2 * 16 * R * HG * VDIM * 4 * ncol,
        4 * MIB,
        in_specs=[pl.BlockSpec(memory_space=pltpu.SMEM)]
        + [pl.BlockSpec(memory_space=pltpu.VMEM)] * 5,
    )(jnp.stack([z, c]), rows, w_own, w_z, w_c, w_zc)
    sums = lax.all_to_all(
        sums.reshape(16, 4 * R, ncol), ("z", "c", "head"), 0, 0, tiled=True
    )
    total = jnp.sum(sums.reshape(4, 4, 4, R, ncol).astype(jnp.float32), axis=1)
    return jnp.transpose(total.astype(jnp.bfloat16), (1, 0, 2, 3)).reshape(16 * R, ncol)


def solution(mesh):
    grid = Mesh(mesh.devices.reshape(4, 2, 2, 2, 2, 4), CTX + ("head",))
    return jax.shard_map(
        local,
        mesh=grid,
        in_specs=(
            P(CTX, "head"),
            P(CTX, "head"),
            P(None, CTX, None),
            P(None, CTX, None),
            P(None, CTX),
            P(),
            P("head", None, None),
            P("head", None, None),
            P("head", CTX),
        ),
        out_specs=P("head", CTX),
        check_vma=False,
    )
```

```python
import functools

import jax
import jax.numpy as jnp
from jax import lax
from jax.experimental import pallas as pl
from jax.experimental.pallas import tpu as pltpu
from jax.sharding import Mesh, PartitionSpec as P

ROPE = 64
NOPE = 128
RANK = 512
VDIM = 128
HG = 16
R = 16
GROUP = 8
ROWS = GROUP * R
ITEMS = HG * ROWS
KEYW = RANK + 128
ITEMW = RANK + 256
SENDW = HG * VDIM + 128
SCALE2 = (NOPE + ROPE) ** -0.5 * 1.4426950408889634
NEG = -1e30
CTX = ("y", "u", "x", "z", "c")
SWAP = ((0, 1), (1, 0))
MIB = 1 << 20


def shift(n, d):
    return [(i, (i + d) % n) for i in range(n)]


def call(kernel, out_shape, flops, nbytes, vmem=40, **kw):
    return pl.pallas_call(
        kernel,
        out_shape=out_shape,
        compiler_params=pltpu.CompilerParams(vmem_limit_bytes=vmem * MIB),
        cost_estimate=pl.CostEstimate(flops=flops, bytes_accessed=nbytes, transcendentals=0),
        **kw,
    )


def nt_dot(a, b):
    return lax.dot_general(a, b, (((1,), (1,)), ((), ())), preferred_element_type=jnp.float32)


def pack_kernel(query_ref, rope_ref, latent_ref, key_rope_ref, pos_ref, q_ref, key_ref):
    key_ref[:, :RANK] = latent_ref[...]
    pos = pos_ref[...].astype(jnp.float32)
    high = jnp.floor(pos * (1 / 128))
    row = lax.broadcasted_iota(jnp.int32, key_rope_ref.shape, 0)
    ext = jnp.where(row == 0, high, jnp.where(row == 1, pos - high * 128, 0.0))
    ext = jnp.concatenate([key_rope_ref[...].astype(jnp.float32), ext], axis=0)
    key_ref[:, RANK:] = jnp.transpose(ext).astype(jnp.bfloat16)
    q_ref[:, : HG * NOPE] = query_ref[...]
    q_ref[:, HG * NOPE :] = rope_ref[...]


def pack(query, q_rope, latent, k_rope, key_pos):
    return call(
        pack_kernel,
        (
            jax.ShapeDtypeStruct((R, HG * (NOPE + ROPE)), jnp.bfloat16),
            jax.ShapeDtypeStruct((latent.shape[0], KEYW), jnp.bfloat16),
        ),
        MIB,
        MIB,
        vmem=60,
    )(query, q_rope, latent, jnp.transpose(k_rope), key_pos)


def absorb_kernel(q_ref, w_ref, out_ref):
    lane = lax.broadcasted_iota(jnp.int32, (ROWS, 128), 1)
    row = lax.broadcasted_iota(jnp.int32, (ROWS, 128), 0)
    one_hot = (lane == row).astype(jnp.bfloat16)
    for h in range(HG):
        rows = slice(h * ROWS, (h + 1) * ROWS)
        latent = jnp.dot(
            q_ref[:, h * NOPE : (h + 1) * NOPE], w_ref[h], preferred_element_type=jnp.float32
        )
        out_ref[rows, :RANK] = latent.astype(jnp.bfloat16)
        start = HG * NOPE + (h // 2) * 128
        pair = q_ref[:, start : start + 128].astype(jnp.float32)
        if h % 2:
            pair = pltpu.roll(pair, ROPE, 1)
        rope = jnp.where(lane < ROPE, pair, 0.0)
        out_ref[rows, RANK : RANK + 128] = rope.astype(jnp.bfloat16)
        out_ref[rows, RANK + 128 :] = one_hot


def absorb(q, w_uk):
    return call(
        absorb_kernel,
        jax.ShapeDtypeStruct((ITEMS, ITEMW), jnp.bfloat16),
        2 * ITEMS * NOPE * RANK,
        6 * MIB,
    )(q, w_uk)


def pack_stats(stats):
    high = stats.astype(jnp.bfloat16).astype(jnp.float32)
    mid = (stats - high).astype(jnp.bfloat16).astype(jnp.float32)
    low = stats - high - mid
    packed = high + pltpu.roll(mid, HG, 1) + pltpu.roll(low, 2 * HG, 1)
    return packed.astype(jnp.bfloat16)


def unpack_stats(packed):
    packed = packed.astype(jnp.float32)
    return packed + pltpu.roll(packed, 128 - HG, 1) + pltpu.roll(packed, 128 - 2 * HG, 1)


def attend_kernel(pieces, last, *refs):
    q_ref, qpos_ref = refs[:2]
    key_refs = refs[2 : 2 + pieces]
    rest = refs[2 + pieces :]
    if last:
        acc_in, st_in, v_ref, keep_ref, send_ref, ext_ref, lse_ref = rest
    else:
        acc_out, st_out, ext_ref = rest
    keys = key_refs[0].shape[0]
    step = pl.program_id(0)

    @pl.when(step == 0)
    def _():
        qpos = qpos_ref[0:1, :]
        for i, key_ref in enumerate(key_refs):
            ext = key_ref[:, RANK:]
            ext_ref[i, :, :128] = ext
            ext = ext.astype(jnp.float32)
            pos = ext[:, ROPE : ROPE + 1] * 128.0 + ext[:, ROPE + 1 : ROPE + 2]
            ext_ref[i, :, 128:] = jnp.where(pos <= qpos, 0.0, NEG).astype(jnp.bfloat16)
        if last:
            lse_ref[...] = jnp.zeros_like(lse_ref)

    tile = q_ref.shape[0]
    q_latent, q_ext = q_ref[:, :RANK], q_ref[:, RANK:]
    scores = [
        (nt_dot(q_latent, key_refs[i][:, :RANK]) + nt_dot(q_ext, ext_ref[i])) * SCALE2
        for i in range(pieces)
    ]
    top = functools.reduce(jnp.maximum, [jnp.max(s, axis=1, keepdims=True) for s in scores])
    if last:
        top = jnp.maximum(top, st_in[:, 0:1])
    weights = [jnp.exp2(s - top) for s in scores]
    total = sum(jnp.sum(w, axis=1, keepdims=True) for w in weights)
    acc = sum(
        jnp.dot(w.astype(jnp.bfloat16), key_refs[i][:, :RANK], preferred_element_type=jnp.float32)
        for i, w in enumerate(weights)
    )
    if not last:
        acc_out[...] = acc
        lane = lax.broadcasted_iota(jnp.int32, (tile, 128), 1)
        st_out[...] = jnp.where(lane == 0, top, total)
        return

    keep = jnp.exp2(st_in[:, 0:1] - top)
    total = total + keep * st_in[:, 1:2]
    context = ((acc + keep * acc_in[...]) / total).astype(jnp.bfloat16)
    lse = top + jnp.log2(total)
    half = ROWS // 2
    lane = lax.broadcasted_iota(jnp.int32, (ROWS, 128), 1)
    for i in range(tile // ROWS):
        rows = slice(i * ROWS, (i + 1) * ROWS)
        head = step * (tile // ROWS) + i
        out = jnp.dot(context[rows], v_ref[i], preferred_element_type=jnp.float32)
        out = out.astype(jnp.bfloat16)
        cols = pl.ds(pl.multiple_of(head * VDIM, VDIM), VDIM)
        keep_ref[:, cols] = out[:half]
        send_ref[:, cols] = out[half:]
        lse_ref[...] = jnp.where(lane == head, lse[rows], lse_ref[...])

    @pl.when(step == pl.num_programs(0) - 1)
    def _():
        packed = pack_stats(lse_ref[...])
        keep_ref[:, HG * VDIM :] = packed[:half]
        send_ref[:, HG * VDIM :] = packed[half:]


def attend(q, qpos, pieces, state=None, value_weight=None, tile=512):
    n, keys = len(pieces), pieces[0].shape[0]
    last = state is not None
    whole = lambda shape: pl.BlockSpec(shape, lambda i: (0, 0))
    part = lambda width: pl.BlockSpec((tile, width), lambda i: (i, 0))
    carried = [part(RANK), part(128)]
    in_specs = [part(ITEMW), whole((8, 128))] + [whole((keys, KEYW))] * n
    scratch = [pltpu.VMEM((n, keys, 256), jnp.bfloat16)]
    args = [q, qpos, *pieces]
    if last:
        heads = tile // ROWS
        in_specs += carried + [pl.BlockSpec((heads, RANK, VDIM), lambda i: (i, 0, 0))]
        args += [*state, value_weight]
        half = jax.ShapeDtypeStruct((ROWS // 2, SENDW), jnp.bfloat16)
        out_shape, out_specs = (half, half), [whole((ROWS // 2, SENDW))] * 2
        scratch.append(pltpu.VMEM((ROWS, 128), jnp.float32))
    else:
        out_shape = (
            jax.ShapeDtypeStruct((ITEMS, RANK), jnp.float32),
            jax.ShapeDtypeStruct((ITEMS, 128), jnp.float32),
        )
        out_specs = carried
    return call(
        functools.partial(attend_kernel, n, last),
        out_shape,
        2 * ITEMS * n * keys * (KEYW + RANK),
        (ITEMS * (ITEMW + RANK) + n * keys * KEYW) * 2,
        grid=(ITEMS // tile,),
        in_specs=in_specs,
        out_specs=out_specs,
        scratch_shapes=scratch,
    )(*args)


def merge(a_ref, b_ref):
    a, b = (unpack_stats(ref[:, HG * VDIM :]) for ref in (a_ref, b_ref))
    top = jnp.maximum(a, b)
    wa, wb = jnp.exp2(a - top), jnp.exp2(b - top)
    total = wa + wb
    wa, wb = wa / total, wb / total
    out = []
    for h in range(HG):
        cols = slice(h * VDIM, (h + 1) * VDIM)
        head = a_ref[:, cols].astype(jnp.float32) * wa[:, h : h + 1]
        head = head + b_ref[:, cols].astype(jnp.float32) * wb[:, h : h + 1]
        out.append((cols, head.astype(jnp.bfloat16)))
    return out, top + jnp.log2(total)


def merge_kernel(a_ref, b_ref, own_ref, send_ref):
    heads, lse = merge(a_ref, b_ref)
    half = own_ref.shape[0]
    lane = lax.broadcasted_iota(jnp.int32, lse.shape, 1)
    packed = pack_stats(jnp.where(lane < HG, lse, 0.0))
    for cols, head in heads + [(slice(HG * VDIM, SENDW), packed)]:
        own_ref[:, cols] = head[:half]
        send_ref[:, cols] = head[half:]


def merge_last_kernel(a_ref, b_ref, out_ref):
    heads, _ = merge(a_ref, b_ref)
    for cols, head in heads:
        for i in range(out_ref.shape[0]):
            out_ref[i, :, cols] = head


def merge_over(axis, own, send):
    half = jax.ShapeDtypeStruct((own.shape[0] // 2, SENDW), jnp.bfloat16)
    return call(merge_kernel, (half, half), MIB, MIB)(own, lax.ppermute(send, axis, SWAP))


def project_kernel(zc_ref, x_ref, *refs):
    out_ref = refs[-1]
    z, c = zc_ref[0], zc_ref[1]
    for k in range(4):
        to_z = z if k % 2 == 0 else 1 - z
        to_c = c if k < 2 else 1 - c
        out_ref[to_z * 2 + to_c] = nt_dot(x_ref[...], refs[k][...]).astype(jnp.bfloat16)


def finish_kernel(sums_ref, out_ref, row_ref):
    ncol = sums_ref.shape[2]
    row_ref[...] = jnp.zeros_like(row_ref)
    for zc in range(4):
        total = sum(sums_ref[zc * 4 + h].astype(jnp.float32) for h in range(4))
        for i in range(4):
            start = (i * 4 + zc) * R
            row_ref[start : start + R, :ncol] = total[i * R : (i + 1) * R]
    out_ref[...] = jnp.transpose(row_ref[...])[:ncol].astype(jnp.bfloat16)


def local(query_unrotated, q_rope, latent, k_rope, key_pos, offset, w_uk, value_up_weight, w_out):
    y, u, x, z, c = (lax.axis_index(n) for n in CTX)

    q_own, keys = pack(query_unrotated, q_rope, latent[0], k_rope[0], key_pos)

    phase = (
        lax.ppermute(keys, "u", SWAP),
        lax.ppermute(keys, "y", shift(4, 1)),
        lax.ppermute(keys, "y", shift(4, 3)),
        lax.ppermute(q_own, "z", SWAP),
        lax.ppermute(q_own, "x", SWAP),
        lax.ppermute(q_own, ("x", "z"), [(i, 3 - i) for i in range(4)]),
    )
    keys_u, keys_up, keys_down, q_z, q_x, q_xz, w_own = lax.optimization_barrier(
        phase + (jnp.transpose(w_out),)
    )

    near = [jnp.concatenate([keys, keys_u]), jnp.concatenate([keys_up, keys_down])]
    far = [lax.ppermute(near[0], "y", shift(4, 2)), lax.ppermute(near[1], "u", SWAP)]
    q_all = jnp.concatenate([q_own, q_z, q_x, q_xz])
    q_all = jnp.concatenate([q_all, lax.ppermute(q_all, "c", SWAP)])
    w_z = lax.ppermute(w_own, "z", SWAP)
    w_c = lax.ppermute(w_own, "c", SWAP)

    row = jnp.arange(ROWS, dtype=jnp.int32)
    part = row // R
    row_z = jnp.where(part % 2 == 0, z, 1 - z)
    row_x = jnp.where(part // 2 % 2 == 0, x, 1 - x)
    row_c = jnp.where(part < 4, c, 1 - c)
    row = ((((y * 2 + u) * 2 + row_x) * 2 + row_z) * 2 + row_c) * R + row % R
    qpos = jnp.broadcast_to((offset[0] + row).astype(jnp.float32)[None, :], (8, ROWS))

    q = absorb(q_all, w_uk)
    state = attend(q, qpos, near)
    state, w_z = lax.optimization_barrier((state, w_z))
    w_zc = lax.ppermute(w_z, "c", SWAP)
    state, far, w_c, w_zc = lax.optimization_barrier((state, far, w_c, w_zc))
    own, send = attend(q, qpos, far, state, value_up_weight)
    own, send = merge_over("c", own, send)
    own, send = merge_over("x", own, send)
    heads = call(
        merge_last_kernel, jax.ShapeDtypeStruct((16, R, HG * VDIM), jnp.bfloat16), MIB, MIB
    )(own, lax.ppermute(send, "z", SWAP))

    rows = lax.all_to_all(heads, ("y", "u", "x"), 0, 0, tiled=True).reshape(16 * R, HG * VDIM)
    ncol = w_out.shape[1]
    sums = call(
        project_kernel,
        jax.ShapeDtypeStruct((4, 16 * R, ncol), jnp.bfloat16),
        2 * 16 * R * HG * VDIM * 4 * ncol,
        4 * MIB,
        in_specs=[pl.BlockSpec(memory_space=pltpu.SMEM)]
        + [pl.BlockSpec(memory_space=pltpu.VMEM)] * 5,
    )(jnp.stack([z, c]), rows, w_own, w_z, w_c, w_zc)
    sums = lax.all_to_all(
        sums.reshape(16, 4 * R, ncol), ("z", "c", "head"), 0, 0, tiled=True
    )
    out = call(
        finish_kernel,
        jax.ShapeDtypeStruct((ncol, 16 * R), jnp.bfloat16),
        MIB,
        MIB,
        scratch_shapes=[pltpu.VMEM((16 * R, 128), jnp.float32)],
    )(sums)
    return jnp.transpose(out)


def solution(mesh):
    grid = Mesh(mesh.devices.reshape(4, 2, 2, 2, 2, 4), CTX + ("head",))
    return jax.shard_map(
        local,
        mesh=grid,
        in_specs=(
            P(CTX, "head"),
            P(CTX, "head"),
            P(None, CTX, None),
            P(None, CTX, None),
            P(None, CTX),
            P(),
            P("head", None, None),
            P("head", None, None),
            P("head", CTX),
        ),
        out_specs=P("head", CTX),
        check_vma=False,
    )
```

```python
import functools

import jax
import jax.numpy as jnp
from jax import lax
from jax.experimental import pallas as pl
from jax.experimental.pallas import tpu as pltpu
from jax.sharding import Mesh, PartitionSpec as P

ROPE = 64
NOPE = 128
RANK = 512
VDIM = 128
HG = 16
R = 16
GROUP = 8
ROWS = GROUP * R
ITEMS = HG * ROWS
KEYW = RANK + 128
ITEMW = RANK + 256
SENDW = HG * VDIM + 128
SCALE2 = (NOPE + ROPE) ** -0.5 * 1.4426950408889634
NEG = -1e30
CTX = ("y", "u", "x", "z", "c")
SWAP = ((0, 1), (1, 0))
MIB = 1 << 20


def shift(n, d):
    return [(i, (i + d) % n) for i in range(n)]


def call(kernel, out_shape, vmem=40, **kw):
    return pl.pallas_call(
        kernel,
        out_shape=out_shape,
        compiler_params=pltpu.CompilerParams(vmem_limit_bytes=vmem * MIB),
        cost_estimate=pl.CostEstimate(flops=1, bytes_accessed=1, transcendentals=0),
        **kw,
    )


def nt_dot(a, b):
    return lax.dot_general(a, b, (((1,), (1,)), ((), ())), preferred_element_type=jnp.float32)


def pack_keys_kernel(latent_ref, key_rope_ref, pos_ref, key_ref):
    key_ref[:, :RANK] = latent_ref[...]
    pos = pos_ref[...].astype(jnp.float32)
    high = jnp.floor(pos * (1 / 128))
    row = lax.broadcasted_iota(jnp.int32, key_rope_ref.shape, 0)
    ext = jnp.where(row == 0, high, jnp.where(row == 1, pos - high * 128, 0.0))
    ext = jnp.concatenate([key_rope_ref[...].astype(jnp.float32), ext], axis=0)
    key_ref[:, RANK:] = jnp.transpose(ext).astype(jnp.bfloat16)


def pack_keys(latent, k_rope, key_pos):
    return call(
        pack_keys_kernel,
        jax.ShapeDtypeStruct((latent.shape[0], KEYW), jnp.bfloat16),
        vmem=60,
    )(latent, jnp.transpose(k_rope), key_pos)


def pack_far_kernel(w_ref, query_ref, rope_ref, out_ref):
    ncol = w_ref.shape[0]
    out_ref[:ncol] = w_ref[...]
    out_ref[ncol : ncol + R] = query_ref[...]
    out_ref[ncol + R :, : HG * ROPE] = rope_ref[...]
    out_ref[ncol + R :, HG * ROPE :] = jnp.zeros((R, HG * (NOPE - ROPE)), jnp.bfloat16)


def pack_far(w_out, query, q_rope):
    ncol = w_out.shape[1]
    return call(
        pack_far_kernel,
        jax.ShapeDtypeStruct((ncol + 2 * R, HG * VDIM), jnp.bfloat16),
        vmem=60,
    )(jnp.transpose(w_out), query, q_rope)


def unpack_queries_kernel(own_ref, far_ref, out_ref):
    ncol = own_ref.shape[0] - 2 * R
    for i, ref in enumerate((own_ref, far_ref)):
        out_ref[i * R : (i + 1) * R, : HG * NOPE] = ref[ncol : ncol + R]
        out_ref[i * R : (i + 1) * R, HG * NOPE :] = ref[ncol + R :, : HG * ROPE]


def unpack_queries(own, far):
    return call(
        unpack_queries_kernel,
        jax.ShapeDtypeStruct((2 * R, HG * (NOPE + ROPE)), jnp.bfloat16),
    )(own, far)


def absorb_kernel(*refs):
    q_refs, (w_ref, out_ref) = refs[:4], refs[4:]
    lane = lax.broadcasted_iota(jnp.int32, (ROWS, 128), 1)
    row = lax.broadcasted_iota(jnp.int32, (ROWS, 128), 0)
    one_hot = (lane == row).astype(jnp.bfloat16)

    def columns(start):
        return jnp.concatenate([ref[:, start : start + 128] for ref in q_refs], axis=0)

    for h in range(HG):
        rows = slice(h * ROWS, (h + 1) * ROWS)
        latent = jnp.dot(columns(h * NOPE), w_ref[h], preferred_element_type=jnp.float32)
        out_ref[rows, :RANK] = latent.astype(jnp.bfloat16)
        pair = columns(HG * NOPE + (h // 2) * 128).astype(jnp.float32)
        if h % 2:
            pair = pltpu.roll(pair, ROPE, 1)
        rope = jnp.where(lane < ROPE, pair, 0.0)
        out_ref[rows, RANK : RANK + 128] = rope.astype(jnp.bfloat16)
        out_ref[rows, RANK + 128 :] = one_hot


def absorb(queries, w_uk):
    return call(absorb_kernel, jax.ShapeDtypeStruct((ITEMS, ITEMW), jnp.bfloat16))(
        *queries, w_uk
    )


def pack_stats(stats):
    high = stats.astype(jnp.bfloat16).astype(jnp.float32)
    mid = (stats - high).astype(jnp.bfloat16).astype(jnp.float32)
    low = stats - high - mid
    packed = high + pltpu.roll(mid, HG, 1) + pltpu.roll(low, 2 * HG, 1)
    return packed.astype(jnp.bfloat16)


def unpack_stats(packed):
    packed = packed.astype(jnp.float32)
    return packed + pltpu.roll(packed, 128 - HG, 1) + pltpu.roll(packed, 128 - 2 * HG, 1)


def attend_kernel(pieces, last, *refs):
    q_ref, qpos_ref = refs[:2]
    key_refs = refs[2 : 2 + pieces]
    rest = refs[2 + pieces :]
    if last:
        acc_in, st_in, v_ref, keep_ref, send_ref, ext_ref, lse_ref = rest
    else:
        acc_out, st_out, ext_ref = rest
    keys = key_refs[0].shape[0]
    step = pl.program_id(0)

    @pl.when(step == 0)
    def _():
        qpos = qpos_ref[0:1, :]
        for i, key_ref in enumerate(key_refs):
            ext = key_ref[:, RANK:]
            ext_ref[i, :, :128] = ext
            ext = ext.astype(jnp.float32)
            pos = ext[:, ROPE : ROPE + 1] * 128.0 + ext[:, ROPE + 1 : ROPE + 2]
            ext_ref[i, :, 128:] = jnp.where(pos <= qpos, 0.0, NEG).astype(jnp.bfloat16)
        if last:
            lse_ref[...] = jnp.zeros_like(lse_ref)

    tile = q_ref.shape[0]
    q_latent, q_ext = q_ref[:, :RANK], q_ref[:, RANK:]
    scores = [
        (nt_dot(q_latent, key_refs[i][:, :RANK]) + nt_dot(q_ext, ext_ref[i])) * SCALE2
        for i in range(pieces)
    ]
    top = functools.reduce(jnp.maximum, [jnp.max(s, axis=1, keepdims=True) for s in scores])
    if last:
        top = jnp.maximum(top, st_in[:, 0:1])
    weights = [jnp.exp2(s - top) for s in scores]
    total = sum(jnp.sum(w, axis=1, keepdims=True) for w in weights)
    acc = sum(
        jnp.dot(w.astype(jnp.bfloat16), key_refs[i][:, :RANK], preferred_element_type=jnp.float32)
        for i, w in enumerate(weights)
    )
    if not last:
        acc_out[...] = acc
        lane = lax.broadcasted_iota(jnp.int32, (tile, 128), 1)
        st_out[...] = jnp.where(lane == 0, top, total)
        return

    keep = jnp.exp2(st_in[:, 0:1] - top)
    total = total + keep * st_in[:, 1:2]
    context = ((acc + keep * acc_in[...]) / total).astype(jnp.bfloat16)
    lse = top + jnp.log2(total)
    half = ROWS // 2
    lane = lax.broadcasted_iota(jnp.int32, (ROWS, 128), 1)
    for i in range(tile // ROWS):
        rows = slice(i * ROWS, (i + 1) * ROWS)
        head = step * (tile // ROWS) + i
        out = jnp.dot(context[rows], v_ref[i], preferred_element_type=jnp.float32)
        out = out.astype(jnp.bfloat16)
        cols = pl.ds(pl.multiple_of(head * VDIM, VDIM), VDIM)
        keep_ref[:, cols] = out[:half]
        send_ref[:, cols] = out[half:]
        lse_ref[...] = jnp.where(lane == head, lse[rows], lse_ref[...])

    @pl.when(step == pl.num_programs(0) - 1)
    def _():
        packed = pack_stats(lse_ref[...])
        keep_ref[:, HG * VDIM :] = packed[:half]
        send_ref[:, HG * VDIM :] = packed[half:]


def attend(q, qpos, pieces, state=None, value_weight=None, tile=512):
    n, keys = len(pieces), pieces[0].shape[0]
    last = state is not None
    whole = lambda shape: pl.BlockSpec(shape, lambda i: (0, 0))
    part = lambda width: pl.BlockSpec((tile, width), lambda i: (i, 0))
    carried = [part(RANK), part(128)]
    in_specs = [part(ITEMW), whole((8, 128))] + [whole((keys, KEYW))] * n
    scratch = [pltpu.VMEM((n, keys, 256), jnp.bfloat16)]
    args = [q, qpos, *pieces]
    if last:
        heads = tile // ROWS
        in_specs += carried + [pl.BlockSpec((heads, RANK, VDIM), lambda i: (i, 0, 0))]
        args += [*state, value_weight]
        half = jax.ShapeDtypeStruct((ROWS // 2, SENDW), jnp.bfloat16)
        out_shape, out_specs = (half, half), [whole((ROWS // 2, SENDW))] * 2
        scratch.append(pltpu.VMEM((ROWS, 128), jnp.float32))
    else:
        out_shape = (
            jax.ShapeDtypeStruct((ITEMS, RANK), jnp.float32),
            jax.ShapeDtypeStruct((ITEMS, 128), jnp.float32),
        )
        out_specs = carried
    return call(
        functools.partial(attend_kernel, n, last),
        out_shape,
        grid=(ITEMS // tile,),
        in_specs=in_specs,
        out_specs=out_specs,
        scratch_shapes=scratch,
    )(*args)


def merge(a_ref, b_ref):
    a, b = (unpack_stats(ref[:, HG * VDIM :]) for ref in (a_ref, b_ref))
    top = jnp.maximum(a, b)
    wa, wb = jnp.exp2(a - top), jnp.exp2(b - top)
    total = wa + wb
    wa, wb = wa / total, wb / total
    out = []
    for h in range(HG):
        cols = slice(h * VDIM, (h + 1) * VDIM)
        head = a_ref[:, cols].astype(jnp.float32) * wa[:, h : h + 1]
        head = head + b_ref[:, cols].astype(jnp.float32) * wb[:, h : h + 1]
        out.append((cols, head.astype(jnp.bfloat16)))
    return out, top + jnp.log2(total)


def merge_kernel(a_ref, b_ref, own_ref, send_ref):
    heads, lse = merge(a_ref, b_ref)
    half = own_ref.shape[0]
    lane = lax.broadcasted_iota(jnp.int32, lse.shape, 1)
    packed = pack_stats(jnp.where(lane < HG, lse, 0.0))
    for cols, head in heads + [(slice(HG * VDIM, SENDW), packed)]:
        own_ref[:, cols] = head[:half]
        send_ref[:, cols] = head[half:]


def merge_last_kernel(a_ref, b_ref, out_ref):
    heads, _ = merge(a_ref, b_ref)
    for cols, head in heads:
        for i in range(out_ref.shape[0]):
            out_ref[i, :, cols] = head


def merge_over(axis, own, send, *beside):
    half = jax.ShapeDtypeStruct((own.shape[0] // 2, SENDW), jnp.bfloat16)
    received, *beside = lax.optimization_barrier((lax.ppermute(send, axis, SWAP), *beside))
    return *call(merge_kernel, (half, half))(own, received), *beside


def project_kernel(zc_ref, x_ref, *refs):
    out_ref = refs[-1]
    z, c = zc_ref[0], zc_ref[1]
    ncol = out_ref.shape[2]
    for k in range(4):
        to_z = z if k % 2 == 0 else 1 - z
        to_c = c if k < 2 else 1 - c
        out_ref[to_z * 2 + to_c] = nt_dot(x_ref[...], refs[k][:ncol]).astype(jnp.bfloat16)


def finish_kernel(sums_ref, out_ref, row_ref):
    ncol = sums_ref.shape[2]
    row_ref[...] = jnp.zeros_like(row_ref)
    for zc in range(4):
        total = sum(sums_ref[zc * 4 + h].astype(jnp.float32) for h in range(4))
        for i in range(4):
            start = (i * 4 + zc) * R
            row_ref[start : start + R, :ncol] = total[i * R : (i + 1) * R]
    out_ref[...] = jnp.transpose(row_ref[...])[:ncol].astype(jnp.bfloat16)


def local(query_unrotated, q_rope, latent, k_rope, key_pos, offset, w_uk, value_up_weight, w_out):
    y, u, x, z, c = (lax.axis_index(n) for n in CTX)

    keys = pack_keys(latent[0], k_rope[0], key_pos)
    keys_u = lax.ppermute(keys, "u", SWAP)
    keys_up = lax.ppermute(keys, "y", shift(4, 1))
    keys_down = lax.ppermute(keys, "y", shift(4, 3))
    keys_far = lax.ppermute(keys, "y", shift(4, 2))
    keys_u, keys_up, keys_down = lax.optimization_barrier((keys_u, keys_up, keys_down))
    far_u = lax.ppermute(keys_u, "y", shift(4, 2))
    up_u = lax.ppermute(keys_up, "u", SWAP)
    down_u = lax.ppermute(keys_down, "u", SWAP)

    own_w = pack_far(w_out, query_unrotated, q_rope)
    z_w = lax.ppermute(own_w, "z", SWAP)
    q_z = unpack_queries(own_w, z_w)
    q_x = lax.ppermute(q_z, "x", SWAP)
    queries = (q_z, q_x, lax.ppermute(q_z, "c", SWAP), lax.ppermute(q_x, "c", SWAP))

    row = jnp.arange(ROWS, dtype=jnp.int32)
    part = row // R
    row_z = jnp.where(part % 2 == 0, z, 1 - z)
    row_x = jnp.where(part // 2 % 2 == 0, x, 1 - x)
    row_c = jnp.where(part < 4, c, 1 - c)
    row = ((((y * 2 + u) * 2 + row_x) * 2 + row_z) * 2 + row_c) * R + row % R
    qpos = jnp.broadcast_to((offset[0] + row).astype(jnp.float32)[None, :], (8, ROWS))

    q = absorb(queries, w_uk)
    state = attend(q, qpos, [keys, keys_u, keys_up, keys_down, keys_far])
    state, far = lax.optimization_barrier((state, [far_u, up_u, down_u]))
    own, send = attend(q, qpos, far, state, value_up_weight)
    own, send = merge_over("c", own, send)
    send, own_w, z_w = lax.optimization_barrier((send, own_w, z_w))
    own, send, c_w = merge_over("x", own, send, lax.ppermute(own_w, "c", SWAP))
    send, z_w = lax.optimization_barrier((send, z_w))
    send, zc_w = lax.optimization_barrier(
        (lax.ppermute(send, "z", SWAP), lax.ppermute(z_w, "c", SWAP))
    )
    heads = call(merge_last_kernel, jax.ShapeDtypeStruct((16, R, HG * VDIM), jnp.bfloat16))(
        own, send
    )

    rows = lax.all_to_all(heads, ("y", "u", "x"), 0, 0, tiled=True).reshape(16 * R, HG * VDIM)
    ncol = w_out.shape[1]
    sums = call(
        project_kernel,
        jax.ShapeDtypeStruct((4, 16 * R, ncol), jnp.bfloat16),
        in_specs=[pl.BlockSpec(memory_space=pltpu.SMEM)]
        + [pl.BlockSpec(memory_space=pltpu.VMEM)] * 5,
    )(jnp.stack([z, c]), rows, own_w, z_w, c_w, zc_w)
    sums = lax.all_to_all(
        sums.reshape(16, 4 * R, ncol), ("z", "c", "head"), 0, 0, tiled=True
    )
    out = call(
        finish_kernel,
        jax.ShapeDtypeStruct((ncol, 16 * R), jnp.bfloat16),
        scratch_shapes=[pltpu.VMEM((16 * R, 128), jnp.float32)],
    )(sums)
    return jnp.transpose(out)


def solution(mesh):
    grid = Mesh(mesh.devices.reshape(4, 2, 2, 2, 2, 4), CTX + ("head",))
    return jax.shard_map(
        local,
        mesh=grid,
        in_specs=(
            P(CTX, "head"),
            P(CTX, "head"),
            P(None, CTX, None),
            P(None, CTX, None),
            P(None, CTX),
            P(),
            P("head", None, None),
            P("head", None, None),
            P("head", CTX),
        ),
        out_specs=P("head", CTX),
        check_vma=False,
    )
```

```python
import functools

import jax
import jax.numpy as jnp
from jax import lax
from jax.experimental import pallas as pl
from jax.experimental.pallas import tpu as pltpu
from jax.sharding import Mesh, PartitionSpec as P

ROPE = 64
NOPE = 128
RANK = 512
VDIM = 128
HG = 16
R = 16
GROUP = 8
ROWS = GROUP * R
ITEMS = HG * ROWS
KEYW = RANK + 128
ITEMW = RANK + 256
SENDW = HG * VDIM + 128
SCALE2 = (NOPE + ROPE) ** -0.5 * 1.4426950408889634
NEG = -1e30
CTX = ("y", "x", "z", "c")
RING = (0, 1, 3, 2)
SWAP = ((0, 1), (1, 0))
MIB = 1 << 20


def shift(d):
    return [(i, (i + d) % 4) for i in range(4)]


def call(kernel, out_shape, vmem=40, **kw):
    return pl.pallas_call(
        kernel,
        out_shape=out_shape,
        compiler_params=pltpu.CompilerParams(vmem_limit_bytes=vmem * MIB),
        cost_estimate=pl.CostEstimate(flops=1, bytes_accessed=1, transcendentals=0),
        **kw,
    )


def nt_dot(a, b):
    return lax.dot_general(a, b, (((1,), (1,)), ((), ())), preferred_element_type=jnp.float32)


def pack_keys_kernel(latent_ref, key_rope_ref, pos_ref, key_ref):
    key_ref[:, :RANK] = latent_ref[...]
    pos = pos_ref[...].astype(jnp.float32)
    high = jnp.floor(pos * (1 / 128))
    row = lax.broadcasted_iota(jnp.int32, key_rope_ref.shape, 0)
    ext = jnp.where(row == 0, high, jnp.where(row == 1, pos - high * 128, 0.0))
    ext = jnp.concatenate([key_rope_ref[...].astype(jnp.float32), ext], axis=0)
    key_ref[:, RANK:] = jnp.transpose(ext).astype(jnp.bfloat16)


def pack_keys(latent, k_rope, key_pos):
    return call(
        pack_keys_kernel,
        jax.ShapeDtypeStruct((latent.shape[0], KEYW), jnp.bfloat16),
        vmem=60,
    )(latent, jnp.transpose(k_rope), key_pos)


def pack_queries_kernel(query_ref, rope_ref, out_ref):
    out_ref[:, : HG * NOPE] = query_ref[...]
    out_ref[:, HG * NOPE :] = rope_ref[...]


def pack_queries(query, q_rope):
    return call(
        pack_queries_kernel,
        jax.ShapeDtypeStruct((R, HG * (NOPE + ROPE)), jnp.bfloat16),
        vmem=60,
    )(query, q_rope)


def join_kernel(*refs):
    start = 0
    for ref in refs[:-1]:
        refs[-1][start : start + ref.shape[0]] = ref[...]
        start += ref.shape[0]


def join(parts):
    shape = (sum(part.shape[0] for part in parts), parts[0].shape[1])
    return call(join_kernel, jax.ShapeDtypeStruct(shape, jnp.bfloat16))(*parts)


def absorb_kernel(*refs):
    q_refs, (w_ref, out_ref) = refs[:2], refs[2:]
    lane = lax.broadcasted_iota(jnp.int32, (ROWS, 128), 1)
    row = lax.broadcasted_iota(jnp.int32, (ROWS, 128), 0)
    one_hot = (lane == row).astype(jnp.bfloat16)

    def columns(start):
        return jnp.concatenate([ref[:, start : start + 128] for ref in q_refs], axis=0)

    for h in range(HG):
        rows = slice(h * ROWS, (h + 1) * ROWS)
        latent = jnp.dot(columns(h * NOPE), w_ref[h], preferred_element_type=jnp.float32)
        out_ref[rows, :RANK] = latent.astype(jnp.bfloat16)
        pair = columns(HG * NOPE + (h // 2) * 128).astype(jnp.float32)
        if h % 2:
            pair = pltpu.roll(pair, ROPE, 1)
        rope = jnp.where(lane < ROPE, pair, 0.0)
        out_ref[rows, RANK : RANK + 128] = rope.astype(jnp.bfloat16)
        out_ref[rows, RANK + 128 :] = one_hot


def absorb(queries, w_uk):
    return call(absorb_kernel, jax.ShapeDtypeStruct((ITEMS, ITEMW), jnp.bfloat16))(
        *queries, w_uk
    )


def pack_stats(stats):
    high = stats.astype(jnp.bfloat16).astype(jnp.float32)
    mid = (stats - high).astype(jnp.bfloat16).astype(jnp.float32)
    low = stats - high - mid
    packed = high + pltpu.roll(mid, HG, 1) + pltpu.roll(low, 2 * HG, 1)
    return packed.astype(jnp.bfloat16)


def unpack_stats(packed):
    packed = packed.astype(jnp.float32)
    return packed + pltpu.roll(packed, 128 - HG, 1) + pltpu.roll(packed, 128 - 2 * HG, 1)


def attend_kernel(pieces, last, *refs):
    q_ref, qpos_ref = refs[:2]
    piece_refs = refs[2 : 2 + pieces]
    rest = refs[2 + pieces :]
    if last:
        acc_in, st_in, v_ref, keep_ref, send_ref, key_ref, lse_ref = rest
    else:
        acc_out, st_out, key_ref = rest
    step = pl.program_id(0)

    @pl.when(step == 0)
    def _():
        qpos = qpos_ref[0:1, :]
        start = 0
        for ref in piece_refs:
            rows = slice(start, start + ref.shape[0])
            start += ref.shape[0]
            key_ref[rows, :KEYW] = ref[...]
            ext = ref[:, RANK:].astype(jnp.float32)
            pos = ext[:, ROPE : ROPE + 1] * 128.0 + ext[:, ROPE + 1 : ROPE + 2]
            key_ref[rows, KEYW:] = jnp.where(pos <= qpos, 0.0, NEG).astype(jnp.bfloat16)
        if last:
            lse_ref[...] = jnp.zeros_like(lse_ref)

    tile = q_ref.shape[0]
    scores = nt_dot(q_ref[...], key_ref[...]) * SCALE2
    top = jnp.max(scores, axis=1, keepdims=True)
    if last:
        top = jnp.maximum(top, st_in[:, 0:1])
    weights = jnp.exp2(scores - top)
    total = jnp.sum(weights, axis=1, keepdims=True)
    acc = jnp.dot(
        weights.astype(jnp.bfloat16), key_ref[:, :RANK], preferred_element_type=jnp.float32
    )
    if not last:
        acc_out[...] = acc
        lane = lax.broadcasted_iota(jnp.int32, (tile, 128), 1)
        st_out[...] = jnp.where(lane == 0, top, total)
        return

    keep = jnp.exp2(st_in[:, 0:1] - top)
    total = total + keep * st_in[:, 1:2]
    context = ((acc + keep * acc_in[...]) / total).astype(jnp.bfloat16)
    lse = top + jnp.log2(total)
    half = ROWS // 2
    lane = lax.broadcasted_iota(jnp.int32, (ROWS, 128), 1)
    for i in range(tile // ROWS):
        rows = slice(i * ROWS, (i + 1) * ROWS)
        head = step * (tile // ROWS) + i
        out = jnp.dot(context[rows], v_ref[i], preferred_element_type=jnp.float32)
        out = out.astype(jnp.bfloat16)
        cols = pl.ds(pl.multiple_of(head * VDIM, VDIM), VDIM)
        keep_ref[:, cols] = out[:half]
        send_ref[:, cols] = out[half:]
        lse_ref[...] = jnp.where(lane == head, lse[rows], lse_ref[...])

    @pl.when(step == pl.num_programs(0) - 1)
    def _():
        packed = pack_stats(lse_ref[...])
        keep_ref[:, HG * VDIM :] = packed[:half]
        send_ref[:, HG * VDIM :] = packed[half:]


def attend(q, qpos, pieces, state=None, value_weight=None, tile=512):
    n, keys = len(pieces), sum(piece.shape[0] for piece in pieces)
    last = state is not None
    whole = lambda shape: pl.BlockSpec(shape, lambda i: (0, 0))
    part = lambda width: pl.BlockSpec((tile, width), lambda i: (i, 0))
    carried = [part(RANK), part(128)]
    in_specs = [part(ITEMW), whole((8, 128))] + [whole(piece.shape) for piece in pieces]
    scratch = [pltpu.VMEM((keys, ITEMW), jnp.bfloat16)]
    args = [q, qpos, *pieces]
    if last:
        heads = tile // ROWS
        in_specs += carried + [pl.BlockSpec((heads, RANK, VDIM), lambda i: (i, 0, 0))]
        args += [*state, value_weight]
        half = jax.ShapeDtypeStruct((ROWS // 2, SENDW), jnp.bfloat16)
        out_shape, out_specs = (half, half), [whole((ROWS // 2, SENDW))] * 2
        scratch.append(pltpu.VMEM((ROWS, 128), jnp.float32))
    else:
        out_shape = (
            jax.ShapeDtypeStruct((ITEMS, RANK), jnp.float32),
            jax.ShapeDtypeStruct((ITEMS, 128), jnp.float32),
        )
        out_specs = carried
    return call(
        functools.partial(attend_kernel, n, last),
        out_shape,
        grid=(ITEMS // tile,),
        in_specs=in_specs,
        out_specs=out_specs,
        scratch_shapes=scratch,
    )(*args)


def merge(refs):
    stats = [unpack_stats(ref[:, HG * VDIM :]) for ref in refs]
    top = functools.reduce(jnp.maximum, stats)
    weights = [jnp.exp2(s - top) for s in stats]
    total = sum(weights)
    weights = [w / total for w in weights]
    out = []
    for h in range(HG):
        cols = slice(h * VDIM, (h + 1) * VDIM)
        head = sum(
            ref[:, cols].astype(jnp.float32) * w[:, h : h + 1] for ref, w in zip(refs, weights)
        )
        out.append((cols, head.astype(jnp.bfloat16)))
    return out, top + jnp.log2(total)


def merge_core_kernel(a_ref, b_ref, *out_refs):
    heads, lse = merge((a_ref, b_ref))
    lane = lax.broadcasted_iota(jnp.int32, lse.shape, 1)
    packed = pack_stats(jnp.where(lane < HG, lse, 0.0))
    for cols, head in heads + [(slice(HG * VDIM, SENDW), packed)]:
        for i, ref in enumerate(out_refs):
            ref[:, cols] = head[i * R : (i + 1) * R]


def merge_ring_kernel(*refs):
    heads, _ = merge(refs[:-1])
    for cols, head in heads:
        for i in range(refs[-1].shape[0]):
            refs[-1][i, :, cols] = head


def project_kernel(zc_ref, x_ref, *refs):
    out_ref = refs[-1]
    z, c = zc_ref[0], zc_ref[1]
    for k in range(4):
        to_z = z if k % 2 == 0 else 1 - z
        to_c = c if k < 2 else 1 - c
        out_ref[to_z * 2 + to_c] = nt_dot(x_ref[...], refs[k][...]).astype(jnp.bfloat16)


def finish_kernel(sums_ref, out_ref, row_ref):
    ncol = sums_ref.shape[2]
    row_ref[...] = jnp.zeros_like(row_ref)
    for zc in range(4):
        total = sum(sums_ref[zc * 4 + h].astype(jnp.float32) for h in range(4))
        for i in range(4):
            start = (i * 4 + zc) * R
            row_ref[start : start + R, :ncol] = total[i * R : (i + 1) * R]
    out_ref[...] = jnp.transpose(row_ref[...])[:ncol].astype(jnp.bfloat16)


def local(query_unrotated, q_rope, latent, k_rope, key_pos, offset, w_uk, value_up_weight, w_out):
    y, x, z, c = (lax.axis_index(n) for n in CTX)

    keys = pack_keys(latent[0], k_rope[0], key_pos)
    q_own = pack_queries(query_unrotated, q_rope)
    z_keys = lax.ppermute(keys, "z", SWAP)
    up, down = (lax.ppermute(keys, "y", shift(d)) for d in (1, 3))
    q_ring = [lax.ppermute(q_own, "x", shift(d)) for d in RING[1:]]
    z_keys, up, down, q_ring, keys, q_own = lax.optimization_barrier(
        (z_keys, up, down, q_ring, keys, q_own)
    )
    near = [join([keys, z_keys]), up, down]
    far = [lax.ppermute(near[0], "y", shift(2))]
    far += [lax.ppermute(z_keys, "y", shift(d)) for d in (1, 3)]
    q_chip = join([q_own, *q_ring])
    q_core = lax.ppermute(q_chip, "c", SWAP)
    q_core, w_own = lax.optimization_barrier((q_core, jnp.transpose(w_out)))
    z_w = lax.ppermute(w_own, "z", SWAP)

    row = jnp.arange(ROWS, dtype=jnp.int32)
    part = row // R
    row_x = (x - jnp.array(RING, jnp.int32)[part % 4]) % 4
    row_c = jnp.where(part < 4, c, 1 - c)
    row = (((y * 4 + row_x) * 2 + z) * 2 + row_c) * R + row % R
    qpos = jnp.broadcast_to((offset[0] + row).astype(jnp.float32)[None, :], (8, ROWS))

    q = absorb((q_chip, q_core), w_uk)
    state = attend(q, qpos, near)
    state, far = lax.optimization_barrier((state, far))
    keep, send = attend(q, qpos, far, state, value_up_weight)

    z_w, send = lax.optimization_barrier((z_w, send))
    parts = call(
        merge_core_kernel, [jax.ShapeDtypeStruct((R, SENDW), jnp.bfloat16)] * 4
    )(keep, lax.ppermute(send, "c", SWAP))
    parts = [parts[0]] + [
        lax.ppermute(part, "x", shift(-d % 4)) for part, d in zip(parts[1:], RING[1:])
    ]
    heads = call(merge_ring_kernel, jax.ShapeDtypeStruct((16, R, HG * VDIM), jnp.bfloat16))(
        *parts
    )

    rows = lax.all_to_all(heads, ("y", "x"), 0, 0, tiled=True).reshape(16 * R, HG * VDIM)
    c_w = lax.ppermute(w_own, "c", SWAP)
    zc_w = lax.ppermute(z_w, "c", SWAP)
    ncol = w_out.shape[1]
    sums = call(
        project_kernel,
        jax.ShapeDtypeStruct((4, 16 * R, ncol), jnp.bfloat16),
        in_specs=[pl.BlockSpec(memory_space=pltpu.SMEM)]
        + [pl.BlockSpec(memory_space=pltpu.VMEM)] * 5,
    )(jnp.stack([z, c]), rows, w_own, z_w, c_w, zc_w)
    sums = lax.all_to_all(
        sums.reshape(16, 4 * R, ncol), ("z", "c", "head"), 0, 0, tiled=True
    )
    out = call(
        finish_kernel,
        jax.ShapeDtypeStruct((ncol, 16 * R), jnp.bfloat16),
        scratch_shapes=[pltpu.VMEM((16 * R, 128), jnp.float32)],
    )(sums)
    return jnp.transpose(out)


def solution(mesh):
    grid = Mesh(mesh.devices.reshape(4, 4, 2, 2, 4), CTX + ("head",))
    return jax.shard_map(
        local,
        mesh=grid,
        in_specs=(
            P(CTX, "head"),
            P(CTX, "head"),
            P(None, CTX, None),
            P(None, CTX, None),
            P(None, CTX),
            P(),
            P("head", None, None),
            P("head", None, None),
            P("head", CTX),
        ),
        out_specs=P("head", CTX),
        check_vma=False,
    )
```

```python
import functools

import jax
import jax.numpy as jnp
from jax import lax
from jax.experimental import pallas as pl
from jax.experimental.pallas import tpu as pltpu
from jax.sharding import Mesh, PartitionSpec as P

ROPE = 64
NOPE = 128
RANK = 512
VDIM = 128
HG = 16
R = 16
GROUP = 8
ROWS = GROUP * R
ITEMS = HG * ROWS
KEYW = RANK + 128
ITEMW = RANK + 256
SENDW = HG * VDIM + 128
SCALE2 = (NOPE + ROPE) ** -0.5 * 1.4426950408889634
NEG = -1e30
CTX = ("y", "x", "z", "c")
RING = (0, 1, 3, 2)
SWAP = ((0, 1), (1, 0))
MIB = 1 << 20


def shift(d):
    return [(i, (i + d) % 4) for i in range(4)]


def call(kernel, out_shape, vmem=40, **kw):
    return pl.pallas_call(
        kernel,
        out_shape=out_shape,
        compiler_params=pltpu.CompilerParams(vmem_limit_bytes=vmem * MIB),
        cost_estimate=pl.CostEstimate(flops=1, bytes_accessed=1, transcendentals=0),
        **kw,
    )


def nt_dot(a, b):
    return lax.dot_general(a, b, (((1,), (1,)), ((), ())), preferred_element_type=jnp.float32)


HBM = pl.BlockSpec(memory_space=pltpu.HBM)


def in_hbm(*arrays):
    return [pltpu.with_memory_space_constraint(a, pltpu.HBM) for a in arrays]


def pack_keys_kernel(latent_ref, key_rope_ref, pos_ref, key_ref, rope, pos, sems):
    copies = [
        pltpu.make_async_copy(key_rope_ref, rope, sems.at[0]),
        pltpu.make_async_copy(pos_ref, pos, sems.at[1]),
        pltpu.make_async_copy(latent_ref, key_ref.at[:, :RANK], sems.at[2]),
    ]
    for copy in copies:
        copy.start()
    copies[0].wait()
    copies[1].wait()
    where = pos[...].astype(jnp.float32)
    high = jnp.floor(where * (1 / 128))
    row = lax.broadcasted_iota(jnp.int32, rope.shape, 0)
    ext = jnp.where(row == 0, high, jnp.where(row == 1, where - high * 128, 0.0))
    ext = jnp.concatenate([rope[...].astype(jnp.float32), ext], axis=0)
    key_ref[:, RANK:] = jnp.transpose(ext).astype(jnp.bfloat16)
    copies[2].wait()


def pack_keys(latent, k_rope, key_pos):
    return call(
        pack_keys_kernel,
        jax.ShapeDtypeStruct((latent.shape[0], KEYW), jnp.bfloat16),
        vmem=16,
        in_specs=[HBM] * 3,
        scratch_shapes=[
            pltpu.VMEM((k_rope.shape[1], k_rope.shape[0]), jnp.bfloat16),
            pltpu.VMEM(key_pos.shape, jnp.int32),
            pltpu.SemaphoreType.DMA((3,)),
        ],
    )(*in_hbm(latent, jnp.transpose(k_rope), key_pos))


def pack_queries_kernel(query_ref, rope_ref, out_ref, sems):
    copies = [
        pltpu.make_async_copy(query_ref, out_ref.at[:, : HG * NOPE], sems.at[0]),
        pltpu.make_async_copy(rope_ref, out_ref.at[:, HG * NOPE :], sems.at[1]),
    ]
    for copy in copies:
        copy.start()
    for copy in copies:
        copy.wait()


def pack_queries(query, q_rope):
    return call(
        pack_queries_kernel,
        jax.ShapeDtypeStruct((R, HG * (NOPE + ROPE)), jnp.bfloat16),
        vmem=16,
        in_specs=[HBM] * 2,
        scratch_shapes=[pltpu.SemaphoreType.DMA((2,))],
    )(*in_hbm(query, q_rope))


def join_kernel(*refs):
    start = 0
    for ref in refs[:-1]:
        refs[-1][start : start + ref.shape[0]] = ref[...]
        start += ref.shape[0]


def join(parts):
    shape = (sum(part.shape[0] for part in parts), parts[0].shape[1])
    return call(join_kernel, jax.ShapeDtypeStruct(shape, jnp.bfloat16))(*parts)


def absorb_kernel(*refs):
    q_refs, (w_ref, out_ref) = refs[:2], refs[2:]
    lane = lax.broadcasted_iota(jnp.int32, (ROWS, 128), 1)
    row = lax.broadcasted_iota(jnp.int32, (ROWS, 128), 0)
    one_hot = (lane == row).astype(jnp.bfloat16)

    def columns(start):
        return jnp.concatenate([ref[:, start : start + 128] for ref in q_refs], axis=0)

    for h in range(HG):
        rows = slice(h * ROWS, (h + 1) * ROWS)
        latent = jnp.dot(columns(h * NOPE), w_ref[h], preferred_element_type=jnp.float32)
        out_ref[rows, :RANK] = latent.astype(jnp.bfloat16)
        pair = columns(HG * NOPE + (h // 2) * 128).astype(jnp.float32)
        if h % 2:
            pair = pltpu.roll(pair, ROPE, 1)
        rope = jnp.where(lane < ROPE, pair, 0.0)
        out_ref[rows, RANK : RANK + 128] = rope.astype(jnp.bfloat16)
        out_ref[rows, RANK + 128 :] = one_hot


def absorb(queries, w_uk):
    return call(absorb_kernel, jax.ShapeDtypeStruct((ITEMS, ITEMW), jnp.bfloat16))(
        *queries, w_uk
    )


def pack_stats(stats):
    high = stats.astype(jnp.bfloat16).astype(jnp.float32)
    mid = (stats - high).astype(jnp.bfloat16).astype(jnp.float32)
    low = stats - high - mid
    packed = high + pltpu.roll(mid, HG, 1) + pltpu.roll(low, 2 * HG, 1)
    return packed.astype(jnp.bfloat16)


def unpack_stats(packed):
    packed = packed.astype(jnp.float32)
    return packed + pltpu.roll(packed, 128 - HG, 1) + pltpu.roll(packed, 128 - 2 * HG, 1)


def attend_kernel(pieces, last, *refs):
    q_ref, qpos_ref = refs[:2]
    piece_refs = refs[2 : 2 + pieces]
    rest = refs[2 + pieces :]
    if last:
        acc_in, st_in, v_ref, keep_ref, send_ref, key_ref, lse_ref = rest
    else:
        acc_out, st_out, key_ref = rest
    step = pl.program_id(0)

    @pl.when(step == 0)
    def _():
        qpos = qpos_ref[0:1, :]
        start = 0
        for ref in piece_refs:
            rows = slice(start, start + ref.shape[0])
            start += ref.shape[0]
            key_ref[rows, :KEYW] = ref[...]
            ext = ref[:, RANK:].astype(jnp.float32)
            pos = ext[:, ROPE : ROPE + 1] * 128.0 + ext[:, ROPE + 1 : ROPE + 2]
            key_ref[rows, KEYW:] = jnp.where(pos <= qpos, 0.0, NEG).astype(jnp.bfloat16)
        if last:
            lse_ref[...] = jnp.zeros_like(lse_ref)

    tile = q_ref.shape[0]
    scores = nt_dot(q_ref[...], key_ref[...]) * SCALE2
    top = jnp.max(scores, axis=1, keepdims=True)
    if last:
        top = jnp.maximum(top, st_in[:, 0:1])
    weights = jnp.exp2(scores - top)
    total = jnp.sum(weights, axis=1, keepdims=True)
    acc = jnp.dot(
        weights.astype(jnp.bfloat16), key_ref[:, :RANK], preferred_element_type=jnp.float32
    )
    if not last:
        acc_out[...] = acc
        lane = lax.broadcasted_iota(jnp.int32, (tile, 128), 1)
        st_out[...] = jnp.where(lane == 0, top, total)
        return

    keep = jnp.exp2(st_in[:, 0:1] - top)
    total = total + keep * st_in[:, 1:2]
    context = ((acc + keep * acc_in[...]) * (1.0 / total)).astype(jnp.bfloat16)
    lse = top + jnp.log2(total)
    half = ROWS // 2
    lane = lax.broadcasted_iota(jnp.int32, (ROWS, 128), 1)
    for i in range(tile // ROWS):
        rows = slice(i * ROWS, (i + 1) * ROWS)
        head = step * (tile // ROWS) + i
        out = jnp.dot(context[rows], v_ref[i], preferred_element_type=jnp.float32)
        out = out.astype(jnp.bfloat16)
        cols = pl.ds(pl.multiple_of(head * VDIM, VDIM), VDIM)
        keep_ref[:, cols] = out[:half]
        send_ref[:, cols] = out[half:]
        lse_ref[...] = jnp.where(lane == head, lse[rows], lse_ref[...])

    @pl.when(step == pl.num_programs(0) - 1)
    def _():
        packed = pack_stats(lse_ref[...])
        keep_ref[:, HG * VDIM :] = packed[:half]
        send_ref[:, HG * VDIM :] = packed[half:]


def attend(q, qpos, pieces, state=None, value_weight=None, tile=512):
    n, keys = len(pieces), sum(piece.shape[0] for piece in pieces)
    last = state is not None
    whole = lambda shape: pl.BlockSpec(shape, lambda i: (0, 0))
    part = lambda width: pl.BlockSpec((tile, width), lambda i: (i, 0))
    carried = [part(RANK), part(128)]
    in_specs = [part(ITEMW), whole((8, 128))] + [whole(piece.shape) for piece in pieces]
    scratch = [pltpu.VMEM((keys, ITEMW), jnp.bfloat16)]
    args = [q, qpos, *pieces]
    if last:
        heads = tile // ROWS
        in_specs += carried + [pl.BlockSpec((heads, RANK, VDIM), lambda i: (i, 0, 0))]
        args += [*state, value_weight]
        half = jax.ShapeDtypeStruct((ROWS // 2, SENDW), jnp.bfloat16)
        out_shape, out_specs = (half, half), [whole((ROWS // 2, SENDW))] * 2
        scratch.append(pltpu.VMEM((ROWS, 128), jnp.float32))
    else:
        out_shape = (
            jax.ShapeDtypeStruct((ITEMS, RANK), jnp.float32),
            jax.ShapeDtypeStruct((ITEMS, 128), jnp.float32),
        )
        out_specs = carried
    return call(
        functools.partial(attend_kernel, n, last),
        out_shape,
        grid=(ITEMS // tile,),
        in_specs=in_specs,
        out_specs=out_specs,
        scratch_shapes=scratch,
    )(*args)


def merge(refs):
    stats = [unpack_stats(ref[:, HG * VDIM :]) for ref in refs]
    top = functools.reduce(jnp.maximum, stats)
    weights = [jnp.exp2(s - top) for s in stats]
    total = sum(weights)
    weights = [w / total for w in weights]
    out = []
    for h in range(HG):
        cols = slice(h * VDIM, (h + 1) * VDIM)
        head = sum(
            ref[:, cols].astype(jnp.float32) * w[:, h : h + 1] for ref, w in zip(refs, weights)
        )
        out.append((cols, head.astype(jnp.bfloat16)))
    return out, top + jnp.log2(total)


def merge_core_kernel(a_ref, b_ref, *out_refs):
    heads, lse = merge((a_ref, b_ref))
    lane = lax.broadcasted_iota(jnp.int32, lse.shape, 1)
    packed = pack_stats(jnp.where(lane < HG, lse, 0.0))
    for cols, head in heads + [(slice(HG * VDIM, SENDW), packed)]:
        for i, ref in enumerate(out_refs):
            ref[:, cols] = head[i * R : (i + 1) * R]


def merge_ring_kernel(*refs):
    heads, _ = merge(refs[:-1])
    for cols, head in heads:
        for i in range(refs[-1].shape[0]):
            refs[-1][i, :, cols] = head


def columns_kernel(zc_ref, *refs):
    z, c = zc_ref[0], zc_ref[1]
    out_ref = refs[4]
    ncol, depth = refs[0].shape
    for k in range(4):
        to_z = z if k % 2 == 0 else 1 - z
        to_c = c if k < 2 else 1 - c
        padded = jnp.concatenate(
            [refs[k][...], jnp.zeros((128 - ncol, depth), jnp.bfloat16)], axis=0
        )
        out_ref[to_z * 2 + to_c] = jnp.transpose(padded)


def project_kernel(x_ref, w_ref, out_ref):
    for k in range(4):
        out = jnp.dot(x_ref[...], w_ref[k], preferred_element_type=jnp.float32)
        out_ref[k] = out[:, : out_ref.shape[2]].astype(jnp.bfloat16)


def finish_kernel(sums_ref, out_ref, row_ref):
    ncol = sums_ref.shape[2]
    row_ref[...] = jnp.zeros_like(row_ref)
    for zc in range(4):
        total = sum(sums_ref[zc * 4 + h].astype(jnp.float32) for h in range(4))
        for i in range(4):
            start = (i * 4 + zc) * R
            row_ref[start : start + R, :ncol] = total[i * R : (i + 1) * R]
    out_ref[...] = jnp.transpose(row_ref[...])[:ncol].astype(jnp.bfloat16)


def local(query_unrotated, q_rope, latent, k_rope, key_pos, offset, w_uk, value_up_weight, w_out):
    y, x, z, c = (lax.axis_index(n) for n in CTX)

    keys = pack_keys(latent[0], k_rope[0], key_pos)
    q_own = pack_queries(query_unrotated, q_rope)
    z_keys = lax.ppermute(keys, "z", SWAP)
    up, down = (lax.ppermute(keys, "y", shift(d)) for d in (1, 3))
    q_ring = [lax.ppermute(q_own, "x", shift(d)) for d in RING[1:]]
    z_keys, up, down, keys = lax.optimization_barrier((z_keys, up, down, keys))
    near = [join([keys, z_keys]), up, down]
    far = [lax.ppermute(near[0], "y", shift(2))]
    far += [lax.ppermute(z_keys, "y", shift(d)) for d in (1, 3)]
    q_chip = join([q_own, *q_ring])
    q_core = lax.ppermute(q_chip, "c", SWAP)
    q_core, w_own = lax.optimization_barrier((q_core, jnp.transpose(w_out)))
    z_w = lax.ppermute(w_own, "z", SWAP)

    row = jnp.arange(ROWS, dtype=jnp.int32)
    part = row // R
    row_x = (x - jnp.array(RING, jnp.int32)[part % 4]) % 4
    row_c = jnp.where(part < 4, c, 1 - c)
    row = (((y * 4 + row_x) * 2 + z) * 2 + row_c) * R + row % R
    qpos = jnp.broadcast_to((offset[0] + row).astype(jnp.float32)[None, :], (8, ROWS))

    q = absorb((q_chip, q_core), w_uk)
    state = attend(q, qpos, near)
    state, far = lax.optimization_barrier((state, far))
    keep, send = attend(q, qpos, far, state, value_up_weight)

    z_w, send = lax.optimization_barrier((z_w, send))
    parts = call(
        merge_core_kernel, [jax.ShapeDtypeStruct((R, SENDW), jnp.bfloat16)] * 4
    )(keep, lax.ppermute(send, "c", SWAP))
    parts = [parts[0]] + [
        lax.ppermute(part, "x", shift(-d % 4)) for part, d in zip(parts[1:], RING[1:])
    ]
    c_w = lax.ppermute(w_own, "c", SWAP)
    zc_w = lax.ppermute(z_w, "c", SWAP)
    parts, c_w, zc_w = lax.optimization_barrier((parts, c_w, zc_w))
    heads = call(merge_ring_kernel, jax.ShapeDtypeStruct((16, R, HG * VDIM), jnp.bfloat16))(
        *parts
    )

    rows = lax.all_to_all(heads, ("y", "x"), 0, 0, tiled=True).reshape(16 * R, HG * VDIM)
    ncol = w_out.shape[1]
    columns = call(
        columns_kernel,
        jax.ShapeDtypeStruct((4, HG * VDIM, 128), jnp.bfloat16),
        in_specs=[pl.BlockSpec(memory_space=pltpu.SMEM)]
        + [pl.BlockSpec(memory_space=pltpu.VMEM)] * 4,
    )(jnp.stack([z, c]), w_own, z_w, c_w, zc_w)
    sums = call(project_kernel, jax.ShapeDtypeStruct((4, 16 * R, ncol), jnp.bfloat16))(
        rows, columns
    )
    sums = lax.all_to_all(
        sums.reshape(16, 4 * R, ncol), ("z", "c", "head"), 0, 0, tiled=True
    )
    out = call(
        finish_kernel,
        jax.ShapeDtypeStruct((ncol, 16 * R), jnp.bfloat16),
        scratch_shapes=[pltpu.VMEM((16 * R, 128), jnp.float32)],
    )(sums)
    return jnp.transpose(out)


def solution(mesh):
    grid = Mesh(mesh.devices.reshape(4, 4, 2, 2, 4), CTX + ("head",))
    return jax.shard_map(
        local,
        mesh=grid,
        in_specs=(
            P(CTX, "head"),
            P(CTX, "head"),
            P(None, CTX, None),
            P(None, CTX, None),
            P(None, CTX),
            P(),
            P("head", None, None),
            P("head", None, None),
            P("head", CTX),
        ),
        out_specs=P("head", CTX),
        check_vma=False,
    )
```

```python
import functools

import jax
import jax.numpy as jnp
from jax import lax
from jax.experimental import pallas as pl
from jax.experimental.pallas import tpu as pltpu
from jax.sharding import Mesh, PartitionSpec as P

ROPE = 64
NOPE = 128
RANK = 512
VDIM = 128
HG = 16
R = 16
GROUP = 8
ROWS = GROUP * R
ITEMS = HG * ROWS
KEYW = RANK + 128
ITEMW = RANK + 256
SENDW = HG * VDIM + 128
SCALE2 = (NOPE + ROPE) ** -0.5 * 1.4426950408889634
NEG = -1e30
CTX = ("y", "x", "z", "c")
RING = (0, 1, 3, 2)
SWAP = ((0, 1), (1, 0))
MIB = 1 << 20


def shift(d):
    return [(i, (i + d) % 4) for i in range(4)]


def call(kernel, out_shape, vmem=40, **kw):
    return pl.pallas_call(
        kernel,
        out_shape=out_shape,
        compiler_params=pltpu.CompilerParams(vmem_limit_bytes=vmem * MIB),
        cost_estimate=pl.CostEstimate(flops=1, bytes_accessed=1, transcendentals=0),
        **kw,
    )


def nt_dot(a, b):
    return lax.dot_general(a, b, (((1,), (1,)), ((), ())), preferred_element_type=jnp.float32)


HBM = pl.BlockSpec(memory_space=pltpu.HBM)


def in_hbm(*arrays):
    return [pltpu.with_memory_space_constraint(a, pltpu.HBM) for a in arrays]


def pack_keys_kernel(latent_ref, key_rope_ref, pos_ref, key_ref, rope, pos, sems):
    copies = [
        pltpu.make_async_copy(key_rope_ref, rope, sems.at[0]),
        pltpu.make_async_copy(pos_ref, pos, sems.at[1]),
        pltpu.make_async_copy(latent_ref, key_ref.at[:, :RANK], sems.at[2]),
    ]
    for copy in copies:
        copy.start()
    copies[0].wait()
    copies[1].wait()
    where = pos[...].astype(jnp.float32)
    high = jnp.floor(where * (1 / 128))
    row = lax.broadcasted_iota(jnp.int32, rope.shape, 0)
    ext = jnp.where(row == 0, high, jnp.where(row == 1, where - high * 128, 0.0))
    ext = jnp.concatenate([rope[...].astype(jnp.float32), ext], axis=0)
    key_ref[:, RANK:] = jnp.transpose(ext).astype(jnp.bfloat16)
    copies[2].wait()


def pack_keys(latent, k_rope, key_pos):
    return call(
        pack_keys_kernel,
        jax.ShapeDtypeStruct((latent.shape[0], KEYW), jnp.bfloat16),
        vmem=16,
        in_specs=[HBM] * 3,
        scratch_shapes=[
            pltpu.VMEM((k_rope.shape[1], k_rope.shape[0]), jnp.bfloat16),
            pltpu.VMEM(key_pos.shape, jnp.int32),
            pltpu.SemaphoreType.DMA((3,)),
        ],
    )(*in_hbm(latent, jnp.transpose(k_rope), key_pos))


def pack_queries_kernel(query_ref, rope_ref, out_ref, sems):
    copies = [
        pltpu.make_async_copy(query_ref, out_ref.at[:, : HG * NOPE], sems.at[0]),
        pltpu.make_async_copy(rope_ref, out_ref.at[:, HG * NOPE :], sems.at[1]),
    ]
    for copy in copies:
        copy.start()
    for copy in copies:
        copy.wait()


def pack_queries(query, q_rope):
    return call(
        pack_queries_kernel,
        jax.ShapeDtypeStruct((R, HG * (NOPE + ROPE)), jnp.bfloat16),
        vmem=16,
        in_specs=[HBM] * 2,
        scratch_shapes=[pltpu.SemaphoreType.DMA((2,))],
    )(*in_hbm(query, q_rope))


def join_kernel(*refs):
    start = 0
    for ref in refs[:-1]:
        refs[-1][start : start + ref.shape[0]] = ref[...]
        start += ref.shape[0]


def join(parts):
    shape = (sum(part.shape[0] for part in parts), parts[0].shape[1])
    return call(join_kernel, jax.ShapeDtypeStruct(shape, jnp.bfloat16))(*parts)


def absorb_kernel(*refs):
    q_refs, (w_ref, out_ref) = refs[:2], refs[2:]
    lane = lax.broadcasted_iota(jnp.int32, (ROWS, 128), 1)
    row = lax.broadcasted_iota(jnp.int32, (ROWS, 128), 0)
    one_hot = (lane == row).astype(jnp.bfloat16)

    def columns(start):
        return jnp.concatenate([ref[:, start : start + 128] for ref in q_refs], axis=0)

    for h in range(HG):
        rows = slice(h * ROWS, (h + 1) * ROWS)
        latent = jnp.dot(columns(h * NOPE), w_ref[h], preferred_element_type=jnp.float32)
        out_ref[rows, :RANK] = latent.astype(jnp.bfloat16)
        pair = columns(HG * NOPE + (h // 2) * 128).astype(jnp.float32)
        if h % 2:
            pair = pltpu.roll(pair, ROPE, 1)
        rope = jnp.where(lane < ROPE, pair, 0.0)
        out_ref[rows, RANK : RANK + 128] = rope.astype(jnp.bfloat16)
        out_ref[rows, RANK + 128 :] = one_hot


def absorb(queries, w_uk):
    return call(absorb_kernel, jax.ShapeDtypeStruct((ITEMS, ITEMW), jnp.bfloat16))(
        *queries, w_uk
    )


def pack_stats(stats):
    high = stats.astype(jnp.bfloat16).astype(jnp.float32)
    mid = (stats - high).astype(jnp.bfloat16).astype(jnp.float32)
    low = stats - high - mid
    packed = high + pltpu.roll(mid, HG, 1) + pltpu.roll(low, 2 * HG, 1)
    return packed.astype(jnp.bfloat16)


def unpack_stats(packed):
    packed = packed.astype(jnp.float32)
    return packed + pltpu.roll(packed, 128 - HG, 1) + pltpu.roll(packed, 128 - 2 * HG, 1)


def attend_kernel(pieces, last, *refs):
    q_ref, qpos_ref, v_ref = refs[:3]
    piece_refs = refs[3 : 3 + pieces]
    rest = refs[3 + pieces :]
    if last:
        part_in, lse_in, keep_ref, send_ref, key_ref, lse_ref = rest
    else:
        part_out, lse_out, key_ref = rest
    step = pl.program_id(0)

    @pl.when(step == 0)
    def _():
        qpos = qpos_ref[0:1, :]
        start = 0
        for ref in piece_refs:
            rows = slice(start, start + ref.shape[0])
            start += ref.shape[0]
            key_ref[rows, :KEYW] = ref[...]
            ext = ref[:, RANK:].astype(jnp.float32)
            pos = ext[:, ROPE : ROPE + 1] * 128.0 + ext[:, ROPE + 1 : ROPE + 2]
            key_ref[rows, KEYW:] = jnp.where(pos <= qpos, 0.0, NEG).astype(jnp.bfloat16)
        if last:
            lse_ref[...] = jnp.zeros_like(lse_ref)

    tile = q_ref.shape[0]
    scores = nt_dot(q_ref[...], key_ref[...]) * SCALE2
    top = jnp.max(scores, axis=1, keepdims=True)
    weights = jnp.exp2(scores - top)
    total = jnp.sum(weights, axis=1, keepdims=True)
    acc = jnp.dot(
        weights.astype(jnp.bfloat16), key_ref[:, :RANK], preferred_element_type=jnp.float32
    )
    context = (acc * (1.0 / total)).astype(jnp.bfloat16)
    lse = top + jnp.log2(total)
    if last:
        earlier = lse_in[:, 0:1]
        top = jnp.maximum(lse, earlier)
        here, there = jnp.exp2(lse - top), jnp.exp2(earlier - top)
        total = here + there
        lse = top + jnp.log2(total)
        inverse = 1.0 / total
        here, there = here * inverse, there * inverse
    else:
        lse_out[...] = jnp.broadcast_to(lse, lse_out.shape)

    half = ROWS // 2
    lane = lax.broadcasted_iota(jnp.int32, (ROWS, 128), 1)
    for i in range(tile // ROWS):
        rows = slice(i * ROWS, (i + 1) * ROWS)
        head = step * (tile // ROWS) + i
        cols = pl.ds(pl.multiple_of(head * VDIM, VDIM), VDIM)
        out = jnp.dot(context[rows], v_ref[i], preferred_element_type=jnp.float32)
        if last:
            out = out * here[rows] + part_in[:, i * VDIM : (i + 1) * VDIM] * there[rows]
            out = out.astype(jnp.bfloat16)
            keep_ref[:, cols] = out[:half]
            send_ref[:, cols] = out[half:]
            lse_ref[...] = jnp.where(lane == head, lse[rows], lse_ref[...])
        else:
            part_out[:, i * VDIM : (i + 1) * VDIM] = out

    if last:

        @pl.when(step == pl.num_programs(0) - 1)
        def _():
            packed = pack_stats(lse_ref[...])
            keep_ref[:, HG * VDIM :] = packed[:half]
            send_ref[:, HG * VDIM :] = packed[half:]


def attend(q, qpos, value_weight, pieces, earlier=None, tile=512):
    n, keys = len(pieces), sum(piece.shape[0] for piece in pieces)
    last = earlier is not None
    heads = tile // ROWS
    whole = lambda shape: pl.BlockSpec(shape, lambda i: (0, 0))
    part = lambda width: pl.BlockSpec((tile, width), lambda i: (i, 0))
    carried = [pl.BlockSpec((ROWS, heads * VDIM), lambda i: (0, i)), part(128)]
    in_specs = [part(ITEMW), whole((8, 128))]
    in_specs += [pl.BlockSpec((heads, RANK, VDIM), lambda i: (i, 0, 0))]
    in_specs += [whole(piece.shape) for piece in pieces]
    scratch = [pltpu.VMEM((keys, ITEMW), jnp.bfloat16)]
    args = [q, qpos, value_weight, *pieces]
    if last:
        in_specs += carried
        args += earlier
        half = jax.ShapeDtypeStruct((ROWS // 2, SENDW), jnp.bfloat16)
        out_shape, out_specs = (half, half), [whole((ROWS // 2, SENDW))] * 2
        scratch.append(pltpu.VMEM((ROWS, 128), jnp.float32))
    else:
        out_shape = (
            jax.ShapeDtypeStruct((ROWS, HG * VDIM), jnp.float32),
            jax.ShapeDtypeStruct((ITEMS, 128), jnp.float32),
        )
        out_specs = carried
    return call(
        functools.partial(attend_kernel, n, last),
        out_shape,
        grid=(ITEMS // tile,),
        in_specs=in_specs,
        out_specs=out_specs,
        scratch_shapes=scratch,
    )(*args)


def merge(refs):
    stats = [unpack_stats(ref[:, HG * VDIM :]) for ref in refs]
    top = functools.reduce(jnp.maximum, stats)
    weights = [jnp.exp2(s - top) for s in stats]
    total = sum(weights)
    weights = [w / total for w in weights]
    out = []
    for h in range(HG):
        cols = slice(h * VDIM, (h + 1) * VDIM)
        head = sum(
            ref[:, cols].astype(jnp.float32) * w[:, h : h + 1] for ref, w in zip(refs, weights)
        )
        out.append((cols, head.astype(jnp.bfloat16)))
    return out, top + jnp.log2(total)


def merge_core_kernel(a_ref, b_ref, *out_refs):
    heads, lse = merge((a_ref, b_ref))
    lane = lax.broadcasted_iota(jnp.int32, lse.shape, 1)
    packed = pack_stats(jnp.where(lane < HG, lse, 0.0))
    for cols, head in heads + [(slice(HG * VDIM, SENDW), packed)]:
        for i, ref in enumerate(out_refs):
            ref[:, cols] = head[i * R : (i + 1) * R]


def merge_ring_kernel(*refs):
    heads, _ = merge(refs[:-1])
    for cols, head in heads:
        for i in range(refs[-1].shape[0]):
            refs[-1][i, :, cols] = head


def columns_kernel(zc_ref, *refs):
    z, c = zc_ref[0], zc_ref[1]
    w_refs, (out_ref, held, sems) = refs[:4], refs[4:]
    ncol, depth = w_refs[0].shape
    copies = [pltpu.make_async_copy(w_refs[k], held.at[k], sems.at[k]) for k in range(4)]
    for copy in copies:
        copy.start()
    for k in range(4):
        to_z = z if k % 2 == 0 else 1 - z
        to_c = c if k < 2 else 1 - c
        copies[k].wait()
        padded = jnp.concatenate(
            [held[k], jnp.zeros((128 - ncol, depth), jnp.bfloat16)], axis=0
        )
        out_ref[to_z * 2 + to_c] = jnp.transpose(padded)


def columns_of(zc, pieces):
    ncol, depth = pieces[0].shape
    return call(
        columns_kernel,
        jax.ShapeDtypeStruct((4, depth, 128), jnp.bfloat16),
        vmem=16,
        in_specs=[pl.BlockSpec(memory_space=pltpu.SMEM)] + [HBM] * 4,
        scratch_shapes=[
            pltpu.VMEM((4, ncol, depth), jnp.bfloat16),
            pltpu.SemaphoreType.DMA((4,)),
        ],
    )(zc, *in_hbm(pieces[0]), *pieces[1:])


def project_kernel(x_ref, w_ref, out_ref):
    for k in range(4):
        out = jnp.dot(x_ref[...], w_ref[k], preferred_element_type=jnp.float32)
        out_ref[k] = out[:, : out_ref.shape[2]].astype(jnp.bfloat16)


def finish_kernel(sums_ref, out_ref, row_ref):
    ncol = sums_ref.shape[2]
    row_ref[...] = jnp.zeros_like(row_ref)
    for zc in range(4):
        total = sum(sums_ref[zc * 4 + h].astype(jnp.float32) for h in range(4))
        for i in range(4):
            start = (i * 4 + zc) * R
            row_ref[start : start + R, :ncol] = total[i * R : (i + 1) * R]
    out_ref[...] = jnp.transpose(row_ref[...])[:ncol].astype(jnp.bfloat16)


def local(query_unrotated, q_rope, latent, k_rope, key_pos, offset, w_uk, value_up_weight, w_out):
    y, x, z, c = (lax.axis_index(n) for n in CTX)

    keys = pack_keys(latent[0], k_rope[0], key_pos)
    keys, query_unrotated = lax.optimization_barrier((keys, query_unrotated))
    q_own = pack_queries(query_unrotated, q_rope)
    z_keys = lax.ppermute(keys, "z", SWAP)
    near = [keys] + [lax.ppermute(keys, "y", shift(d)) for d in RING[1:]]
    z_keys, near = lax.optimization_barrier((z_keys, near))
    far = [z_keys] + [lax.ppermute(z_keys, "y", shift(d)) for d in RING[1:]]

    q_chip = join([q_own] + [lax.ppermute(q_own, "x", shift(d)) for d in RING[1:]])
    q_chip, w_own = lax.optimization_barrier((q_chip, jnp.transpose(w_out)))
    q_core = lax.ppermute(q_chip, "c", SWAP)
    z_w = lax.ppermute(w_own, "z", SWAP)

    row = jnp.arange(ROWS, dtype=jnp.int32)
    part = row // R
    row_x = (x - jnp.array(RING, jnp.int32)[part % 4]) % 4
    row_c = jnp.where(part < 4, c, 1 - c)
    row = (((y * 4 + row_x) * 2 + z) * 2 + row_c) * R + row % R
    qpos = jnp.broadcast_to((offset[0] + row).astype(jnp.float32)[None, :], (8, ROWS))

    q = absorb((q_chip, q_core), w_uk)
    earlier = attend(q, qpos, value_up_weight, near)
    earlier, far = lax.optimization_barrier((earlier, far))
    keep, send = attend(q, qpos, value_up_weight, far, earlier)

    z_w, send = lax.optimization_barrier((z_w, send))
    parts = call(
        merge_core_kernel, [jax.ShapeDtypeStruct((R, SENDW), jnp.bfloat16)] * 4
    )(keep, lax.ppermute(send, "c", SWAP))
    parts = [parts[0]] + [
        lax.ppermute(part, "x", shift(-d % 4)) for part, d in zip(parts[1:], RING[1:])
    ]
    c_w = lax.ppermute(w_own, "c", SWAP)
    zc_w = lax.ppermute(z_w, "c", SWAP)
    parts, c_w, zc_w = lax.optimization_barrier((parts, c_w, zc_w))
    heads = call(merge_ring_kernel, jax.ShapeDtypeStruct((16, R, HG * VDIM), jnp.bfloat16))(
        *parts
    )

    rows = lax.all_to_all(heads, ("y", "x"), 0, 0, tiled=True).reshape(16 * R, HG * VDIM)
    ncol = w_out.shape[1]
    columns = columns_of(jnp.stack([z, c]), (w_own, z_w, c_w, zc_w))
    sums = call(project_kernel, jax.ShapeDtypeStruct((4, 16 * R, ncol), jnp.bfloat16))(
        rows, columns
    )
    sums = lax.all_to_all(
        sums.reshape(16, 4 * R, ncol), ("z", "c", "head"), 0, 0, tiled=True
    )
    out = call(
        finish_kernel,
        jax.ShapeDtypeStruct((ncol, 16 * R), jnp.bfloat16),
        scratch_shapes=[pltpu.VMEM((16 * R, 128), jnp.float32)],
    )(sums)
    return jnp.transpose(out)


def solution(mesh):
    grid = Mesh(mesh.devices.reshape(4, 4, 2, 2, 4), CTX + ("head",))
    return jax.shard_map(
        local,
        mesh=grid,
        in_specs=(
            P(CTX, "head"),
            P(CTX, "head"),
            P(None, CTX, None),
            P(None, CTX, None),
            P(None, CTX),
            P(),
            P("head", None, None),
            P("head", None, None),
            P("head", CTX),
        ),
        out_specs=P("head", CTX),
        check_vma=False,
    )
```

```python
import functools

import jax
import jax.numpy as jnp
from jax import lax
from jax.experimental import pallas as pl
from jax.experimental.pallas import tpu as pltpu
from jax.sharding import Mesh, PartitionSpec as P

ROPE = 64
NOPE = 128
RANK = 512
VDIM = 128
HG = 16
R = 16
GROUP = 8
ROWS = GROUP * R
ITEMS = HG * ROWS
KEYW = RANK + 128
ITEMW = RANK + 256
SENDW = HG * VDIM + 128
SCALE2 = (NOPE + ROPE) ** -0.5 * 1.4426950408889634
NEG = -1e30
CTX = ("y", "x", "z", "c")
RING = (0, 1, 3, 2)
SWAP = ((0, 1), (1, 0))
MIB = 1 << 20


def shift(d):
    return [(i, (i + d) % 4) for i in range(4)]


def call(kernel, out_shape, vmem=8, **kw):
    return pl.pallas_call(
        kernel,
        out_shape=out_shape,
        compiler_params=pltpu.CompilerParams(vmem_limit_bytes=vmem * MIB),
        cost_estimate=pl.CostEstimate(flops=1, bytes_accessed=1, transcendentals=0),
        **kw,
    )


def nt_dot(a, b):
    return lax.dot_general(a, b, (((1,), (1,)), ((), ())), preferred_element_type=jnp.float32)


HBM = pl.BlockSpec(memory_space=pltpu.HBM)


def in_hbm(*arrays):
    return [pltpu.with_memory_space_constraint(a, pltpu.HBM) for a in arrays]


def pack_kernel(
    latent_ref, key_rope_ref, pos_ref, query_ref, q_rope_ref, key_ref, q_ref, rope, pos, sems
):
    copies = [
        pltpu.make_async_copy(key_rope_ref, rope, sems.at[0]),
        pltpu.make_async_copy(pos_ref, pos, sems.at[1]),
        pltpu.make_async_copy(latent_ref, key_ref.at[:, :RANK], sems.at[2]),
        pltpu.make_async_copy(query_ref, q_ref.at[:, : HG * NOPE], sems.at[3]),
        pltpu.make_async_copy(q_rope_ref, q_ref.at[:, HG * NOPE :], sems.at[4]),
    ]
    for copy in copies:
        copy.start()
    copies[0].wait()
    copies[1].wait()
    where = pos[...].astype(jnp.float32)
    high = jnp.floor(where * (1 / 128))
    row = lax.broadcasted_iota(jnp.int32, rope.shape, 0)
    ext = jnp.where(row == 0, high, jnp.where(row == 1, where - high * 128, 0.0))
    ext = jnp.concatenate([rope[...].astype(jnp.float32), ext], axis=0)
    key_ref[:, RANK:] = jnp.transpose(ext).astype(jnp.bfloat16)
    for copy in copies[2:]:
        copy.wait()


def pack(latent, k_rope, key_pos, query, q_rope):
    return call(
        pack_kernel,
        (
            jax.ShapeDtypeStruct((latent.shape[0], KEYW), jnp.bfloat16),
            jax.ShapeDtypeStruct((R, HG * (NOPE + ROPE)), jnp.bfloat16),
        ),
        in_specs=[HBM] * 5,
        scratch_shapes=[
            pltpu.VMEM((k_rope.shape[1], k_rope.shape[0]), jnp.bfloat16),
            pltpu.VMEM(key_pos.shape, jnp.int32),
            pltpu.SemaphoreType.DMA((5,)),
        ],
    )(*in_hbm(latent, jnp.transpose(k_rope), key_pos, query, q_rope))


def join_kernel(*refs):
    start = 0
    for ref in refs[:-1]:
        refs[-1][start : start + ref.shape[0]] = ref[...]
        start += ref.shape[0]


def join(parts):
    shape = (sum(part.shape[0] for part in parts), parts[0].shape[1])
    return call(join_kernel, jax.ShapeDtypeStruct(shape, jnp.bfloat16))(*parts)


def absorb_kernel(*refs):
    q_refs, (w_hbm, out_ref, w_ref, sems) = refs[:2], refs[2:]
    step = HG // 4
    copies = [
        pltpu.make_async_copy(
            w_hbm.at[i * step : (i + 1) * step],
            w_ref.at[i * step : (i + 1) * step],
            sems.at[i],
        )
        for i in range(4)
    ]
    for copy in copies:
        copy.start()
    lane = lax.broadcasted_iota(jnp.int32, (ROWS, 128), 1)
    row = lax.broadcasted_iota(jnp.int32, (ROWS, 128), 0)
    one_hot = (lane == row).astype(jnp.bfloat16)

    def columns(start):
        return jnp.concatenate([ref[:, start : start + 128] for ref in q_refs], axis=0)

    for h in range(HG):
        if h % step == 0:
            copies[h // step].wait()
        rows = slice(h * ROWS, (h + 1) * ROWS)
        latent = jnp.dot(columns(h * NOPE), w_ref[h], preferred_element_type=jnp.float32)
        out_ref[rows, :RANK] = latent.astype(jnp.bfloat16)
        pair = columns(HG * NOPE + (h // 2) * 128).astype(jnp.float32)
        if h % 2:
            pair = pltpu.roll(pair, ROPE, 1)
        rope = jnp.where(lane < ROPE, pair, 0.0)
        out_ref[rows, RANK : RANK + 128] = rope.astype(jnp.bfloat16)
        out_ref[rows, RANK + 128 :] = one_hot


def absorb(queries, w_uk):
    return call(
        absorb_kernel,
        jax.ShapeDtypeStruct((ITEMS, ITEMW), jnp.bfloat16),
        vmem=16,
        in_specs=[pl.BlockSpec(memory_space=pltpu.VMEM)] * 2 + [HBM],
        scratch_shapes=[
            pltpu.VMEM(w_uk.shape, jnp.bfloat16),
            pltpu.SemaphoreType.DMA((4,)),
        ],
    )(*queries, *in_hbm(w_uk))


def pack_stats(stats):
    high = stats.astype(jnp.bfloat16).astype(jnp.float32)
    mid = (stats - high).astype(jnp.bfloat16).astype(jnp.float32)
    low = stats - high - mid
    packed = high + pltpu.roll(mid, HG, 1) + pltpu.roll(low, 2 * HG, 1)
    return packed.astype(jnp.bfloat16)


def unpack_stats(packed):
    packed = packed.astype(jnp.float32)
    return packed + pltpu.roll(packed, 128 - HG, 1) + pltpu.roll(packed, 128 - 2 * HG, 1)


def attend_kernel(pieces, last, *refs):
    q_ref, qpos_ref, v_ref = refs[:3]
    piece_refs = refs[3 : 3 + pieces]
    rest = refs[3 + pieces :]
    if last:
        part_in, lse_in, keep_ref, send_ref, key_ref, lse_ref = rest
    else:
        part_out, lse_out, key_ref = rest
    step = pl.program_id(0)

    @pl.when(step == 0)
    def _():
        qpos = qpos_ref[0:1, :]
        start = 0
        for ref in piece_refs:
            rows = slice(start, start + ref.shape[0])
            start += ref.shape[0]
            key_ref[rows, :KEYW] = ref[...]
            ext = ref[:, RANK:].astype(jnp.float32)
            pos = ext[:, ROPE : ROPE + 1] * 128.0 + ext[:, ROPE + 1 : ROPE + 2]
            key_ref[rows, KEYW:] = jnp.where(pos <= qpos, 0.0, NEG).astype(jnp.bfloat16)
        if last:
            lse_ref[...] = jnp.zeros_like(lse_ref)

    tile = q_ref.shape[0]
    scores = nt_dot(q_ref[...], key_ref[...]) * SCALE2
    top = jnp.max(scores, axis=1, keepdims=True)
    weights = jnp.exp2(scores - top)
    total = jnp.sum(weights, axis=1, keepdims=True)
    acc = jnp.dot(
        weights.astype(jnp.bfloat16), key_ref[:, :RANK], preferred_element_type=jnp.float32
    )
    context = (acc * (1.0 / total)).astype(jnp.bfloat16)
    lse = top + jnp.log2(total)
    if last:
        earlier = lse_in[:, 0:1]
        top = jnp.maximum(lse, earlier)
        here, there = jnp.exp2(lse - top), jnp.exp2(earlier - top)
        total = here + there
        lse = top + jnp.log2(total)
        inverse = 1.0 / total
        here, there = here * inverse, there * inverse
    else:
        lse_out[...] = jnp.broadcast_to(lse, lse_out.shape)

    half = ROWS // 2
    lane = lax.broadcasted_iota(jnp.int32, (ROWS, 128), 1)
    for i in range(tile // ROWS):
        rows = slice(i * ROWS, (i + 1) * ROWS)
        head = step * (tile // ROWS) + i
        cols = pl.ds(pl.multiple_of(head * VDIM, VDIM), VDIM)
        out = jnp.dot(context[rows], v_ref[i], preferred_element_type=jnp.float32)
        if last:
            out = out * here[rows] + part_in[:, i * VDIM : (i + 1) * VDIM] * there[rows]
            out = out.astype(jnp.bfloat16)
            keep_ref[:, cols] = out[:half]
            send_ref[:, cols] = out[half:]
            lse_ref[...] = jnp.where(lane == head, lse[rows], lse_ref[...])
        else:
            part_out[:, i * VDIM : (i + 1) * VDIM] = out

    if last:

        @pl.when(step == pl.num_programs(0) - 1)
        def _():
            packed = pack_stats(lse_ref[...])
            keep_ref[:, HG * VDIM :] = packed[:half]
            send_ref[:, HG * VDIM :] = packed[half:]


def attend(q, qpos, value_weight, pieces, earlier=None, tile=512):
    n, keys = len(pieces), sum(piece.shape[0] for piece in pieces)
    last = earlier is not None
    heads = tile // ROWS
    whole = lambda shape: pl.BlockSpec(shape, lambda i: (0, 0))
    part = lambda width: pl.BlockSpec((tile, width), lambda i: (i, 0))
    carried = [pl.BlockSpec((ROWS, heads * VDIM), lambda i: (0, i)), part(128)]
    in_specs = [part(ITEMW), whole((8, 128))]
    in_specs += [pl.BlockSpec((heads, RANK, VDIM), lambda i: (i, 0, 0))]
    in_specs += [whole(piece.shape) for piece in pieces]
    scratch = [pltpu.VMEM((keys, ITEMW), jnp.bfloat16)]
    args = [q, qpos, value_weight, *pieces]
    if last:
        in_specs += carried
        args += earlier
        half = jax.ShapeDtypeStruct((ROWS // 2, SENDW), jnp.bfloat16)
        out_shape, out_specs = (half, half), [whole((ROWS // 2, SENDW))] * 2
        scratch.append(pltpu.VMEM((ROWS, 128), jnp.float32))
    else:
        out_shape = (
            jax.ShapeDtypeStruct((ROWS, HG * VDIM), jnp.float32),
            jax.ShapeDtypeStruct((ITEMS, 128), jnp.float32),
        )
        out_specs = carried
    return call(
        functools.partial(attend_kernel, n, last),
        out_shape,
        vmem=32,
        grid=(ITEMS // tile,),
        in_specs=in_specs,
        out_specs=out_specs,
        scratch_shapes=scratch,
    )(*args)


def merge(refs):
    stats = [unpack_stats(ref[:, HG * VDIM :]) for ref in refs]
    top = functools.reduce(jnp.maximum, stats)
    weights = [jnp.exp2(s - top) for s in stats]
    total = sum(weights)
    weights = [w / total for w in weights]
    out = []
    for h in range(HG):
        cols = slice(h * VDIM, (h + 1) * VDIM)
        head = sum(
            ref[:, cols].astype(jnp.float32) * w[:, h : h + 1] for ref, w in zip(refs, weights)
        )
        out.append((cols, head.astype(jnp.bfloat16)))
    return out, top + jnp.log2(total)


def merge_core_kernel(a_ref, b_ref, *out_refs):
    heads, lse = merge((a_ref, b_ref))
    lane = lax.broadcasted_iota(jnp.int32, lse.shape, 1)
    packed = pack_stats(jnp.where(lane < HG, lse, 0.0))
    for cols, head in heads + [(slice(HG * VDIM, SENDW), packed)]:
        for i, ref in enumerate(out_refs):
            ref[:, cols] = head[i * R : (i + 1) * R]


def merge_ring_kernel(*refs):
    heads, _ = merge(refs[:-1])
    for cols, head in heads:
        for i in range(refs[-1].shape[0]):
            refs[-1][i, :, cols] = head


def columns_kernel(zc_ref, *refs):
    z, c = zc_ref[0], zc_ref[1]
    w_refs, (out_ref, held, sems) = refs[:4], refs[4:]
    ncol, depth = w_refs[0].shape
    copies = [pltpu.make_async_copy(w_refs[k], held.at[k], sems.at[k]) for k in range(4)]
    for copy in copies:
        copy.start()
    for k in range(4):
        to_z = z if k % 2 == 0 else 1 - z
        to_c = c if k < 2 else 1 - c
        copies[k].wait()
        padded = jnp.concatenate(
            [held[k], jnp.zeros((128 - ncol, depth), jnp.bfloat16)], axis=0
        )
        out_ref[to_z * 2 + to_c] = jnp.transpose(padded)


def columns_of(zc, pieces):
    ncol, depth = pieces[0].shape
    return call(
        columns_kernel,
        jax.ShapeDtypeStruct((4, depth, 128), jnp.bfloat16),
        vmem=16,
        in_specs=[pl.BlockSpec(memory_space=pltpu.SMEM)] + [HBM] * 4,
        scratch_shapes=[
            pltpu.VMEM((4, ncol, depth), jnp.bfloat16),
            pltpu.SemaphoreType.DMA((4,)),
        ],
    )(zc, *in_hbm(pieces[0]), *pieces[1:])


def project_kernel(x_ref, w_ref, out_ref):
    for k in range(4):
        out = jnp.dot(x_ref[...], w_ref[k], preferred_element_type=jnp.float32)
        out_ref[k] = out[:, : out_ref.shape[2]].astype(jnp.bfloat16)


def finish_kernel(sums_ref, out_ref, row_ref):
    ncol = sums_ref.shape[2]
    row_ref[...] = jnp.zeros_like(row_ref)
    for zc in range(4):
        total = sum(sums_ref[zc * 4 + h].astype(jnp.float32) for h in range(4))
        for i in range(4):
            start = (i * 4 + zc) * R
            row_ref[start : start + R, :ncol] = total[i * R : (i + 1) * R]
    out_ref[...] = jnp.transpose(row_ref[...])[:ncol].astype(jnp.bfloat16)


def local(query_unrotated, q_rope, latent, k_rope, key_pos, offset, w_uk, value_up_weight, w_out):
    y, x, z, c = (lax.axis_index(n) for n in CTX)

    keys, q_own = pack(latent[0], k_rope[0], key_pos, query_unrotated, q_rope)
    z_keys = lax.ppermute(keys, "z", SWAP)
    up, down, across = (lax.ppermute(keys, "y", shift(d)) for d in (1, 3, 2))
    q_ring = [lax.ppermute(q_own, "x", shift(1)), lax.ppermute(q_own, "x", shift(3))]
    q_ring, q_own, w_own = lax.optimization_barrier((q_ring, q_own, jnp.transpose(w_out)))
    q_ring.append(lax.ppermute(q_own, "x", shift(2)))
    z_keys, up, down, across, q_ring[0] = lax.optimization_barrier((z_keys, up, down, across, q_ring[0]))
    near = [keys, z_keys, up, down, across]
    far = [lax.ppermute(z_keys, "y", shift(d)) for d in RING[1:]]
    q_chip = join([q_own, *q_ring])
    q_core = lax.ppermute(q_chip, "c", SWAP)
    z_w = lax.ppermute(w_own, "z", SWAP)

    row = jnp.arange(ROWS, dtype=jnp.int32)
    part = row // R
    row_x = (x - jnp.array(RING, jnp.int32)[part % 4]) % 4
    row_c = jnp.where(part < 4, c, 1 - c)
    row = (((y * 4 + row_x) * 2 + z) * 2 + row_c) * R + row % R
    qpos = jnp.broadcast_to((offset[0] + row).astype(jnp.float32)[None, :], (8, ROWS))

    q = absorb((q_chip, q_core), w_uk)
    earlier = attend(q, qpos, value_up_weight, near)
    earlier, far = lax.optimization_barrier((earlier, far))
    keep, send = attend(q, qpos, value_up_weight, far, earlier)

    z_w, send = lax.optimization_barrier((z_w, send))
    parts = call(
        merge_core_kernel, [jax.ShapeDtypeStruct((R, SENDW), jnp.bfloat16)] * 4
    )(keep, lax.ppermute(send, "c", SWAP))
    parts = [parts[0]] + [
        lax.ppermute(part, "x", shift(-d % 4)) for part, d in zip(parts[1:], RING[1:])
    ]
    c_w = lax.ppermute(w_own, "c", SWAP)
    zc_w = lax.ppermute(z_w, "c", SWAP)
    parts, c_w = lax.optimization_barrier((parts, c_w))
    heads = call(merge_ring_kernel, jax.ShapeDtypeStruct((16, R, HG * VDIM), jnp.bfloat16))(
        *parts
    )

    rows = lax.all_to_all(heads, ("y", "x"), 0, 0, tiled=True).reshape(16 * R, HG * VDIM)
    ncol = w_out.shape[1]
    columns = columns_of(jnp.stack([z, c]), (w_own, z_w, c_w, zc_w))
    sums = call(
        project_kernel, jax.ShapeDtypeStruct((4, 16 * R, ncol), jnp.bfloat16), vmem=16
    )(rows, columns)
    sums = lax.all_to_all(
        sums.reshape(16, 4 * R, ncol), ("z", "c", "head"), 0, 0, tiled=True
    )
    out = call(
        finish_kernel,
        jax.ShapeDtypeStruct((ncol, 16 * R), jnp.bfloat16),
        scratch_shapes=[pltpu.VMEM((16 * R, 128), jnp.float32)],
    )(sums)
    return jnp.transpose(out)


def solution(mesh):
    grid = Mesh(mesh.devices.reshape(4, 4, 2, 2, 4), CTX + ("head",))
    return jax.shard_map(
        local,
        mesh=grid,
        in_specs=(
            P(CTX, "head"),
            P(CTX, "head"),
            P(None, CTX, None),
            P(None, CTX, None),
            P(None, CTX),
            P(),
            P("head", None, None),
            P("head", None, None),
            P("head", CTX),
        ),
        out_specs=P("head", CTX),
        check_vma=False,
    )
```

```python
import functools

import jax
import jax.numpy as jnp
from jax import lax
from jax.experimental import pallas as pl
from jax.experimental.pallas import tpu as pltpu
from jax.sharding import Mesh, PartitionSpec as P

ROPE = 64
NOPE = 128
RANK = 512
VDIM = 128
HG = 16
R = 16
GROUP = 8
ROWS = GROUP * R
ITEMS = HG * ROWS
KEYW = RANK + 128
ITEMW = RANK + 256
SENDW = HG * VDIM + 128
SCALE2 = (NOPE + ROPE) ** -0.5 * 1.4426950408889634
NEG = -1e30
CTX = ("y", "x", "z", "c")
RING = (0, 1, 3, 2)
SWAP = ((0, 1), (1, 0))
MIB = 1 << 20


def shift(d):
    return [(i, (i + d) % 4) for i in range(4)]


def call(kernel, out_shape, vmem=8, **kw):
    return pl.pallas_call(
        kernel,
        out_shape=out_shape,
        compiler_params=pltpu.CompilerParams(vmem_limit_bytes=vmem * MIB),
        cost_estimate=pl.CostEstimate(flops=1, bytes_accessed=1, transcendentals=0),
        **kw,
    )


def nt_dot(a, b):
    return lax.dot_general(a, b, (((1,), (1,)), ((), ())), preferred_element_type=jnp.float32)


HBM = pl.BlockSpec(memory_space=pltpu.HBM)


def in_hbm(*arrays):
    return [pltpu.with_memory_space_constraint(a, pltpu.HBM) for a in arrays]


def pack_kernel(
    latent_ref, key_rope_ref, pos_ref, query_ref, q_rope_ref, key_ref, q_ref, rope, pos, sems
):
    copies = [
        pltpu.make_async_copy(key_rope_ref, rope, sems.at[0]),
        pltpu.make_async_copy(pos_ref, pos, sems.at[1]),
        pltpu.make_async_copy(latent_ref, key_ref.at[:, :RANK], sems.at[2]),
        pltpu.make_async_copy(query_ref, q_ref.at[:, : HG * NOPE], sems.at[3]),
        pltpu.make_async_copy(q_rope_ref, q_ref.at[:, HG * NOPE :], sems.at[4]),
    ]
    for copy in copies:
        copy.start()
    copies[0].wait()
    copies[1].wait()
    where = pos[...].astype(jnp.float32)
    high = jnp.floor(where * (1 / 128))
    row = lax.broadcasted_iota(jnp.int32, rope.shape, 0)
    ext = jnp.where(row == 0, high, jnp.where(row == 1, where - high * 128, 0.0))
    ext = jnp.concatenate([rope[...].astype(jnp.float32), ext], axis=0)
    key_ref[:, RANK:] = jnp.transpose(ext).astype(jnp.bfloat16)
    for copy in copies[2:]:
        copy.wait()


def pack(latent, k_rope, key_pos, query, q_rope):
    return call(
        pack_kernel,
        (
            jax.ShapeDtypeStruct((latent.shape[0], KEYW), jnp.bfloat16),
            jax.ShapeDtypeStruct((R, HG * (NOPE + ROPE)), jnp.bfloat16),
        ),
        in_specs=[HBM] * 5,
        scratch_shapes=[
            pltpu.VMEM((k_rope.shape[1], k_rope.shape[0]), jnp.bfloat16),
            pltpu.VMEM(key_pos.shape, jnp.int32),
            pltpu.SemaphoreType.DMA((5,)),
        ],
    )(*in_hbm(latent, jnp.transpose(k_rope), key_pos, query, q_rope))


def join_kernel(*refs):
    start = 0
    for ref in refs[:-1]:
        refs[-1][start : start + ref.shape[0]] = ref[...]
        start += ref.shape[0]


def join(parts):
    shape = (sum(part.shape[0] for part in parts), parts[0].shape[1])
    return call(join_kernel, jax.ShapeDtypeStruct(shape, jnp.bfloat16))(*parts)


def absorb_kernel(*refs):
    q_refs, (w_hbm, out_ref, w_ref, sems) = refs[:2], refs[2:]
    step = HG // 4
    copies = [
        pltpu.make_async_copy(
            w_hbm.at[i * step : (i + 1) * step],
            w_ref.at[i * step : (i + 1) * step],
            sems.at[i],
        )
        for i in range(4)
    ]
    for copy in copies:
        copy.start()
    lane = lax.broadcasted_iota(jnp.int32, (ROWS, 128), 1)
    row = lax.broadcasted_iota(jnp.int32, (ROWS, 128), 0)
    one_hot = (lane == row).astype(jnp.bfloat16)

    def columns(start):
        return jnp.concatenate([ref[:, start : start + 128] for ref in q_refs], axis=0)

    for h in range(HG):
        if h % step == 0:
            copies[h // step].wait()
        rows = slice(h * ROWS, (h + 1) * ROWS)
        latent = jnp.dot(columns(h * NOPE), w_ref[h], preferred_element_type=jnp.float32)
        out_ref[rows, :RANK] = latent.astype(jnp.bfloat16)
        pair = columns(HG * NOPE + (h // 2) * 128).astype(jnp.float32)
        if h % 2:
            pair = pltpu.roll(pair, ROPE, 1)
        rope = jnp.where(lane < ROPE, pair, 0.0)
        out_ref[rows, RANK : RANK + 128] = rope.astype(jnp.bfloat16)
        out_ref[rows, RANK + 128 :] = one_hot


def absorb(queries, w_uk):
    return call(
        absorb_kernel,
        jax.ShapeDtypeStruct((ITEMS, ITEMW), jnp.bfloat16),
        vmem=16,
        in_specs=[pl.BlockSpec(memory_space=pltpu.VMEM)] * 2 + [HBM],
        scratch_shapes=[
            pltpu.VMEM(w_uk.shape, jnp.bfloat16),
            pltpu.SemaphoreType.DMA((4,)),
        ],
    )(*queries, *in_hbm(w_uk))


def pack_stats(stats):
    high = stats.astype(jnp.bfloat16).astype(jnp.float32)
    mid = (stats - high).astype(jnp.bfloat16).astype(jnp.float32)
    low = stats - high - mid
    packed = high + pltpu.roll(mid, HG, 1) + pltpu.roll(low, 2 * HG, 1)
    return packed.astype(jnp.bfloat16)


def unpack_stats(packed):
    packed = packed.astype(jnp.float32)
    return packed + pltpu.roll(packed, 128 - HG, 1) + pltpu.roll(packed, 128 - 2 * HG, 1)


def attend_kernel(pieces, last, tile, unroll, *refs):
    q_ref, qpos_ref, v_ref = refs[:3]
    piece_refs = refs[3 : 3 + pieces]
    rest = refs[3 + pieces :]
    if last:
        part_in, lse_in, keep_ref, send_ref, key_ref, lse_ref = rest
        lse_ref[...] = jnp.zeros_like(lse_ref)
    else:
        part_out, lse_out, key_ref = rest

    qpos = qpos_ref[0:1, :]
    start = 0
    for ref in piece_refs:
        rows = slice(start, start + ref.shape[0])
        start += ref.shape[0]
        key_ref[rows, :KEYW] = ref[...]
        ext = ref[:, RANK:].astype(jnp.float32)
        pos = ext[:, ROPE : ROPE + 1] * 128.0 + ext[:, ROPE + 1 : ROPE + 2]
        key_ref[rows, KEYW:] = jnp.where(pos <= qpos, 0.0, NEG).astype(jnp.bfloat16)

    half = ROWS // 2
    heads = tile // ROWS

    def body(step):
        items = pl.ds(pl.multiple_of(step * tile, tile), tile)
        scores = nt_dot(q_ref[items, :], key_ref[...]) * SCALE2
        top = jnp.max(scores, axis=1, keepdims=True)
        weights = jnp.exp2(scores - top)
        total = jnp.sum(weights, axis=1, keepdims=True)
        acc = jnp.dot(
            weights.astype(jnp.bfloat16), key_ref[:, :RANK], preferred_element_type=jnp.float32
        )
        context = (acc * (1.0 / total)).astype(jnp.bfloat16)
        lse = top + jnp.log2(total)
        if last:
            earlier = lse_in[items, 0:1]
            top = jnp.maximum(lse, earlier)
            here, there = jnp.exp2(lse - top), jnp.exp2(earlier - top)
            total = here + there
            lse = top + jnp.log2(total)
            inverse = 1.0 / total
            here, there = here * inverse, there * inverse
        else:
            lse_out[items, :] = jnp.broadcast_to(lse, (tile, 128))

        lane = lax.broadcasted_iota(jnp.int32, (ROWS, 128), 1)
        for i in range(heads):
            rows = slice(i * ROWS, (i + 1) * ROWS)
            head = step * heads + i
            cols = pl.ds(pl.multiple_of(head * VDIM, VDIM), VDIM)
            out = jnp.dot(context[rows], v_ref[head], preferred_element_type=jnp.float32)
            if last:
                out = out * here[rows] + part_in[:, cols] * there[rows]
                out = out.astype(jnp.bfloat16)
                keep_ref[:, cols] = out[:half]
                send_ref[:, cols] = out[half:]
                lse_ref[...] = jnp.where(lane == head, lse[rows], lse_ref[...])
            else:
                part_out[:, cols] = out

    pl.loop(0, ITEMS // tile, unroll=unroll)(body)

    if last:
        packed = pack_stats(lse_ref[...])
        keep_ref[:, HG * VDIM :] = packed[:half]
        send_ref[:, HG * VDIM :] = packed[half:]


def attend(q, qpos, value_weight, pieces, earlier=None, tile=512, unroll=4):
    n, keys = len(pieces), sum(piece.shape[0] for piece in pieces)
    last = earlier is not None
    scratch = [pltpu.VMEM((keys, ITEMW), jnp.bfloat16)]
    if last:
        half = jax.ShapeDtypeStruct((ROWS // 2, SENDW), jnp.bfloat16)
        out_shape = (half, half)
        scratch.append(pltpu.VMEM((ROWS, 128), jnp.float32))
    else:
        out_shape = (
            jax.ShapeDtypeStruct((ROWS, HG * VDIM), jnp.float32),
            jax.ShapeDtypeStruct((ITEMS, 128), jnp.float32),
        )
    return call(
        functools.partial(attend_kernel, n, last, tile, unroll),
        out_shape,
        vmem=36,
        scratch_shapes=scratch,
    )(q, qpos, value_weight, *pieces, *(earlier or ()))


def merge(refs):
    stats = [unpack_stats(ref[:, HG * VDIM :]) for ref in refs]
    top = functools.reduce(jnp.maximum, stats)
    weights = [jnp.exp2(s - top) for s in stats]
    total = sum(weights)
    weights = [w / total for w in weights]
    out = []
    for h in range(HG):
        cols = slice(h * VDIM, (h + 1) * VDIM)
        head = sum(
            ref[:, cols].astype(jnp.float32) * w[:, h : h + 1] for ref, w in zip(refs, weights)
        )
        out.append((cols, head.astype(jnp.bfloat16)))
    return out, top + jnp.log2(total)


def merge_core_kernel(a_ref, b_ref, *out_refs):
    heads, lse = merge((a_ref, b_ref))
    lane = lax.broadcasted_iota(jnp.int32, lse.shape, 1)
    packed = pack_stats(jnp.where(lane < HG, lse, 0.0))
    for cols, head in heads + [(slice(HG * VDIM, SENDW), packed)]:
        for i, ref in enumerate(out_refs):
            ref[:, cols] = head[i * R : (i + 1) * R]


def merge_ring_kernel(*refs):
    heads, _ = merge(refs[:-1])
    for cols, head in heads:
        for i in range(refs[-1].shape[0]):
            refs[-1][i, :, cols] = head


def columns_kernel(zc_ref, *refs):
    z, c = zc_ref[0], zc_ref[1]
    w_refs, (out_ref, held, sems) = refs[:4], refs[4:]
    ncol, depth = w_refs[0].shape
    copies = [pltpu.make_async_copy(w_refs[k], held.at[k], sems.at[k]) for k in range(4)]
    for copy in copies:
        copy.start()
    for k in range(4):
        to_z = z if k % 2 == 0 else 1 - z
        to_c = c if k < 2 else 1 - c
        copies[k].wait()
        padded = jnp.concatenate(
            [held[k], jnp.zeros((128 - ncol, depth), jnp.bfloat16)], axis=0
        )
        out_ref[to_z * 2 + to_c] = jnp.transpose(padded)


def columns_of(zc, pieces):
    ncol, depth = pieces[0].shape
    return call(
        columns_kernel,
        jax.ShapeDtypeStruct((4, depth, 128), jnp.bfloat16),
        vmem=16,
        in_specs=[pl.BlockSpec(memory_space=pltpu.SMEM)] + [HBM] * 4,
        scratch_shapes=[
            pltpu.VMEM((4, ncol, depth), jnp.bfloat16),
            pltpu.SemaphoreType.DMA((4,)),
        ],
    )(zc, *in_hbm(pieces[0]), *pieces[1:])


def project_kernel(x_ref, w_ref, out_ref):
    for k in range(4):
        out = jnp.dot(x_ref[...], w_ref[k], preferred_element_type=jnp.float32)
        out_ref[k] = out[:, : out_ref.shape[2]].astype(jnp.bfloat16)


def finish_kernel(sums_ref, out_ref, row_ref):
    ncol = sums_ref.shape[2]
    row_ref[...] = jnp.zeros_like(row_ref)
    for zc in range(4):
        total = sum(sums_ref[zc * 4 + h].astype(jnp.float32) for h in range(4))
        for i in range(4):
            start = (i * 4 + zc) * R
            row_ref[start : start + R, :ncol] = total[i * R : (i + 1) * R]
    out_ref[...] = jnp.transpose(row_ref[...])[:ncol].astype(jnp.bfloat16)


def local(query_unrotated, q_rope, latent, k_rope, key_pos, offset, w_uk, value_up_weight, w_out):
    y, x, z, c = (lax.axis_index(n) for n in CTX)

    keys, q_own = pack(latent[0], k_rope[0], key_pos, query_unrotated, q_rope)
    z_keys = lax.ppermute(keys, "z", SWAP)
    up, down, across = (lax.ppermute(keys, "y", shift(d)) for d in (1, 3, 2))
    q_ring = [lax.ppermute(q_own, "x", shift(1)), lax.ppermute(q_own, "x", shift(3))]
    q_ring, q_own = lax.optimization_barrier((q_ring, q_own))
    q_ring.append(lax.ppermute(q_own, "x", shift(2)))
    z_keys, up, down, across = lax.optimization_barrier((z_keys, up, down, across))
    near = [keys, up, down, across]
    far = [z_keys] + [lax.ppermute(z_keys, "y", shift(d)) for d in RING[1:]]
    q_chip, w_own = lax.optimization_barrier((join([q_own, *q_ring]), jnp.transpose(w_out)))
    q_core = lax.ppermute(q_chip, "c", SWAP)
    z_w = lax.ppermute(w_own, "z", SWAP)

    row = jnp.arange(ROWS, dtype=jnp.int32)
    part = row // R
    row_x = (x - jnp.array(RING, jnp.int32)[part % 4]) % 4
    row_c = jnp.where(part < 4, c, 1 - c)
    row = (((y * 4 + row_x) * 2 + z) * 2 + row_c) * R + row % R
    qpos = jnp.broadcast_to((offset[0] + row).astype(jnp.float32)[None, :], (8, ROWS))

    q = absorb((q_chip, q_core), w_uk)
    earlier = attend(q, qpos, value_up_weight, near)
    earlier, far = lax.optimization_barrier((earlier, far))
    keep, send = attend(q, qpos, value_up_weight, far, earlier)

    z_w, send = lax.optimization_barrier((z_w, send))
    parts = call(
        merge_core_kernel, [jax.ShapeDtypeStruct((R, SENDW), jnp.bfloat16)] * 4
    )(keep, lax.ppermute(send, "c", SWAP))
    parts = [parts[0]] + [
        lax.ppermute(part, "x", shift(-d % 4)) for part, d in zip(parts[1:], RING[1:])
    ]
    c_w = lax.ppermute(w_own, "c", SWAP)
    zc_w = lax.ppermute(z_w, "c", SWAP)
    parts, c_w = lax.optimization_barrier((parts, c_w))
    heads = call(merge_ring_kernel, jax.ShapeDtypeStruct((16, R, HG * VDIM), jnp.bfloat16))(
        *parts
    )

    rows = lax.all_to_all(heads, ("y", "x"), 0, 0, tiled=True).reshape(16 * R, HG * VDIM)
    ncol = w_out.shape[1]
    columns = columns_of(jnp.stack([z, c]), (w_own, z_w, c_w, zc_w))
    sums = call(
        project_kernel, jax.ShapeDtypeStruct((4, 16 * R, ncol), jnp.bfloat16), vmem=16
    )(rows, columns)
    sums = lax.all_to_all(
        sums.reshape(16, 4 * R, ncol), ("z", "c", "head"), 0, 0, tiled=True
    )
    out = call(
        finish_kernel,
        jax.ShapeDtypeStruct((ncol, 16 * R), jnp.bfloat16),
        scratch_shapes=[pltpu.VMEM((16 * R, 128), jnp.float32)],
    )(sums)
    return jnp.transpose(out)


def solution(mesh):
    grid = Mesh(mesh.devices.reshape(4, 4, 2, 2, 4), CTX + ("head",))
    return jax.shard_map(
        local,
        mesh=grid,
        in_specs=(
            P(CTX, "head"),
            P(CTX, "head"),
            P(None, CTX, None),
            P(None, CTX, None),
            P(None, CTX),
            P(),
            P("head", None, None),
            P("head", None, None),
            P("head", CTX),
        ),
        out_specs=P("head", CTX),
        check_vma=False,
    )
```

```python
import functools

import jax
import jax.numpy as jnp
from jax import lax
from jax.experimental import pallas as pl
from jax.experimental.pallas import tpu as pltpu
from jax.sharding import Mesh, PartitionSpec as P

ROPE = 64
NOPE = 128
RANK = 512
VDIM = 128
HG = 16
R = 16
GROUP = 8
ROWS = GROUP * R
ITEMS = HG * ROWS
KEYW = RANK + 128
ITEMW = RANK + 256
SENDW = HG * VDIM + 128
SCALE2 = (NOPE + ROPE) ** -0.5 * 1.4426950408889634
NEG = -1e30
CTX = ("y", "x", "z", "c")
RING = (0, 1, 3, 2)
SWAP = ((0, 1), (1, 0))
MIB = 1 << 20


def shift(d):
    return [(i, (i + d) % 4) for i in range(4)]


def call(kernel, out_shape, vmem=8, **kw):
    return pl.pallas_call(
        kernel,
        out_shape=out_shape,
        compiler_params=pltpu.CompilerParams(vmem_limit_bytes=vmem * MIB),
        cost_estimate=pl.CostEstimate(flops=1, bytes_accessed=1, transcendentals=0),
        **kw,
    )


def nt_dot(a, b):
    return lax.dot_general(a, b, (((1,), (1,)), ((), ())), preferred_element_type=jnp.float32)


HBM = pl.BlockSpec(memory_space=pltpu.HBM)


def in_hbm(*arrays):
    return [pltpu.with_memory_space_constraint(a, pltpu.HBM) for a in arrays]


def pack_kernel(
    latent_ref, key_rope_ref, pos_ref, query_ref, q_rope_ref, key_ref, q_ref, rope, pos, sems
):
    copies = [
        pltpu.make_async_copy(key_rope_ref, rope, sems.at[0]),
        pltpu.make_async_copy(pos_ref, pos, sems.at[1]),
        pltpu.make_async_copy(latent_ref, key_ref.at[:, :RANK], sems.at[2]),
        pltpu.make_async_copy(query_ref, q_ref.at[:, : HG * NOPE], sems.at[3]),
        pltpu.make_async_copy(q_rope_ref, q_ref.at[:, HG * NOPE :], sems.at[4]),
    ]
    for copy in copies:
        copy.start()
    copies[0].wait()
    copies[1].wait()
    where = pos[...].astype(jnp.float32)
    high = jnp.floor(where * (1 / 128))
    row = lax.broadcasted_iota(jnp.int32, rope.shape, 0)
    ext = jnp.where(row == 0, high, jnp.where(row == 1, where - high * 128, 0.0))
    ext = jnp.concatenate([rope[...].astype(jnp.float32), ext], axis=0)
    key_ref[:, RANK:] = jnp.transpose(ext).astype(jnp.bfloat16)
    for copy in copies[2:]:
        copy.wait()


def pack(latent, k_rope, key_pos, query, q_rope):
    return call(
        pack_kernel,
        (
            jax.ShapeDtypeStruct((latent.shape[0], KEYW), jnp.bfloat16),
            jax.ShapeDtypeStruct((R, HG * (NOPE + ROPE)), jnp.bfloat16),
        ),
        in_specs=[HBM] * 5,
        scratch_shapes=[
            pltpu.VMEM((k_rope.shape[1], k_rope.shape[0]), jnp.bfloat16),
            pltpu.VMEM(key_pos.shape, jnp.int32),
            pltpu.SemaphoreType.DMA((5,)),
        ],
    )(*in_hbm(latent, jnp.transpose(k_rope), key_pos, query, q_rope))


def join_kernel(*refs):
    parts, (w_hbm, out_ref, w_ref, sem) = refs[:4], refs[4:]
    copy = pltpu.make_async_copy(w_hbm, w_ref, sem)
    copy.start()
    for i, ref in enumerate(parts):
        out_ref[i * R : (i + 1) * R] = ref[...]
    copy.wait()


def join(parts, w_uk):
    return call(
        join_kernel,
        (
            jax.ShapeDtypeStruct((4 * R, parts[0].shape[1]), jnp.bfloat16),
            jax.ShapeDtypeStruct(w_uk.shape, jnp.bfloat16),
        ),
        in_specs=[pl.BlockSpec(memory_space=pltpu.VMEM)] * 4 + [HBM],
        scratch_shapes=[pltpu.SemaphoreType.DMA],
    )(*parts, *in_hbm(w_uk))


def absorb_kernel(*refs):
    q_refs, (w_ref, out_ref) = refs[:2], refs[2:]
    lane = lax.broadcasted_iota(jnp.int32, (ROWS, 128), 1)
    row = lax.broadcasted_iota(jnp.int32, (ROWS, 128), 0)
    one_hot = (lane == row).astype(jnp.bfloat16)

    def columns(start):
        return jnp.concatenate([ref[:, start : start + 128] for ref in q_refs], axis=0)

    for h in range(HG):
        rows = slice(h * ROWS, (h + 1) * ROWS)
        latent = jnp.dot(columns(h * NOPE), w_ref[h], preferred_element_type=jnp.float32)
        out_ref[rows, :RANK] = latent.astype(jnp.bfloat16)
        pair = columns(HG * NOPE + (h // 2) * 128).astype(jnp.float32)
        if h % 2:
            pair = pltpu.roll(pair, ROPE, 1)
        rope = jnp.where(lane < ROPE, pair, 0.0)
        out_ref[rows, RANK : RANK + 128] = rope.astype(jnp.bfloat16)
        out_ref[rows, RANK + 128 :] = one_hot


def absorb(queries, w_uk):
    return call(absorb_kernel, jax.ShapeDtypeStruct((ITEMS, ITEMW), jnp.bfloat16))(
        *queries, w_uk
    )


def pack_stats(stats):
    high = stats.astype(jnp.bfloat16).astype(jnp.float32)
    mid = (stats - high).astype(jnp.bfloat16).astype(jnp.float32)
    low = stats - high - mid
    packed = high + pltpu.roll(mid, HG, 1) + pltpu.roll(low, 2 * HG, 1)
    return packed.astype(jnp.bfloat16)


def unpack_stats(packed):
    packed = packed.astype(jnp.float32)
    return packed + pltpu.roll(packed, 128 - HG, 1) + pltpu.roll(packed, 128 - 2 * HG, 1)


def attend_kernel(pieces, last, tile, unroll, *refs):
    q_ref, qpos_ref, v_ref = refs[:3]
    piece_refs = refs[3 : 3 + pieces]
    rest = refs[3 + pieces :]
    if last:
        part_in, lse_in, keep_ref, send_ref, key_ref, lse_ref = rest
        lse_ref[...] = jnp.zeros_like(lse_ref)
    else:
        part_out, lse_out, key_ref = rest

    qpos = qpos_ref[0:1, :]
    start = 0
    for ref in piece_refs:
        rows = slice(start, start + ref.shape[0])
        start += ref.shape[0]
        key_ref[rows, :KEYW] = ref[...]
        ext = ref[:, RANK:].astype(jnp.float32)
        pos = ext[:, ROPE : ROPE + 1] * 128.0 + ext[:, ROPE + 1 : ROPE + 2]
        key_ref[rows, KEYW:] = jnp.where(pos <= qpos, 0.0, NEG).astype(jnp.bfloat16)

    half = ROWS // 2
    heads = tile // ROWS

    def body(step):
        items = pl.ds(pl.multiple_of(step * tile, tile), tile)
        scores = nt_dot(q_ref[items, :], key_ref[...]) * SCALE2
        top = jnp.max(scores, axis=1, keepdims=True)
        weights = jnp.exp2(scores - top)
        total = jnp.sum(weights, axis=1, keepdims=True)
        acc = jnp.dot(
            weights.astype(jnp.bfloat16), key_ref[:, :RANK], preferred_element_type=jnp.float32
        )
        context = (acc * (1.0 / total)).astype(jnp.bfloat16)
        lse = top + jnp.log2(total)
        if last:
            earlier = lse_in[items, 0:1]
            top = jnp.maximum(lse, earlier)
            here, there = jnp.exp2(lse - top), jnp.exp2(earlier - top)
            total = here + there
            lse = top + jnp.log2(total)
            inverse = 1.0 / total
            here, there = here * inverse, there * inverse
        else:
            lse_out[items, :] = jnp.broadcast_to(lse, (tile, 128))

        lane = lax.broadcasted_iota(jnp.int32, (ROWS, 128), 1)
        for i in range(heads):
            rows = slice(i * ROWS, (i + 1) * ROWS)
            head = step * heads + i
            cols = pl.ds(pl.multiple_of(head * VDIM, VDIM), VDIM)
            out = jnp.dot(context[rows], v_ref[head], preferred_element_type=jnp.float32)
            if last:
                out = out * here[rows] + part_in[:, cols] * there[rows]
                out = out.astype(jnp.bfloat16)
                keep_ref[:, cols] = out[:half]
                send_ref[:, cols] = out[half:]
                lse_ref[...] = jnp.where(lane == head, lse[rows], lse_ref[...])
            else:
                part_out[:, cols] = out

    pl.loop(0, ITEMS // tile, unroll=unroll)(body)

    if last:
        packed = pack_stats(lse_ref[...])
        keep_ref[:, HG * VDIM :] = packed[:half]
        send_ref[:, HG * VDIM :] = packed[half:]


def attend(q, qpos, value_weight, pieces, earlier=None, tile=512, unroll=4):
    n, keys = len(pieces), sum(piece.shape[0] for piece in pieces)
    last = earlier is not None
    scratch = [pltpu.VMEM((keys, ITEMW), jnp.bfloat16)]
    if last:
        half = jax.ShapeDtypeStruct((ROWS // 2, SENDW), jnp.bfloat16)
        out_shape = (half, half)
        scratch.append(pltpu.VMEM((ROWS, 128), jnp.float32))
    else:
        out_shape = (
            jax.ShapeDtypeStruct((ROWS, HG * VDIM), jnp.float32),
            jax.ShapeDtypeStruct((ITEMS, 128), jnp.float32),
        )
    return call(
        functools.partial(attend_kernel, n, last, tile, unroll),
        out_shape,
        vmem=36,
        scratch_shapes=scratch,
    )(q, qpos, value_weight, *pieces, *(earlier or ()))


def merge(refs):
    stats = [unpack_stats(ref[:, HG * VDIM :]) for ref in refs]
    top = functools.reduce(jnp.maximum, stats)
    weights = [jnp.exp2(s - top) for s in stats]
    total = sum(weights)
    weights = [w / total for w in weights]
    out = []
    for h in range(HG):
        cols = slice(h * VDIM, (h + 1) * VDIM)
        head = sum(
            ref[:, cols].astype(jnp.float32) * w[:, h : h + 1] for ref, w in zip(refs, weights)
        )
        out.append((cols, head.astype(jnp.bfloat16)))
    return out, top + jnp.log2(total)


def merge_core_kernel(a_ref, b_ref, *out_refs):
    heads, lse = merge((a_ref, b_ref))
    lane = lax.broadcasted_iota(jnp.int32, lse.shape, 1)
    packed = pack_stats(jnp.where(lane < HG, lse, 0.0))
    for cols, head in heads + [(slice(HG * VDIM, SENDW), packed)]:
        for i, ref in enumerate(out_refs):
            ref[:, cols] = head[i * R : (i + 1) * R]


def merge_ring_kernel(*refs):
    heads, _ = merge(refs[:-1])
    for cols, head in heads:
        for i in range(refs[-1].shape[0]):
            refs[-1][i, :, cols] = head


def columns_kernel(zc_ref, *refs):
    z, c = zc_ref[0], zc_ref[1]
    w_refs, (out_ref, held, sems) = refs[:4], refs[4:]
    ncol, depth = w_refs[0].shape
    copies = [pltpu.make_async_copy(w_refs[k], held.at[k], sems.at[k]) for k in range(4)]
    for copy in copies:
        copy.start()
    for k in range(4):
        to_z = z if k % 2 == 0 else 1 - z
        to_c = c if k < 2 else 1 - c
        copies[k].wait()
        padded = jnp.concatenate(
            [held[k], jnp.zeros((128 - ncol, depth), jnp.bfloat16)], axis=0
        )
        out_ref[to_z * 2 + to_c] = jnp.transpose(padded)


def columns_of(zc, pieces):
    ncol, depth = pieces[0].shape
    return call(
        columns_kernel,
        jax.ShapeDtypeStruct((4, depth, 128), jnp.bfloat16),
        vmem=16,
        in_specs=[pl.BlockSpec(memory_space=pltpu.SMEM)] + [HBM] * 4,
        scratch_shapes=[
            pltpu.VMEM((4, ncol, depth), jnp.bfloat16),
            pltpu.SemaphoreType.DMA((4,)),
        ],
    )(zc, *in_hbm(pieces[0]), *pieces[1:])


def project_kernel(x_ref, w_ref, out_ref):
    for k in range(4):
        out = jnp.dot(x_ref[...], w_ref[k], preferred_element_type=jnp.float32)
        out_ref[k] = out[:, : out_ref.shape[2]].astype(jnp.bfloat16)


def finish_kernel(sums_ref, out_ref, row_ref):
    ncol = sums_ref.shape[2]
    row_ref[...] = jnp.zeros_like(row_ref)
    for zc in range(4):
        total = sum(sums_ref[zc * 4 + h].astype(jnp.float32) for h in range(4))
        for i in range(4):
            start = (i * 4 + zc) * R
            row_ref[start : start + R, :ncol] = total[i * R : (i + 1) * R]
    out_ref[...] = jnp.transpose(row_ref[...])[:ncol].astype(jnp.bfloat16)


def local(query_unrotated, q_rope, latent, k_rope, key_pos, offset, w_uk, value_up_weight, w_out):
    y, x, z, c = (lax.axis_index(n) for n in CTX)

    keys, q_own = pack(latent[0], k_rope[0], key_pos, query_unrotated, q_rope)
    z_keys = lax.ppermute(keys, "z", SWAP)
    up, down, across = (lax.ppermute(keys, "y", shift(d)) for d in (1, 3, 2))
    q_ring = [lax.ppermute(q_own, "x", shift(1)), lax.ppermute(q_own, "x", shift(3))]
    q_ring, q_own = lax.optimization_barrier((q_ring, q_own))
    q_ring.append(lax.ppermute(q_own, "x", shift(2)))
    z_keys, up, down, across = lax.optimization_barrier((z_keys, up, down, across))
    near = [keys, up, down, across]
    far = [z_keys] + [lax.ppermute(z_keys, "y", shift(d)) for d in RING[1:]]
    q_ring, w_own = lax.optimization_barrier((q_ring, jnp.transpose(w_out)))
    z_w = lax.ppermute(w_own, "z", SWAP)
    q_chip, w_absorb = join([q_own, *q_ring], w_uk)
    q_core = lax.ppermute(q_chip, "c", SWAP)

    row = jnp.arange(ROWS, dtype=jnp.int32)
    part = row // R
    row_x = (x - jnp.array(RING, jnp.int32)[part % 4]) % 4
    row_c = jnp.where(part < 4, c, 1 - c)
    row = (((y * 4 + row_x) * 2 + z) * 2 + row_c) * R + row % R
    qpos = jnp.broadcast_to((offset[0] + row).astype(jnp.float32)[None, :], (8, ROWS))

    q = absorb((q_chip, q_core), w_absorb)
    earlier = attend(q, qpos, value_up_weight, near)
    earlier, far = lax.optimization_barrier((earlier, far))
    keep, send = attend(q, qpos, value_up_weight, far, earlier)
    send, w_own = lax.optimization_barrier((send, w_own))

    z_w, send = lax.optimization_barrier((z_w, send))
    parts = call(
        merge_core_kernel, [jax.ShapeDtypeStruct((R, SENDW), jnp.bfloat16)] * 4
    )(keep, lax.ppermute(send, "c", SWAP))
    parts = [parts[0]] + [
        lax.ppermute(part, "x", shift(-d % 4)) for part, d in zip(parts[1:], RING[1:])
    ]
    c_w = lax.ppermute(w_own, "c", SWAP)
    zc_w = lax.ppermute(z_w, "c", SWAP)
    heads = call(merge_ring_kernel, jax.ShapeDtypeStruct((16, R, HG * VDIM), jnp.bfloat16))(
        *parts
    )

    rows = lax.all_to_all(heads, ("y", "x"), 0, 0, tiled=True).reshape(16 * R, HG * VDIM)
    ncol = w_out.shape[1]
    columns = columns_of(jnp.stack([z, c]), (w_own, z_w, c_w, zc_w))
    sums = call(
        project_kernel, jax.ShapeDtypeStruct((4, 16 * R, ncol), jnp.bfloat16), vmem=16
    )(rows, columns)
    sums = lax.all_to_all(
        sums.reshape(16, 4 * R, ncol), ("z", "c", "head"), 0, 0, tiled=True
    )
    out = call(
        finish_kernel,
        jax.ShapeDtypeStruct((ncol, 16 * R), jnp.bfloat16),
        scratch_shapes=[pltpu.VMEM((16 * R, 128), jnp.float32)],
    )(sums)
    return jnp.transpose(out)


def solution(mesh):
    grid = Mesh(mesh.devices.reshape(4, 4, 2, 2, 4), CTX + ("head",))
    return jax.shard_map(
        local,
        mesh=grid,
        in_specs=(
            P(CTX, "head"),
            P(CTX, "head"),
            P(None, CTX, None),
            P(None, CTX, None),
            P(None, CTX),
            P(),
            P("head", None, None),
            P("head", None, None),
            P("head", CTX),
        ),
        out_specs=P("head", CTX),
        check_vma=False,
    )
```

```python
import functools

import jax
import jax.numpy as jnp
from jax import lax
from jax.experimental import pallas as pl
from jax.experimental.pallas import tpu as pltpu
from jax.sharding import Mesh, PartitionSpec as P

ROPE = 64
NOPE = 128
RANK = 512
VDIM = 128
HG = 16
R = 16
GROUP = 8
ROWS = GROUP * R
ITEMS = HG * ROWS
KEYW = RANK + 128
ITEMW = RANK + 256
SENDW = HG * VDIM + 128
SCALE2 = (NOPE + ROPE) ** -0.5 * 1.4426950408889634
NEG = -1e30
CTX = ("y", "x", "z", "c")
RING = (0, 1, 3, 2)
SWAP = ((0, 1), (1, 0))
MIB = 1 << 20


def shift(d):
    return [(i, (i + d) % 4) for i in range(4)]


def call(kernel, out_shape, vmem=8, **kw):
    return pl.pallas_call(
        kernel,
        out_shape=out_shape,
        compiler_params=pltpu.CompilerParams(vmem_limit_bytes=vmem * MIB),
        cost_estimate=pl.CostEstimate(flops=1, bytes_accessed=1, transcendentals=0),
        **kw,
    )


def nt_dot(a, b):
    return lax.dot_general(a, b, (((1,), (1,)), ((), ())), preferred_element_type=jnp.float32)


HBM = pl.BlockSpec(memory_space=pltpu.HBM)


def in_hbm(*arrays):
    return [pltpu.with_memory_space_constraint(a, pltpu.HBM) for a in arrays]


def pack_kernel(
    latent_ref, key_rope_ref, pos_ref, query_ref, q_rope_ref, key_ref, q_ref, rope, pos, sems
):
    copies = [
        pltpu.make_async_copy(key_rope_ref, rope, sems.at[0]),
        pltpu.make_async_copy(pos_ref, pos, sems.at[1]),
        pltpu.make_async_copy(latent_ref, key_ref.at[:, :RANK], sems.at[2]),
    ]
    for i in range(4):
        copies += [
            pltpu.make_async_copy(query_ref, q_ref.at[i, :, : HG * NOPE], sems.at[3 + 2 * i]),
            pltpu.make_async_copy(q_rope_ref, q_ref.at[i, :, HG * NOPE :], sems.at[4 + 2 * i]),
        ]
    for copy in copies:
        copy.start()
    copies[0].wait()
    copies[1].wait()
    where = pos[...].astype(jnp.float32)
    high = jnp.floor(where * (1 / 128))
    row = lax.broadcasted_iota(jnp.int32, rope.shape, 0)
    ext = jnp.where(row == 0, high, jnp.where(row == 1, where - high * 128, 0.0))
    ext = jnp.concatenate([rope[...].astype(jnp.float32), ext], axis=0)
    key_ref[:, RANK:] = jnp.transpose(ext).astype(jnp.bfloat16)
    for copy in copies[2:]:
        copy.wait()


def pack(latent, k_rope, key_pos, query, q_rope):
    return call(
        pack_kernel,
        (
            jax.ShapeDtypeStruct((latent.shape[0], KEYW), jnp.bfloat16),
            jax.ShapeDtypeStruct((4, R, HG * (NOPE + ROPE)), jnp.bfloat16),
        ),
        in_specs=[HBM] * 5,
        scratch_shapes=[
            pltpu.VMEM((k_rope.shape[1], k_rope.shape[0]), jnp.bfloat16),
            pltpu.VMEM(key_pos.shape, jnp.int32),
            pltpu.SemaphoreType.DMA((11,)),
        ],
    )(*in_hbm(latent, jnp.transpose(k_rope), key_pos, query, q_rope))


def absorb_kernel(*refs):
    q_refs, (w_hbm, out_ref, w_ref, sems) = refs[:2], refs[2:]
    step = HG // 4
    copies = [
        pltpu.make_async_copy(
            w_hbm.at[i * step : (i + 1) * step],
            w_ref.at[i * step : (i + 1) * step],
            sems.at[i],
        )
        for i in range(4)
    ]
    for copy in copies:
        copy.start()
    lane = lax.broadcasted_iota(jnp.int32, (ROWS, 128), 1)
    row = lax.broadcasted_iota(jnp.int32, (ROWS, 128), 0)
    one_hot = (lane == row).astype(jnp.bfloat16)

    def columns(start):
        return jnp.concatenate([ref[:, start : start + 128] for ref in q_refs], axis=0)

    for h in range(HG):
        if h % step == 0:
            copies[h // step].wait()
        rows = slice(h * ROWS, (h + 1) * ROWS)
        latent = jnp.dot(columns(h * NOPE), w_ref[h], preferred_element_type=jnp.float32)
        out_ref[rows, :RANK] = latent.astype(jnp.bfloat16)
        pair = columns(HG * NOPE + (h // 2) * 128).astype(jnp.float32)
        if h % 2:
            pair = pltpu.roll(pair, ROPE, 1)
        rope = jnp.where(lane < ROPE, pair, 0.0)
        out_ref[rows, RANK : RANK + 128] = rope.astype(jnp.bfloat16)
        out_ref[rows, RANK + 128 :] = one_hot


def absorb(queries, w_uk):
    return call(
        absorb_kernel,
        jax.ShapeDtypeStruct((ITEMS, ITEMW), jnp.bfloat16),
        vmem=16,
        in_specs=[pl.BlockSpec(memory_space=pltpu.VMEM)] * 2 + [HBM],
        scratch_shapes=[
            pltpu.VMEM(w_uk.shape, jnp.bfloat16),
            pltpu.SemaphoreType.DMA((4,)),
        ],
    )(*queries, *in_hbm(w_uk))


def pack_stats(stats):
    high = stats.astype(jnp.bfloat16).astype(jnp.float32)
    mid = (stats - high).astype(jnp.bfloat16).astype(jnp.float32)
    low = stats - high - mid
    packed = high + pltpu.roll(mid, HG, 1) + pltpu.roll(low, 2 * HG, 1)
    return packed.astype(jnp.bfloat16)


def unpack_stats(packed):
    packed = packed.astype(jnp.float32)
    return packed + pltpu.roll(packed, 128 - HG, 1) + pltpu.roll(packed, 128 - 2 * HG, 1)


def attend_kernel(pieces, last, tile, unroll, *refs):
    q_ref, qpos_ref, v_ref = refs[:3]
    piece_refs = refs[3 : 3 + pieces]
    rest = refs[3 + pieces :]
    if last:
        part_in, lse_in, keep_ref, send_ref, key_ref, lse_ref = rest
        lse_ref[...] = jnp.zeros_like(lse_ref)
    else:
        part_out, lse_out, key_ref = rest

    qpos = qpos_ref[0:1, :]
    start = 0
    for ref in piece_refs:
        rows = slice(start, start + ref.shape[0])
        start += ref.shape[0]
        key_ref[rows, :KEYW] = ref[...]
        ext = ref[:, RANK:].astype(jnp.float32)
        pos = ext[:, ROPE : ROPE + 1] * 128.0 + ext[:, ROPE + 1 : ROPE + 2]
        key_ref[rows, KEYW:] = jnp.where(pos <= qpos, 0.0, NEG).astype(jnp.bfloat16)

    half = ROWS // 2
    heads = tile // ROWS

    def body(step):
        items = pl.ds(pl.multiple_of(step * tile, tile), tile)
        scores = nt_dot(q_ref[items, :], key_ref[...]) * SCALE2
        top = jnp.max(scores, axis=1, keepdims=True)
        weights = jnp.exp2(scores - top)
        total = jnp.sum(weights, axis=1, keepdims=True)
        acc = jnp.dot(
            weights.astype(jnp.bfloat16), key_ref[:, :RANK], preferred_element_type=jnp.float32
        )
        context = (acc * (1.0 / total)).astype(jnp.bfloat16)
        lse = top + jnp.log2(total)
        if last:
            earlier = lse_in[items, 0:1]
            top = jnp.maximum(lse, earlier)
            here, there = jnp.exp2(lse - top), jnp.exp2(earlier - top)
            total = here + there
            lse = top + jnp.log2(total)
            inverse = 1.0 / total
            here, there = here * inverse, there * inverse
        else:
            lse_out[items, :] = jnp.broadcast_to(lse, (tile, 128))

        lane = lax.broadcasted_iota(jnp.int32, (ROWS, 128), 1)
        for i in range(heads):
            rows = slice(i * ROWS, (i + 1) * ROWS)
            head = step * heads + i
            cols = pl.ds(pl.multiple_of(head * VDIM, VDIM), VDIM)
            out = jnp.dot(context[rows], v_ref[head], preferred_element_type=jnp.float32)
            if last:
                out = out * here[rows] + part_in[:, cols] * there[rows]
                out = out.astype(jnp.bfloat16)
                keep_ref[:, cols] = out[:half]
                send_ref[:, cols] = out[half:]
                lse_ref[...] = jnp.where(lane == head, lse[rows], lse_ref[...])
            else:
                part_out[:, cols] = out

    pl.loop(0, ITEMS // tile, unroll=unroll)(body)

    if last:
        packed = pack_stats(lse_ref[...])
        keep_ref[:, HG * VDIM :] = packed[:half]
        send_ref[:, HG * VDIM :] = packed[half:]


def attend(q, qpos, value_weight, pieces, earlier=None, tile=512, unroll=4):
    n, keys = len(pieces), sum(piece.shape[0] for piece in pieces)
    last = earlier is not None
    scratch = [pltpu.VMEM((keys, ITEMW), jnp.bfloat16)]
    if last:
        half = jax.ShapeDtypeStruct((ROWS // 2, SENDW), jnp.bfloat16)
        out_shape = (half, half)
        scratch.append(pltpu.VMEM((ROWS, 128), jnp.float32))
    else:
        out_shape = (
            jax.ShapeDtypeStruct((ROWS, HG * VDIM), jnp.float32),
            jax.ShapeDtypeStruct((ITEMS, 128), jnp.float32),
        )
    return call(
        functools.partial(attend_kernel, n, last, tile, unroll),
        out_shape,
        vmem=36,
        scratch_shapes=scratch,
    )(q, qpos, value_weight, *pieces, *(earlier or ()))


def merge(refs, rows=slice(None)):
    stats = [unpack_stats(ref[rows, HG * VDIM :]) for ref in refs]
    top = functools.reduce(jnp.maximum, stats)
    weights = [jnp.exp2(s - top) for s in stats]
    total = sum(weights)
    weights = [w / total for w in weights]
    out = []
    for h in range(HG):
        cols = slice(h * VDIM, (h + 1) * VDIM)
        head = sum(
            ref[rows, cols].astype(jnp.float32) * w[:, h : h + 1]
            for ref, w in zip(refs, weights)
        )
        out.append((cols, head.astype(jnp.bfloat16)))
    return out, top + jnp.log2(total)


def merge_core_kernel(x_ref, a_ref, b_ref, *out_refs):
    for d, ref in enumerate(out_refs):
        block = lax.rem(x_ref[0] + d, 4)
        rows = pl.ds(pl.multiple_of(block * R, R), R)
        heads, lse = merge((a_ref, b_ref), rows)
        lane = lax.broadcasted_iota(jnp.int32, lse.shape, 1)
        packed = pack_stats(jnp.where(lane < HG, lse, 0.0))
        for cols, head in heads + [(slice(HG * VDIM, SENDW), packed)]:
            ref[:, cols] = head


def merge_ring_kernel(*refs):
    heads, _ = merge(refs[:-1])
    for cols, head in heads:
        for i in range(refs[-1].shape[0]):
            refs[-1][i, :, cols] = head


def columns_kernel(zc_ref, *refs):
    z, c = zc_ref[0], zc_ref[1]
    w_refs, (out_ref, held, sems) = refs[:4], refs[4:]
    ncol, depth = w_refs[0].shape
    copies = [pltpu.make_async_copy(w_refs[k], held.at[k], sems.at[k]) for k in range(4)]
    for copy in copies:
        copy.start()
    for k in range(4):
        to_z = z if k % 2 == 0 else 1 - z
        to_c = c if k < 2 else 1 - c
        copies[k].wait()
        padded = jnp.concatenate(
            [held[k], jnp.zeros((128 - ncol, depth), jnp.bfloat16)], axis=0
        )
        out_ref[to_z * 2 + to_c] = jnp.transpose(padded)


def columns_of(zc, pieces):
    ncol, depth = pieces[0].shape
    return call(
        columns_kernel,
        jax.ShapeDtypeStruct((4, depth, 128), jnp.bfloat16),
        vmem=16,
        in_specs=[pl.BlockSpec(memory_space=pltpu.SMEM)] + [HBM] * 4,
        scratch_shapes=[
            pltpu.VMEM((4, ncol, depth), jnp.bfloat16),
            pltpu.SemaphoreType.DMA((4,)),
        ],
    )(zc, *in_hbm(pieces[0]), *pieces[1:])


def project_kernel(x_ref, w_ref, out_ref):
    for k in range(4):
        out = jnp.dot(x_ref[...], w_ref[k], preferred_element_type=jnp.float32)
        out_ref[k] = out[:, : out_ref.shape[2]].astype(jnp.bfloat16)


def finish_kernel(sums_ref, out_ref, row_ref):
    ncol = sums_ref.shape[2]
    row_ref[...] = jnp.zeros_like(row_ref)
    for zc in range(4):
        total = sum(sums_ref[zc * 4 + h].astype(jnp.float32) for h in range(4))
        for i in range(4):
            start = (i * 4 + zc) * R
            row_ref[start : start + R, :ncol] = total[i * R : (i + 1) * R]
    out_ref[...] = jnp.transpose(row_ref[...])[:ncol].astype(jnp.bfloat16)


def local(query_unrotated, q_rope, latent, k_rope, key_pos, offset, w_uk, value_up_weight, w_out):
    y, x, z, c = (lax.axis_index(n) for n in CTX)

    keys, q_own = pack(latent[0], k_rope[0], key_pos, query_unrotated, q_rope)
    z_keys = lax.ppermute(keys, "z", SWAP)
    up, down, across = (lax.ppermute(keys, "y", shift(d)) for d in (1, 3, 2))
    q_chip = lax.all_to_all(q_own, "x", 0, 0, tiled=True).reshape(4 * R, -1)
    z_keys, up, down, across = lax.optimization_barrier((z_keys, up, down, across))
    near = [keys, up, down, across]
    far = [z_keys] + [lax.ppermute(z_keys, "y", shift(d)) for d in RING[1:]]
    q_chip, w_own = lax.optimization_barrier((q_chip, jnp.transpose(w_out)))
    q_core = lax.ppermute(q_chip, "c", SWAP)
    z_w = lax.ppermute(w_own, "z", SWAP)

    row = jnp.arange(ROWS, dtype=jnp.int32)
    part = row // R
    row_x = part % 4
    row_c = jnp.where(part < 4, c, 1 - c)
    row = (((y * 4 + row_x) * 2 + z) * 2 + row_c) * R + row % R
    qpos = jnp.broadcast_to((offset[0] + row).astype(jnp.float32)[None, :], (8, ROWS))

    q = absorb((q_chip, q_core), w_uk)
    earlier = attend(q, qpos, value_up_weight, near)
    earlier, far = lax.optimization_barrier((earlier, far))
    keep, send = attend(q, qpos, value_up_weight, far, earlier)

    parts = call(
        merge_core_kernel,
        [jax.ShapeDtypeStruct((R, SENDW), jnp.bfloat16)] * 4,
        in_specs=[pl.BlockSpec(memory_space=pltpu.SMEM)]
        + [pl.BlockSpec(memory_space=pltpu.VMEM)] * 2,
    )(x.reshape(1), keep, lax.ppermute(send, "c", SWAP))
    parts = [parts[0]] + [lax.ppermute(parts[d], "x", shift(d)) for d in (1, 2, 3)]
    zc_w = lax.ppermute(z_w, "c", SWAP)
    heads = call(merge_ring_kernel, jax.ShapeDtypeStruct((16, R, HG * VDIM), jnp.bfloat16))(
        *parts
    )

    heads, w_own = lax.optimization_barrier((heads, w_own))
    c_w = lax.ppermute(w_own, "c", SWAP)
    rows = lax.all_to_all(heads, ("y", "x"), 0, 0, tiled=True).reshape(16 * R, HG * VDIM)
    ncol = w_out.shape[1]
    columns = columns_of(jnp.stack([z, c]), (w_own, z_w, c_w, zc_w))
    sums = call(
        project_kernel, jax.ShapeDtypeStruct((4, 16 * R, ncol), jnp.bfloat16), vmem=16
    )(rows, columns)
    sums = lax.all_to_all(
        sums.reshape(16, 4 * R, ncol), ("z", "c", "head"), 0, 0, tiled=True
    )
    out = call(
        finish_kernel,
        jax.ShapeDtypeStruct((ncol, 16 * R), jnp.bfloat16),
        scratch_shapes=[pltpu.VMEM((16 * R, 128), jnp.float32)],
    )(sums)
    return jnp.transpose(out)


def solution(mesh):
    grid = Mesh(mesh.devices.reshape(4, 4, 2, 2, 4), CTX + ("head",))
    return jax.shard_map(
        local,
        mesh=grid,
        in_specs=(
            P(CTX, "head"),
            P(CTX, "head"),
            P(None, CTX, None),
            P(None, CTX, None),
            P(None, CTX),
            P(),
            P("head", None, None),
            P("head", None, None),
            P("head", CTX),
        ),
        out_specs=P("head", CTX),
        check_vma=False,
    )
```

```python
import functools

import jax
import jax.numpy as jnp
from jax import lax
from jax.experimental import pallas as pl
from jax.experimental.pallas import tpu as pltpu
from jax.sharding import Mesh, PartitionSpec as P

ROPE = 64
NOPE = 128
RANK = 512
VDIM = 128
HG = 16
R = 16
GROUP = 8
ROWS = GROUP * R
ITEMS = HG * ROWS
KEYW = RANK + 128
ITEMW = RANK + 256
SENDW = HG * VDIM + 128
SCALE2 = (NOPE + ROPE) ** -0.5 * 1.4426950408889634
NEG = -1e30
CTX = ("y", "x", "z", "c")
RING = (0, 1, 3, 2)
SWAP = ((0, 1), (1, 0))
MIB = 1 << 20


def shift(d):
    return [(i, (i + d) % 4) for i in range(4)]


def call(kernel, out_shape, vmem=8, **kw):
    return pl.pallas_call(
        kernel,
        out_shape=out_shape,
        compiler_params=pltpu.CompilerParams(vmem_limit_bytes=vmem * MIB),
        cost_estimate=pl.CostEstimate(flops=1, bytes_accessed=1, transcendentals=0),
        **kw,
    )


def nt_dot(a, b):
    return lax.dot_general(a, b, (((1,), (1,)), ((), ())), preferred_element_type=jnp.float32)


HBM = pl.BlockSpec(memory_space=pltpu.HBM)


def in_hbm(*arrays):
    return [pltpu.with_memory_space_constraint(a, pltpu.HBM) for a in arrays]


def pack_kernel(
    latent_ref, key_rope_ref, pos_ref, query_ref, q_rope_ref, key_ref, q_ref, rope, pos, sems
):
    copies = [
        pltpu.make_async_copy(key_rope_ref, rope, sems.at[0]),
        pltpu.make_async_copy(pos_ref, pos, sems.at[1]),
        pltpu.make_async_copy(latent_ref, key_ref.at[:, :RANK], sems.at[2]),
        pltpu.make_async_copy(query_ref, q_ref.at[:, : HG * NOPE], sems.at[3]),
        pltpu.make_async_copy(q_rope_ref, q_ref.at[:, HG * NOPE :], sems.at[4]),
    ]
    for copy in copies:
        copy.start()
    copies[0].wait()
    copies[1].wait()
    where = pos[...].astype(jnp.float32)
    high = jnp.floor(where * (1 / 128))
    row = lax.broadcasted_iota(jnp.int32, rope.shape, 0)
    ext = jnp.where(row == 0, high, jnp.where(row == 1, where - high * 128, 0.0))
    ext = jnp.concatenate([rope[...].astype(jnp.float32), ext], axis=0)
    key_ref[:, RANK:] = jnp.transpose(ext).astype(jnp.bfloat16)
    for copy in copies[2:]:
        copy.wait()


def pack(latent, k_rope, key_pos, query, q_rope):
    return call(
        pack_kernel,
        (
            jax.ShapeDtypeStruct((latent.shape[0], KEYW), jnp.bfloat16),
            jax.ShapeDtypeStruct((R, HG * (NOPE + ROPE)), jnp.bfloat16),
        ),
        in_specs=[HBM] * 5,
        scratch_shapes=[
            pltpu.VMEM((k_rope.shape[1], k_rope.shape[0]), jnp.bfloat16),
            pltpu.VMEM(key_pos.shape, jnp.int32),
            pltpu.SemaphoreType.DMA((5,)),
        ],
    )(*in_hbm(latent, jnp.transpose(k_rope), key_pos, query, q_rope))


def join_kernel(*refs):
    start = 0
    for ref in refs[:-1]:
        refs[-1][start : start + ref.shape[0]] = ref[...]
        start += ref.shape[0]


def join(parts):
    shape = (sum(part.shape[0] for part in parts), parts[0].shape[1])
    return call(join_kernel, jax.ShapeDtypeStruct(shape, jnp.bfloat16))(*parts)


def absorb_kernel(*refs):
    q_refs, (w_hbm, out_ref, w_ref, sems) = refs[:2], refs[2:]
    step = HG // 4
    copies = [
        pltpu.make_async_copy(
            w_hbm.at[i * step : (i + 1) * step],
            w_ref.at[i * step : (i + 1) * step],
            sems.at[i],
        )
        for i in range(4)
    ]
    for copy in copies:
        copy.start()
    lane = lax.broadcasted_iota(jnp.int32, (ROWS, 128), 1)
    row = lax.broadcasted_iota(jnp.int32, (ROWS, 128), 0)
    one_hot = (lane == row).astype(jnp.bfloat16)

    def columns(start):
        return jnp.concatenate([ref[:, start : start + 128] for ref in q_refs], axis=0)

    for h in range(HG):
        rows = slice(h * ROWS, (h + 1) * ROWS)
        pair = columns(HG * NOPE + (h // 2) * 128).astype(jnp.float32)
        if h % 2:
            pair = pltpu.roll(pair, ROPE, 1)
        rope = jnp.where(lane < ROPE, pair, 0.0)
        out_ref[rows, RANK : RANK + 128] = rope.astype(jnp.bfloat16)
        out_ref[rows, RANK + 128 :] = one_hot
    for h in range(HG):
        if h % step == 0:
            copies[h // step].wait()
        rows = slice(h * ROWS, (h + 1) * ROWS)
        latent = jnp.dot(columns(h * NOPE), w_ref[h], preferred_element_type=jnp.float32)
        out_ref[rows, :RANK] = latent.astype(jnp.bfloat16)


def absorb(queries, w_uk):
    return call(
        absorb_kernel,
        jax.ShapeDtypeStruct((ITEMS, ITEMW), jnp.bfloat16),
        vmem=16,
        in_specs=[pl.BlockSpec(memory_space=pltpu.VMEM)] * 2 + [HBM],
        scratch_shapes=[
            pltpu.VMEM(w_uk.shape, jnp.bfloat16),
            pltpu.SemaphoreType.DMA((4,)),
        ],
    )(*queries, *in_hbm(w_uk))


def pack_stats(stats):
    high = stats.astype(jnp.bfloat16).astype(jnp.float32)
    mid = (stats - high).astype(jnp.bfloat16).astype(jnp.float32)
    low = stats - high - mid
    packed = high + pltpu.roll(mid, HG, 1) + pltpu.roll(low, 2 * HG, 1)
    return packed.astype(jnp.bfloat16)


def unpack_stats(packed):
    packed = packed.astype(jnp.float32)
    return packed + pltpu.roll(packed, 128 - HG, 1) + pltpu.roll(packed, 128 - 2 * HG, 1)


def attend_kernel(pieces, last, tile, unroll, *refs):
    q_ref, qpos_ref, v_ref = refs[:3]
    piece_refs = refs[3 : 3 + pieces]
    rest = refs[3 + pieces :]
    if last:
        part_in, lse_in, keep_ref, send_ref, key_ref, lse_ref = rest
        lse_ref[...] = jnp.zeros_like(lse_ref)
    else:
        part_out, lse_out, key_ref = rest

    qpos = qpos_ref[0:1, :]
    start = 0
    for ref in piece_refs:
        rows = slice(start, start + ref.shape[0])
        start += ref.shape[0]
        key_ref[rows, :KEYW] = ref[...]
        ext = ref[:, RANK:].astype(jnp.float32)
        pos = ext[:, ROPE : ROPE + 1] * 128.0 + ext[:, ROPE + 1 : ROPE + 2]
        key_ref[rows, KEYW:] = jnp.where(pos <= qpos, 0.0, NEG).astype(jnp.bfloat16)

    half = ROWS // 2
    heads = tile // ROWS

    def body(step):
        items = pl.ds(pl.multiple_of(step * tile, tile), tile)
        scores = nt_dot(q_ref[items, :], key_ref[...]) * SCALE2
        top = jnp.max(scores, axis=1, keepdims=True)
        weights = jnp.exp2(scores - top)
        total = jnp.sum(weights, axis=1, keepdims=True)
        acc = jnp.dot(
            weights.astype(jnp.bfloat16), key_ref[:, :RANK], preferred_element_type=jnp.float32
        )
        context = (acc * (1.0 / total)).astype(jnp.bfloat16)
        lse = top + jnp.log2(total)
        if last:
            earlier = lse_in[items, 0:1]
            top = jnp.maximum(lse, earlier)
            here, there = jnp.exp2(lse - top), jnp.exp2(earlier - top)
            total = here + there
            lse = top + jnp.log2(total)
            inverse = 1.0 / total
            here, there = here * inverse, there * inverse
        else:
            lse_out[items, :] = jnp.broadcast_to(lse, (tile, 128))

        lane = lax.broadcasted_iota(jnp.int32, (ROWS, 128), 1)
        for i in range(heads):
            rows = slice(i * ROWS, (i + 1) * ROWS)
            head = step * heads + i
            cols = pl.ds(pl.multiple_of(head * VDIM, VDIM), VDIM)
            out = jnp.dot(context[rows], v_ref[head], preferred_element_type=jnp.float32)
            if last:
                out = out * here[rows] + part_in[:, cols] * there[rows]
                out = out.astype(jnp.bfloat16)
                keep_ref[:, cols] = out[:half]
                send_ref[:, cols] = out[half:]
                lse_ref[...] = jnp.where(lane == head, lse[rows], lse_ref[...])
            else:
                part_out[:, cols] = out

    pl.loop(0, ITEMS // tile, unroll=unroll)(body)

    if last:
        packed = pack_stats(lse_ref[...])
        keep_ref[:, HG * VDIM :] = packed[:half]
        send_ref[:, HG * VDIM :] = packed[half:]


def attend(q, qpos, value_weight, pieces, earlier=None, tile=1024, unroll=2):
    n, keys = len(pieces), sum(piece.shape[0] for piece in pieces)
    last = earlier is not None
    scratch = [pltpu.VMEM((keys, ITEMW), jnp.bfloat16)]
    if last:
        half = jax.ShapeDtypeStruct((ROWS // 2, SENDW), jnp.bfloat16)
        out_shape = (half, half)
        scratch.append(pltpu.VMEM((ROWS, 128), jnp.float32))
    else:
        out_shape = (
            jax.ShapeDtypeStruct((ROWS, HG * VDIM), jnp.float32),
            jax.ShapeDtypeStruct((ITEMS, 128), jnp.float32),
        )
    return call(
        functools.partial(attend_kernel, n, last, tile, unroll),
        out_shape,
        vmem=36,
        scratch_shapes=scratch,
    )(q, qpos, value_weight, *pieces, *(earlier or ()))


def merge(refs):
    stats = [unpack_stats(ref[:, HG * VDIM :]) for ref in refs]
    top = functools.reduce(jnp.maximum, stats)
    weights = [jnp.exp2(s - top) for s in stats]
    total = sum(weights)
    weights = [w / total for w in weights]
    out = []
    for h in range(HG):
        cols = slice(h * VDIM, (h + 1) * VDIM)
        head = sum(
            ref[:, cols].astype(jnp.float32) * w[:, h : h + 1] for ref, w in zip(refs, weights)
        )
        out.append((cols, head.astype(jnp.bfloat16)))
    return out, top + jnp.log2(total)


def merge_core_kernel(a_ref, b_ref, *out_refs):
    heads, lse = merge((a_ref, b_ref))
    lane = lax.broadcasted_iota(jnp.int32, lse.shape, 1)
    packed = pack_stats(jnp.where(lane < HG, lse, 0.0))
    for cols, head in heads + [(slice(HG * VDIM, SENDW), packed)]:
        for i, ref in enumerate(out_refs):
            ref[:, cols] = head[i * R : (i + 1) * R]


def merge_ring_kernel(*refs):
    heads, _ = merge(refs[:-1])
    for cols, head in heads:
        for i in range(refs[-1].shape[0]):
            refs[-1][i, :, cols] = head


def columns_kernel(zc_ref, own_ref, *refs):
    z, c = zc_ref[0], zc_ref[1]
    w_refs, (out_ref, held, sem) = refs[:3], refs[3:]
    ncol, depth = held.shape
    copy = pltpu.make_async_copy(own_ref, held, sem)
    copy.start()
    for k in (1, 2, 3, 0):
        to_z = z if k % 2 == 0 else 1 - z
        to_c = c if k < 2 else 1 - c
        if k == 0:
            copy.wait()
        piece = held[...] if k == 0 else w_refs[k - 1][...]
        padded = jnp.concatenate([piece, jnp.zeros((128 - ncol, depth), jnp.bfloat16)], axis=0)
        lanes = pl.ds(pl.multiple_of((to_z * 2 + to_c) * 128, 128), 128)
        out_ref[:, lanes] = jnp.transpose(padded)


def columns_of(zc, pieces):
    ncol, depth = pieces[0].shape
    return call(
        columns_kernel,
        jax.ShapeDtypeStruct((depth, 4 * 128), jnp.bfloat16),
        vmem=16,
        in_specs=[pl.BlockSpec(memory_space=pltpu.SMEM), HBM]
        + [pl.BlockSpec(memory_space=pltpu.VMEM)] * 3,
        scratch_shapes=[
            pltpu.VMEM((ncol, depth), jnp.bfloat16),
            pltpu.SemaphoreType.DMA,
        ],
    )(zc, *in_hbm(pieces[0]), *pieces[1:])


def project_kernel(x_ref, w_ref, out_ref):
    ncol = out_ref.shape[2]
    out = jnp.dot(x_ref[...], w_ref[...], preferred_element_type=jnp.float32)
    for k in range(4):
        out_ref[k] = out[:, k * 128 : k * 128 + ncol].astype(jnp.bfloat16)


def finish_kernel(sums_ref, out_ref, row_ref):
    ncol = sums_ref.shape[2]
    row_ref[...] = jnp.zeros_like(row_ref)
    for zc in range(4):
        total = sum(sums_ref[zc * 4 + h].astype(jnp.float32) for h in range(4))
        for i in range(4):
            start = (i * 4 + zc) * R
            row_ref[start : start + R, :ncol] = total[i * R : (i + 1) * R]
    out_ref[...] = jnp.transpose(row_ref[...])[:ncol].astype(jnp.bfloat16)


def local(query_unrotated, q_rope, latent, k_rope, key_pos, offset, w_uk, value_up_weight, w_out):
    y, x, z, c = (lax.axis_index(n) for n in CTX)

    keys, q_own = pack(latent[0], k_rope[0], key_pos, query_unrotated, q_rope)
    z_keys = lax.ppermute(keys, "z", SWAP)
    up, down, across = (lax.ppermute(keys, "y", shift(d)) for d in (1, 3, 2))
    q_ring = [lax.ppermute(q_own, "x", shift(1)), lax.ppermute(q_own, "x", shift(3))]
    q_ring, q_own = lax.optimization_barrier((q_ring, q_own))
    q_ring.append(lax.ppermute(q_own, "x", shift(2)))
    z_keys, up, down, across = lax.optimization_barrier((z_keys, up, down, across))
    near = [keys, up, down, across]
    far = [z_keys] + [lax.ppermute(z_keys, "y", shift(d)) for d in RING[1:]]
    q_chip, w_own = lax.optimization_barrier((join([q_own, *q_ring]), jnp.transpose(w_out)))
    q_core = lax.ppermute(q_chip, "c", SWAP)
    z_w = lax.ppermute(w_own, "z", SWAP)

    row = jnp.arange(ROWS, dtype=jnp.int32)
    part = row // R
    row_x = (x - jnp.array(RING, jnp.int32)[part % 4]) % 4
    row_c = jnp.where(part < 4, c, 1 - c)
    row = (((y * 4 + row_x) * 2 + z) * 2 + row_c) * R + row % R
    qpos = jnp.broadcast_to((offset[0] + row).astype(jnp.float32)[None, :], (8, ROWS))

    q = absorb((q_chip, q_core), w_uk)
    earlier = attend(q, qpos, value_up_weight, near)
    earlier, far = lax.optimization_barrier((earlier, far))
    keep, send = attend(q, qpos, value_up_weight, far, earlier)

    z_w, send = lax.optimization_barrier((z_w, send))
    parts = call(
        merge_core_kernel, [jax.ShapeDtypeStruct((R, SENDW), jnp.bfloat16)] * 4
    )(keep, lax.ppermute(send, "c", SWAP))
    parts = [parts[0]] + [
        lax.ppermute(part, "x", shift(-d % 4)) for part, d in zip(parts[1:], RING[1:])
    ]
    c_w = lax.ppermute(w_own, "c", SWAP)
    zc_w = lax.ppermute(z_w, "c", SWAP)
    parts, c_w = lax.optimization_barrier((parts, c_w))
    heads = call(merge_ring_kernel, jax.ShapeDtypeStruct((16, R, HG * VDIM), jnp.bfloat16))(
        *parts
    )

    rows = lax.all_to_all(heads, ("y", "x"), 0, 0, tiled=True).reshape(16 * R, HG * VDIM)
    ncol = w_out.shape[1]
    columns = columns_of(jnp.stack([z, c]), (w_own, z_w, c_w, zc_w))
    sums = call(
        project_kernel, jax.ShapeDtypeStruct((4, 16 * R, ncol), jnp.bfloat16), vmem=16
    )(rows, columns)
    sums = lax.all_to_all(
        sums.reshape(16, 4 * R, ncol), ("z", "c", "head"), 0, 0, tiled=True
    )
    out = call(
        finish_kernel,
        jax.ShapeDtypeStruct((ncol, 16 * R), jnp.bfloat16),
        scratch_shapes=[pltpu.VMEM((16 * R, 128), jnp.float32)],
    )(sums)
    return jnp.transpose(out)


def solution(mesh):
    grid = Mesh(mesh.devices.reshape(4, 4, 2, 2, 4), CTX + ("head",))
    return jax.shard_map(
        local,
        mesh=grid,
        in_specs=(
            P(CTX, "head"),
            P(CTX, "head"),
            P(None, CTX, None),
            P(None, CTX, None),
            P(None, CTX),
            P(),
            P("head", None, None),
            P("head", None, None),
            P("head", CTX),
        ),
        out_specs=P("head", CTX),
        check_vma=False,
    )
```

```python
import functools

import jax
import jax.numpy as jnp
from jax import lax
from jax.experimental import pallas as pl
from jax.experimental.pallas import tpu as pltpu
from jax.sharding import Mesh, PartitionSpec as P

ROPE = 64
NOPE = 128
RANK = 512
VDIM = 128
HG = 16
R = 16
GROUP = 8
ROWS = GROUP * R
ITEMS = HG * ROWS
KEYW = RANK + 128
ITEMW = RANK + 256
SENDW = HG * VDIM + 128
SCALE2 = (NOPE + ROPE) ** -0.5 * 1.4426950408889634
NEG = -1e30
CTX = ("y", "x", "z", "c")
RING = (0, 1, 3, 2)
SWAP = ((0, 1), (1, 0))
MIB = 1 << 20


def shift(d):
    return [(i, (i + d) % 4) for i in range(4)]


def call(kernel, out_shape, vmem=8, **kw):
    return pl.pallas_call(
        kernel,
        out_shape=out_shape,
        compiler_params=pltpu.CompilerParams(vmem_limit_bytes=vmem * MIB),
        cost_estimate=pl.CostEstimate(flops=1, bytes_accessed=1, transcendentals=0),
        **kw,
    )


def nt_dot(a, b):
    return lax.dot_general(a, b, (((1,), (1,)), ((), ())), preferred_element_type=jnp.float32)


HBM = pl.BlockSpec(memory_space=pltpu.HBM)


def in_hbm(*arrays):
    return [pltpu.with_memory_space_constraint(a, pltpu.HBM) for a in arrays]


def pack_kernel(
    latent_ref, key_rope_ref, pos_ref, query_ref, q_rope_ref, key_ref, q_ref, rope, pos, sems
):
    copies = [
        pltpu.make_async_copy(key_rope_ref, rope, sems.at[0]),
        pltpu.make_async_copy(pos_ref, pos, sems.at[1]),
        pltpu.make_async_copy(latent_ref, key_ref.at[:, :RANK], sems.at[2]),
        pltpu.make_async_copy(query_ref, q_ref.at[:, : HG * NOPE], sems.at[3]),
        pltpu.make_async_copy(q_rope_ref, q_ref.at[:, HG * NOPE :], sems.at[4]),
    ]
    for copy in copies:
        copy.start()
    copies[0].wait()
    copies[1].wait()
    where = pos[...].astype(jnp.float32)
    high = jnp.floor(where * (1 / 128))
    row = lax.broadcasted_iota(jnp.int32, rope.shape, 0)
    ext = jnp.where(row == 0, high, jnp.where(row == 1, where - high * 128, 0.0))
    ext = jnp.concatenate([rope[...].astype(jnp.float32), ext], axis=0)
    key_ref[:, RANK:] = jnp.transpose(ext).astype(jnp.bfloat16)
    for copy in copies[2:]:
        copy.wait()


def pack(latent, k_rope, key_pos, query, q_rope):
    return call(
        pack_kernel,
        (
            jax.ShapeDtypeStruct((latent.shape[0], KEYW), jnp.bfloat16),
            jax.ShapeDtypeStruct((R, HG * (NOPE + ROPE)), jnp.bfloat16),
        ),
        in_specs=[HBM] * 5,
        scratch_shapes=[
            pltpu.VMEM((k_rope.shape[1], k_rope.shape[0]), jnp.bfloat16),
            pltpu.VMEM(key_pos.shape, jnp.int32),
            pltpu.SemaphoreType.DMA((5,)),
        ],
    )(*in_hbm(latent, jnp.transpose(k_rope), key_pos, query, q_rope))


def join_kernel(*refs):
    start = 0
    for ref in refs[:-1]:
        refs[-1][start : start + ref.shape[0]] = ref[...]
        start += ref.shape[0]


def join(parts):
    shape = (sum(part.shape[0] for part in parts), parts[0].shape[1])
    return call(join_kernel, jax.ShapeDtypeStruct(shape, jnp.bfloat16))(*parts)


def absorb_kernel(*refs):
    q_refs, (w_hbm, out_ref, w_ref, sems) = refs[:2], refs[2:]
    step = HG // 4
    copies = [
        pltpu.make_async_copy(
            w_hbm.at[i * step : (i + 1) * step],
            w_ref.at[i * step : (i + 1) * step],
            sems.at[i],
        )
        for i in range(4)
    ]
    for copy in copies:
        copy.start()
    lane = lax.broadcasted_iota(jnp.int32, (ROWS, 128), 1)
    row = lax.broadcasted_iota(jnp.int32, (ROWS, 128), 0)
    one_hot = (lane == row).astype(jnp.bfloat16)

    def columns(start):
        return jnp.concatenate([ref[:, start : start + 128] for ref in q_refs], axis=0)

    for h in range(HG):
        rows = slice(h * ROWS, (h + 1) * ROWS)
        pair = columns(HG * NOPE + (h // 2) * 128).astype(jnp.float32)
        if h % 2:
            pair = pltpu.roll(pair, ROPE, 1)
        rope = jnp.where(lane < ROPE, pair, 0.0)
        out_ref[rows, RANK : RANK + 128] = rope.astype(jnp.bfloat16)
        out_ref[rows, RANK + 128 :] = one_hot
    for h in range(HG):
        if h % step == 0:
            copies[h // step].wait()
        rows = slice(h * ROWS, (h + 1) * ROWS)
        latent = jnp.dot(columns(h * NOPE), w_ref[h], preferred_element_type=jnp.float32)
        out_ref[rows, :RANK] = latent.astype(jnp.bfloat16)


def absorb(queries, w_uk):
    return call(
        absorb_kernel,
        jax.ShapeDtypeStruct((ITEMS, ITEMW), jnp.bfloat16),
        vmem=16,
        in_specs=[pl.BlockSpec(memory_space=pltpu.VMEM)] * 2 + [HBM],
        scratch_shapes=[
            pltpu.VMEM(w_uk.shape, jnp.bfloat16),
            pltpu.SemaphoreType.DMA((4,)),
        ],
    )(*queries, *in_hbm(w_uk))


def pack_stats(stats):
    high = stats.astype(jnp.bfloat16).astype(jnp.float32)
    mid = (stats - high).astype(jnp.bfloat16).astype(jnp.float32)
    low = stats - high - mid
    packed = high + pltpu.roll(mid, HG, 1) + pltpu.roll(low, 2 * HG, 1)
    return packed.astype(jnp.bfloat16)


def unpack_stats(packed):
    packed = packed.astype(jnp.float32)
    return packed + pltpu.roll(packed, 128 - HG, 1) + pltpu.roll(packed, 128 - 2 * HG, 1)


def attend_kernel(pieces, last, tile, unroll, *refs):
    q_ref, qpos_ref, v_ref = refs[:3]
    piece_refs = refs[3 : 3 + pieces]
    rest = refs[3 + pieces :]
    if last:
        part_in, lse_in, keep_ref, send_ref, key_ref, lse_ref = rest
        lse_ref[...] = jnp.zeros_like(lse_ref)
    else:
        part_out, lse_out, key_ref = rest

    qpos = qpos_ref[0:1, :]
    start = 0
    for ref in piece_refs:
        rows = slice(start, start + ref.shape[0])
        start += ref.shape[0]
        key_ref[rows, :KEYW] = ref[...]
        ext = ref[:, RANK:].astype(jnp.float32)
        pos = ext[:, ROPE : ROPE + 1] * 128.0 + ext[:, ROPE + 1 : ROPE + 2]
        key_ref[rows, KEYW:] = jnp.where(pos <= qpos, 0.0, NEG).astype(jnp.bfloat16)

    half = ROWS // 2
    heads = tile // ROWS

    def body(step):
        items = pl.ds(pl.multiple_of(step * tile, tile), tile)
        scores = nt_dot(q_ref[items, :], key_ref[...]) * SCALE2
        top = jnp.max(scores, axis=1, keepdims=True)
        weights = jnp.exp2(scores - top)
        total = jnp.sum(weights, axis=1, keepdims=True)
        acc = jnp.dot(
            weights.astype(jnp.bfloat16), key_ref[:, :RANK], preferred_element_type=jnp.float32
        )
        context = (acc * (1.0 / total)).astype(jnp.bfloat16)
        lse = top + jnp.log2(total)
        if last:
            earlier = lse_in[items, 0:1]
            top = jnp.maximum(lse, earlier)
            here, there = jnp.exp2(lse - top), jnp.exp2(earlier - top)
            total = here + there
            lse = top + jnp.log2(total)
            inverse = 1.0 / total
            here, there = here * inverse, there * inverse
        else:
            lse_out[items, :] = jnp.broadcast_to(lse, (tile, 128))

        lane = lax.broadcasted_iota(jnp.int32, (ROWS, 128), 1)
        for i in range(heads):
            rows = slice(i * ROWS, (i + 1) * ROWS)
            head = step * heads + i
            cols = pl.ds(pl.multiple_of(head * VDIM, VDIM), VDIM)
            out = jnp.dot(context[rows], v_ref[head], preferred_element_type=jnp.float32)
            if last:
                out = out * here[rows] + part_in[:, cols] * there[rows]
                out = out.astype(jnp.bfloat16)
                keep_ref[:, cols] = out[:half]
                send_ref[:, cols] = out[half:]
                lse_ref[...] = jnp.where(lane == head, lse[rows], lse_ref[...])
            else:
                part_out[:, cols] = out

    pl.loop(0, ITEMS // tile, unroll=unroll)(body)

    if last:
        packed = pack_stats(lse_ref[...])
        keep_ref[:, HG * VDIM :] = packed[:half]
        send_ref[:, HG * VDIM :] = packed[half:]


def attend(q, qpos, value_weight, pieces, earlier=None, tile=1024, unroll=2):
    n, keys = len(pieces), sum(piece.shape[0] for piece in pieces)
    last = earlier is not None
    scratch = [pltpu.VMEM((keys, ITEMW), jnp.bfloat16)]
    if last:
        half = jax.ShapeDtypeStruct((ROWS // 2, SENDW), jnp.bfloat16)
        out_shape = (half, half)
        scratch.append(pltpu.VMEM((ROWS, 128), jnp.float32))
    else:
        out_shape = (
            jax.ShapeDtypeStruct((ROWS, HG * VDIM), jnp.float32),
            jax.ShapeDtypeStruct((ITEMS, 128), jnp.float32),
        )
    return call(
        functools.partial(attend_kernel, n, last, tile, unroll),
        out_shape,
        vmem=36,
        scratch_shapes=scratch,
    )(q, qpos, value_weight, *pieces, *(earlier or ()))


def merge(refs):
    stats = [unpack_stats(ref[:, HG * VDIM :]) for ref in refs]
    top = functools.reduce(jnp.maximum, stats)
    weights = [jnp.exp2(s - top) for s in stats]
    total = sum(weights)
    weights = [w / total for w in weights]
    out = []
    for h in range(HG):
        cols = slice(h * VDIM, (h + 1) * VDIM)
        head = sum(
            ref[:, cols].astype(jnp.float32) * w[:, h : h + 1] for ref, w in zip(refs, weights)
        )
        out.append((cols, head.astype(jnp.bfloat16)))
    return out, top + jnp.log2(total)


def merge_core_kernel(a_ref, b_ref, *out_refs):
    heads, lse = merge((a_ref, b_ref))
    lane = lax.broadcasted_iota(jnp.int32, lse.shape, 1)
    packed = pack_stats(jnp.where(lane < HG, lse, 0.0))
    for cols, head in heads + [(slice(HG * VDIM, SENDW), packed)]:
        for i, ref in enumerate(out_refs):
            ref[:, cols] = head[i * R : (i + 1) * R]


def merge_ring_kernel(*refs):
    part_refs, (out_ref, held, sems) = refs[:4], refs[4:]
    heads, _ = merge(part_refs)
    half = HG * VDIM // 2
    copies = []
    for i, (cols, head) in enumerate(heads):
        held[:, cols] = head
        if (i + 1) % (HG // 2) == 0:
            k = i // (HG // 2)
            lanes = slice(k * half, (k + 1) * half)
            for n in range(16):
                copy = pltpu.make_async_copy(
                    held.at[:, lanes], out_ref.at[n, :, lanes], sems.at[k, n]
                )
                copy.start()
                copies.append(copy)
    for copy in copies:
        copy.wait()


def columns_kernel(zc_ref, own_ref, *refs):
    z, c = zc_ref[0], zc_ref[1]
    w_refs, (out_ref, held, sem) = refs[:3], refs[3:]
    ncol, depth = held.shape
    copy = pltpu.make_async_copy(own_ref, held, sem)
    copy.start()
    for k in (1, 2, 3, 0):
        to_z = z if k % 2 == 0 else 1 - z
        to_c = c if k < 2 else 1 - c
        if k == 0:
            copy.wait()
        piece = held[...] if k == 0 else w_refs[k - 1][...]
        padded = jnp.concatenate([piece, jnp.zeros((128 - ncol, depth), jnp.bfloat16)], axis=0)
        lanes = pl.ds(pl.multiple_of((to_z * 2 + to_c) * 128, 128), 128)
        out_ref[:, lanes] = jnp.transpose(padded)


def columns_of(zc, pieces):
    ncol, depth = pieces[0].shape
    return call(
        columns_kernel,
        jax.ShapeDtypeStruct((depth, 4 * 128), jnp.bfloat16),
        vmem=16,
        in_specs=[pl.BlockSpec(memory_space=pltpu.SMEM), HBM]
        + [pl.BlockSpec(memory_space=pltpu.VMEM)] * 3,
        scratch_shapes=[
            pltpu.VMEM((ncol, depth), jnp.bfloat16),
            pltpu.SemaphoreType.DMA,
        ],
    )(zc, *in_hbm(pieces[0]), *pieces[1:])


def project_kernel(x_ref, w_ref, out_ref):
    ncol = out_ref.shape[2]
    out = jnp.dot(x_ref[...], w_ref[...], preferred_element_type=jnp.float32)
    for k in range(4):
        out_ref[k] = out[:, k * 128 : k * 128 + ncol].astype(jnp.bfloat16)


def finish_kernel(sums_ref, out_ref, row_ref):
    ncol = sums_ref.shape[2]
    row_ref[...] = jnp.zeros_like(row_ref)
    for zc in range(4):
        total = sum(sums_ref[zc * 4 + h].astype(jnp.float32) for h in range(4))
        for i in range(4):
            start = (i * 4 + zc) * R
            row_ref[start : start + R, :ncol] = total[i * R : (i + 1) * R]
    out_ref[...] = jnp.transpose(row_ref[...])[:ncol].astype(jnp.bfloat16)


def local(query_unrotated, q_rope, latent, k_rope, key_pos, offset, w_uk, value_up_weight, w_out):
    y, x, z, c = (lax.axis_index(n) for n in CTX)

    keys, q_own = pack(latent[0], k_rope[0], key_pos, query_unrotated, q_rope)
    z_keys = lax.ppermute(keys, "z", SWAP)
    up, down, across = (lax.ppermute(keys, "y", shift(d)) for d in (1, 3, 2))
    q_ring = [lax.ppermute(q_own, "x", shift(1)), lax.ppermute(q_own, "x", shift(3))]
    q_ring, q_own = lax.optimization_barrier((q_ring, q_own))
    q_ring.append(lax.ppermute(q_own, "x", shift(2)))
    z_keys, up, down, across = lax.optimization_barrier((z_keys, up, down, across))
    near = [keys, up, down, across]
    far = [z_keys] + [lax.ppermute(z_keys, "y", shift(d)) for d in RING[1:]]
    q_chip, w_own = lax.optimization_barrier((join([q_own, *q_ring]), jnp.transpose(w_out)))
    q_core = lax.ppermute(q_chip, "c", SWAP)
    z_w = lax.ppermute(w_own, "z", SWAP)

    row = jnp.arange(ROWS, dtype=jnp.int32)
    part = row // R
    row_x = (x - jnp.array(RING, jnp.int32)[part % 4]) % 4
    row_c = jnp.where(part < 4, c, 1 - c)
    row = (((y * 4 + row_x) * 2 + z) * 2 + row_c) * R + row % R
    qpos = jnp.broadcast_to((offset[0] + row).astype(jnp.float32)[None, :], (8, ROWS))

    q = absorb((q_chip, q_core), w_uk)
    earlier = attend(q, qpos, value_up_weight, near)
    earlier, far = lax.optimization_barrier((earlier, far))
    keep, send = attend(q, qpos, value_up_weight, far, earlier)

    z_w, send = lax.optimization_barrier((z_w, send))
    parts = call(
        merge_core_kernel, [jax.ShapeDtypeStruct((R, SENDW), jnp.bfloat16)] * 4
    )(keep, lax.ppermute(send, "c", SWAP))
    parts = [parts[0]] + [
        lax.ppermute(part, "x", shift(-d % 4)) for part, d in zip(parts[1:], RING[1:])
    ]
    c_w = lax.ppermute(w_own, "c", SWAP)
    zc_w = lax.ppermute(z_w, "c", SWAP)
    parts, c_w = lax.optimization_barrier((parts, c_w))
    heads = call(
        merge_ring_kernel,
        jax.ShapeDtypeStruct((16, R, HG * VDIM), jnp.bfloat16),
        out_specs=HBM,
        scratch_shapes=[
            pltpu.VMEM((R, HG * VDIM), jnp.bfloat16),
            pltpu.SemaphoreType.DMA((2, 16)),
        ],
    )(*parts)

    rows = lax.all_to_all(heads, ("y", "x"), 0, 0, tiled=True).reshape(16 * R, HG * VDIM)
    ncol = w_out.shape[1]
    columns = columns_of(jnp.stack([z, c]), (w_own, z_w, c_w, zc_w))
    sums = call(
        project_kernel, jax.ShapeDtypeStruct((4, 16 * R, ncol), jnp.bfloat16), vmem=16
    )(rows, columns)
    sums = lax.all_to_all(
        sums.reshape(16, 4 * R, ncol), ("z", "c", "head"), 0, 0, tiled=True
    )
    out = call(
        finish_kernel,
        jax.ShapeDtypeStruct((ncol, 16 * R), jnp.bfloat16),
        scratch_shapes=[pltpu.VMEM((16 * R, 128), jnp.float32)],
    )(sums)
    return jnp.transpose(out)


def solution(mesh):
    grid = Mesh(mesh.devices.reshape(4, 4, 2, 2, 4), CTX + ("head",))
    return jax.shard_map(
        local,
        mesh=grid,
        in_specs=(
            P(CTX, "head"),
            P(CTX, "head"),
            P(None, CTX, None),
            P(None, CTX, None),
            P(None, CTX),
            P(),
            P("head", None, None),
            P("head", None, None),
            P("head", CTX),
        ),
        out_specs=P("head", CTX),
        check_vma=False,
    )
```
